32 devices in a mesh: dp: 4 (over z), seq: 8 (over y, x, core).
Axes of the slice: x: 2, y: 2, z: 4, core: 2. Of those that a mesh axis runs over, the one named last changes fastest.
Arguments:
- tokens: bfloat16 [8, 512, 1536], P('dp', 'seq'), may hold values from -6 to 6
- doc_lengths: int32 [8, 8], P('dp'), may hold values from 1 to 480, as said below
- query_weight: bfloat16 [1536, 1536], P(('dp', 'seq')), may hold values from -0.15625 to 0.15625
- key_weight: bfloat16 [1536, 256], P(('dp', 'seq')), may hold values from -0.15625 to 0.15625
- value_weight: bfloat16 [1536, 256], P(('dp', 'seq')), may hold values from -0.15625 to 0.15625
- query_bias: bfloat16 [1536], P(('dp', 'seq')), may hold values from -3 to 3
- key_bias: bfloat16 [256], P(('dp', 'seq')), may hold values from -3 to 3
- value_bias: bfloat16 [256], P(('dp', 'seq')), may hold values from -3 to 3
- output_weight: bfloat16 [1536, 1536], P(('dp', 'seq')), may hold values from -0.3125 to 0.3125
- attention_norm_gain: bfloat16 [1536], P(('dp', 'seq')), may hold values from 0.099609375 to 1.8984375
- feedforward_norm_gain: bfloat16 [1536], P(('dp', 'seq')), may hold values from 0.099609375 to 1.8984375
- gate_weight: bfloat16 [1536, 8960], P(('dp', 'seq')), may hold values from -0.15625 to 0.15625
- up_weight: bfloat16 [1536, 8960], P(('dp', 'seq')), may hold values from -0.15625 to 0.15625
- down_weight: bfloat16 [8960, 1536], P(('dp', 'seq')), may hold values from -0.125 to 0.125
- cotangent: bfloat16 [8, 512, 1536], P('dp', 'seq'), may hold values from -6 to 6
Outputs:
- layer_output: bfloat16 [8, 512, 1536], P('dp', 'seq')
- input_grad: bfloat16 [8, 512, 1536], P('dp', 'seq')
- grad_query_weight: float32 [1536, 1536], P(('dp', 'seq'))
- grad_key_weight: float32 [1536, 256], P(('dp', 'seq'))
- grad_value_weight: float32 [1536, 256], P(('dp', 'seq'))
- grad_query_bias: float32 [1536], P(('dp', 'seq'))
- grad_key_bias: float32 [256], P(('dp', 'seq'))
- grad_value_bias: float32 [256], P(('dp', 'seq'))
- grad_output_weight: float32 [1536, 1536], P(('dp', 'seq'))
- grad_input_gain: float32 [1536], P(('dp', 'seq'))
- grad_post_gain: float32 [1536], P(('dp', 'seq'))
- grad_gate_weight: float32 [1536, 8960], P(('dp', 'seq'))
- grad_up_weight: float32 [1536, 8960], P(('dp', 'seq'))
- grad_down_weight: float32 [8960, 1536], P(('dp', 'seq'))
The draws below stay inside these ranges and needn't reach their ends.
Inputs may be any that keep to these rules, and one draw needn't show every extreme that they name: `doc_lengths`: each row's 8 lengths sum to 512.
All inputs are finite; a program needn't handle non-finite values.
Results may differ from the reference program's by a relative error of at most 0.029.
Values may be sent and summed in bfloat16 or wider, within the bound.
No kernel may reach another device: no remote copies, remote signals or barrier semaphores. Data moves between devices by JAX's collectives and lax.ppermute only.
A program may use at most 512 MiB of HBM per device.

```python
import jax
import jax.numpy as jnp
from jax import lax

D = 1536
H = 12
KV = 2
HD = 128
FF = 8960
ROWS = 2
SEG = 64
DOCS = 8
QW = 1536
KW = 256
HPG = 6
ROW_LEN = 512
ROWS_ALL = 8
N_DP = 4


def spread_counts(key, row_total, slots, amount):
    weights_int = jax.random.randint(key, (row_total, slots), 1, 100)
    spare = amount - slots
    shares = 1 + weights_int * spare // jnp.sum(weights_int, axis=1, keepdims=True)
    column = jnp.arange(slots)[None, :]
    leftover = amount - jnp.sum(shares, axis=1, keepdims=True)
    return shares + jnp.where(column == 0, leftover, 0)


def draw_doc_lengths(key, part):
    key = jax.random.fold_in(key, 11)
    key_drawn, key_short, key_place, key_pick = jax.random.split(key, 4)
    drawn_rows = spread_counts(key_drawn, ROWS_ALL, DOCS, ROW_LEN)
    short_rows = spread_counts(key_short, ROWS_ALL, DOCS - 1, SEG // 2)
    place = jax.random.randint(key_place, (ROWS_ALL, 1), 0, DOCS)
    column = jnp.arange(DOCS)[None, :]
    source = jnp.clip(column - (column > place).astype(jnp.int32), 0, DOCS - 2)
    short_full = jnp.take_along_axis(short_rows, source, axis=1)
    long_rows = jnp.where(column == place, ROW_LEN - SEG // 2, short_full)
    chosen = jax.random.randint(key_pick, (N_DP,), 0, ROWS)
    row_ids = jnp.arange(ROWS_ALL)
    is_long = row_ids % ROWS == chosen[row_ids // ROWS]
    return jnp.where(is_long[:, None], long_rows, drawn_rows).astype(jnp.int32)


def block_levels(key, shape, pieces, least, top_value):
    loudness, own = 1.0, jax.random.fold_in(key, 6)
    for axis_at, parts in pieces:
        heights = jnp.exp(jax.random.uniform(jax.random.fold_in(own, axis_at), (parts,), jnp.float32, least / len(pieces), top_value / len(pieces)))
        loudness = loudness * jnp.repeat(heights, shape[axis_at] // parts).reshape([-1 if axis == axis_at else 1 for axis in range(len(shape))])
    return loudness


def scatter_about(stream_key, dims, scale, limit, pieces=(), kind=jnp.bfloat16):
    entries = scale * jax.random.normal(stream_key, dims, jnp.float32)
    if pieces:
        entries = entries * block_levels(stream_key, dims, pieces, -0.22, 0.18)
    return jnp.clip(entries, -limit, limit).astype(kind)


def setup_inputs(seed: int = 0) -> dict:
    streams_of = jax.random.split(jax.random.key(seed), 16)
    tokens = scatter_about(streams_of[0], (ROWS_ALL, ROW_LEN, D), 1.0, 6.0, ((0, 4), (1, 8)))
    doc_lengths = draw_doc_lengths(jax.random.fold_in(streams_of[15], 71), 0)
    query_weight = scatter_about(streams_of[2], (D, QW), D ** -0.5, 0.15625, ((0, 32),))
    key_weight = scatter_about(streams_of[3], (D, KW), D ** -0.5, 0.15625, ((0, 32),))
    value_weight = scatter_about(streams_of[4], (D, KW), D ** -0.5, 0.15625, ((0, 32),))
    query_bias = scatter_about(streams_of[5], (QW,), 0.5, 3.0, ((0, 32),))
    key_bias = scatter_about(streams_of[6], (KW,), 0.5, 3.0, ((0, 32),))
    value_bias = scatter_about(streams_of[7], (KW,), 0.5, 3.0, ((0, 32),))
    output_weight = scatter_about(streams_of[8], (QW, D), (QW // 4) ** -0.5, 0.3125, ((0, 32),))
    attention_norm_gain = jnp.clip(1.0 + 0.18 * jax.random.normal(streams_of[9], (D,), jnp.float32), 0.099609375, 1.8984375).astype(jnp.bfloat16)
    feedforward_norm_gain = jnp.clip(1.0 + 0.18 * jax.random.normal(streams_of[10], (D,), jnp.float32), 0.099609375, 1.8984375).astype(jnp.bfloat16)
    gate_weight = scatter_about(streams_of[11], (D, FF), D ** -0.5, 0.15625, ((0, 32),))
    up_weight = scatter_about(streams_of[12], (D, FF), D ** -0.5, 0.15625, ((0, 32),))
    down_weight = scatter_about(streams_of[13], (FF, D), (FF // 4) ** -0.5, 0.125, ((0, 32),))
    cotangent = scatter_about(streams_of[14], (ROWS_ALL, ROW_LEN, D), 1.0, 6.0, ((0, 4), (1, 8)))
    return {"tokens": tokens, "doc_lengths": doc_lengths, "query_weight": query_weight, "key_weight": key_weight, "value_weight": value_weight, "query_bias": query_bias, "key_bias": key_bias, "value_bias": value_bias, "output_weight": output_weight, "attention_norm_gain": attention_norm_gain, "feedforward_norm_gain": feedforward_norm_gain, "gate_weight": gate_weight, "up_weight": up_weight, "down_weight": down_weight, "cotangent": cotangent}


epsilon = 1e-06
rope_base = 10000.0
masked_value = -1e+30
highest_mode = lax.Precision.HIGHEST

@jax.custom_vjp
def low(v):
    return lax.optimization_barrier(v.astype(jnp.bfloat16)).astype(jnp.float32)

@jax.custom_vjp
def low_back(v):
    return v

def low_keep(v):
    return (low(v), None)

def low_pass(kept, grad):
    return (grad,)

def back_keep(v):
    return (v, None)

def back_low(kept, grad):
    return (low(grad),)
low.defvjp(low_keep, low_pass)
low_back.defvjp(back_keep, back_low)

def matmul(left, right):
    return jnp.dot(left, right, precision=highest_mode)

def root_mean_square_scale(values):
    return lax.rsqrt(lax.optimization_barrier(jnp.mean(values * values, axis=-1, keepdims=True)) + epsilon)

def rope_tables(within):
    steps_even = jnp.arange(0, HD, 2).astype(jnp.float32)
    inverse = rope_base ** (-steps_even / HD)
    phase = within.astype(jnp.float32)[:, None] * inverse[None, :]
    phase = jnp.concatenate([phase, phase], axis=-1)
    return (jnp.cos(phase)[:, None, :], jnp.sin(phase)[:, None, :])

def rotate(values, cosine, sine):
    halfway = values.shape[-1] // 2
    first = values[..., :halfway]
    second = values[..., halfway:]
    return values * cosine + jnp.concatenate([-second, first], axis=-1) * sine

def doc_tables(row_lengths, positions):
    ends = jnp.cumsum(row_lengths)
    passed = ends[None, :] <= positions[:, None]
    doc_index = lax.optimization_barrier(jnp.sum(passed.astype(jnp.int32), axis=-1)).astype(jnp.int32)
    starts = lax.optimization_barrier(jnp.sum(jnp.where(passed, row_lengths[None, :], 0), axis=-1)).astype(jnp.int32)
    return (doc_index, (positions - starts).astype(jnp.int32))

def layer_row(tokens_per_row, query_weight, key_weight, value_weight, query_bias, key_bias, value_bias, output_weight, attention_norm_gain, feedforward_norm_gain, gate_weight, up_weight, down_weight, doc_index, within):
    length = tokens_per_row.shape[0]
    first_normalized = tokens_per_row * root_mean_square_scale(tokens_per_row)
    first_normed = low(first_normalized * attention_norm_gain)
    query_pre = low_back(matmul(first_normed, query_weight) + query_bias)
    key_pre = low_back(matmul(first_normed, key_weight) + key_bias)
    value_all = low(low_back(matmul(first_normed, value_weight) + value_bias))
    cosine, sine = rope_tables(within)
    queries = low(rotate(query_pre.reshape(length, H, HD), cosine, sine))
    key_rows = low(rotate(key_pre.reshape(length, KV, HD), cosine, sine))
    value_rows = value_all.reshape(length, KV, HD)
    key_heads = jnp.repeat(key_rows, HPG, axis=1)
    value_heads = jnp.repeat(value_rows, HPG, axis=1)
    query_block = min(512, length)
    block_total = length // query_block
    positions = jnp.arange(length, dtype=jnp.int32)
    scaling = 1.0 / HD ** 0.5

    def attend(block_index):
        offset = (block_index * query_block).astype(jnp.int32)
        query_part = lax.dynamic_slice_in_dim(queries, offset, query_block, 0)
        query_doc = lax.dynamic_slice_in_dim(doc_index, offset, query_block, 0)
        query_pos = offset + jnp.arange(query_block, dtype=jnp.int32)
        scores = low_back(jnp.einsum('qhd,khd->hqk', query_part, key_heads, precision=highest_mode) * scaling)
        allowed = (query_doc[:, None] == doc_index[None, :]) & (positions[None, :] <= query_pos[:, None])
        masked = jnp.where(allowed[None], scores, masked_value)
        row_top = lax.optimization_barrier(jnp.max(masked, axis=-1, keepdims=True))
        log_total = row_top + jnp.log(lax.optimization_barrier(jnp.sum(jnp.exp(masked - row_top), axis=-1, keepdims=True)))
        soft_probs = jnp.exp(masked - log_total)
        return jnp.einsum('hqk,khd->qhd', low(soft_probs), value_heads, precision=highest_mode)
    mixed = lax.map(jax.checkpoint(attend), jnp.arange(block_total, dtype=jnp.int32))
    attended = low(low_back(mixed.reshape(length, H * HD)))
    first_hidden = tokens_per_row + low_back(matmul(attended, output_weight))
    second_normalized = first_hidden * root_mean_square_scale(first_hidden)
    second_normed = low(second_normalized * feedforward_norm_gain)
    gate_pre = low_back(matmul(second_normed, gate_weight))
    up_pre = low_back(matmul(second_normed, up_weight))
    hidden = low(jax.nn.silu(gate_pre) * up_pre)
    return first_hidden + matmul(hidden, down_weight)

def reference(tokens, doc_lengths, query_weight, key_weight, value_weight, query_bias, key_bias, value_bias, output_weight, attention_norm_gain, feedforward_norm_gain, gate_weight, up_weight, down_weight, cotangent):
    params = tuple((item.astype(jnp.float32) for item in (query_weight, key_weight, value_weight, query_bias, key_bias, value_bias, output_weight, attention_norm_gain, feedforward_norm_gain, gate_weight, up_weight, down_weight)))
    positions = jnp.arange(ROW_LEN, dtype=jnp.int32)

    def per_row(totals, inputs):
        tokens_per_row, row_lengths, row_cotangent = inputs
        doc_index, within = doc_tables(row_lengths, positions)

        def forward(row_input, *weights):
            return layer_row(row_input, *weights, doc_index, within)
        result, pullback = jax.vjp(forward, tokens_per_row.astype(jnp.float32), *params)
        grads = pullback(row_cotangent.astype(jnp.float32))
        new_totals = tuple((running + piece for running, piece in zip(totals, grads[1:])))
        return (new_totals, (result.astype(jnp.bfloat16), grads[0].astype(jnp.bfloat16)))
    initial = tuple((jnp.zeros(item.shape, jnp.float32) for item in params))
    totals, (outputs, input_grads) = lax.scan(per_row, initial, (tokens, doc_lengths, cotangent))
    return (outputs, input_grads, totals[0], totals[1], totals[2], totals[3], totals[4], totals[5], totals[6], totals[7], totals[8], totals[9], totals[10], totals[11])
```

```python
import math

import jax
import jax.numpy as jnp
from jax import lax
from jax.sharding import Mesh
from jax.sharding import PartitionSpec as P

H = 12
KV = 2
HD = 128
HPG = 6


epsilon = 1e-06
rope_base = 10000.0
masked_value = -1e30


def root_mean_square_scale(values):
    return lax.rsqrt(jnp.mean(values * values, axis=-1, keepdims=True) + epsilon)


def rope_tables(within):
    steps_even = jnp.arange(0, HD, 2).astype(jnp.float32)
    inverse = rope_base ** (-steps_even / HD)
    phase = within.astype(jnp.float32)[:, None] * inverse[None, :]
    phase = jnp.concatenate([phase, phase], axis=-1)
    return (jnp.cos(phase)[:, None, :], jnp.sin(phase)[:, None, :])


def rotate(values, cosine, sine):
    halfway = values.shape[-1] // 2
    return (
        values * cosine
        + jnp.concatenate([-values[..., halfway:], values[..., :halfway]], axis=-1) * sine
    )


def rotate_back(grads, cosine, sine):
    halfway = grads.shape[-1] // 2
    turned = grads * sine
    return grads * cosine + jnp.concatenate(
        [turned[..., halfway:], -turned[..., :halfway]], axis=-1
    )


def doc_tables(doc_ends, doc_lengths, positions):
    passed = doc_ends[:, None, :] <= positions[None, :, None]
    doc_index = jnp.sum(passed.astype(jnp.int32), axis=-1)
    starts = jnp.sum(jnp.where(passed, doc_lengths[:, None, :], 0), axis=-1)
    return (doc_index, positions[None, :] - starts)


def contract_rows(left, right):
    return lax.dot_general(
        left, right, (((0,), (0,)), ((), ())), preferred_element_type=jnp.float32
    )


def contract_cols(left, right):
    return lax.dot_general(
        left, right, (((1,), (1,)), ((), ())), preferred_element_type=jnp.float32
    )


def to_groups(flat_heads, local_rows, shard_tokens):
    shaped = flat_heads.reshape(local_rows, shard_tokens, KV, HPG, HD).transpose(0, 2, 3, 1, 4)
    return shaped.reshape(local_rows, KV, HPG * shard_tokens, HD)


def from_groups(grouped, local_rows, shard_tokens):
    shaped = grouped.reshape(local_rows, KV, HPG, shard_tokens, HD).transpose(0, 3, 1, 2, 4)
    return shaped.reshape(local_rows * shard_tokens, H * HD)


def swapped(values, axis):
    return lax.ppermute(values, axis, [(0, 1), (1, 0)])


def shifted(values, amount):
    count = lax.axis_size("z")
    return lax.ppermute(values, "z", [(i, (i + amount) % count) for i in range(count)])


def pick(values, index, axis):
    return lax.dynamic_index_in_dim(values, index, axis, keepdims=False)


def place(buffer, block, index):
    rest = buffer.ndim - len(index)
    lead = (1,) * len(index)
    shaped = block.reshape(lead + buffer.shape[len(index) :])
    return lax.dynamic_update_slice(buffer, shaped, tuple(index) + (0,) * rest)


def gather_group(rows):
    pieces = [rows] + [shifted(rows, k) for k in range(1, lax.axis_size("z"))]
    mine = jnp.concatenate(pieces, axis=0)
    return jnp.concatenate([mine, swapped(mine, "c")], axis=0)


def scatter_group(partial, count):
    half = partial.shape[0] // 2
    kept = partial[:half].astype(jnp.float32) + swapped(partial[half:], "c").astype(jnp.float32)
    blocks = kept.reshape((lax.axis_size("z"), count) + partial.shape[1:])
    total = blocks[0]
    for k in range(1, lax.axis_size("z")):
        total = total + shifted(blocks[k].astype(jnp.bfloat16), -k).astype(jnp.float32)
    return total


def gather_columns(gate_weight, up_weight):
    rows, hidden = gate_weight.shape
    nz, ny, nx, nc = (lax.axis_size(a) for a in ("z", "y", "x", "c"))
    z, y, x, c = (lax.axis_index(a) for a in ("z", "y", "x", "c"))
    unit = hidden // (nz * ny * nx * nc)
    wide = ny * nx * unit
    both = jnp.stack([gate_weight, up_weight]).reshape(2, rows, nz, ny, nx, nc, unit)
    both = both.transpose(5, 2, 0, 1, 3, 4, 6).reshape(nc, nz, 2, rows, wide)
    kept = pick(both, c, 0)
    came = swapped(pick(both, 1 - c, 0), "c")
    cores = jnp.where(c == 0, jnp.stack([kept, came]), jnp.stack([came, kept]))
    cores = cores.transpose(1, 2, 0, 3, 4)
    shares = jnp.zeros((2, nz, nc, rows, wide), both.dtype)
    for k in range(nz):
        piece = pick(cores, (z + k) % nz, 0)
        if k:
            piece = shifted(piece, k)
        shares = lax.dynamic_update_slice(shares, piece[:, None], (0, (z - k) % nz, 0, 0, 0))
    if ny != 2 or nx != 2:
        whole = lax.all_gather(shares, ("y", "x"), axis=2).reshape(2, -1, wide)
        return whole[0], whole[1]
    from_x = swapped(shares, "x")
    from_y = swapped(shares, "y")
    gate_far = swapped(from_x[0], "y")
    up_far = swapped(from_y[1], "x")
    whole = []
    for m, far in enumerate((gate_far, up_far)):
        buffer = jnp.zeros((nz, ny, nx, nc, rows, wide), both.dtype)
        for piece, at_y, at_x in (
            (shares[m], y, x),
            (from_x[m], y, 1 - x),
            (from_y[m], 1 - y, x),
            (far, 1 - y, 1 - x),
        ):
            buffer = lax.dynamic_update_slice(
                buffer, piece[:, None, None], (0, at_y, at_x, 0, 0, 0)
            )
        whole.append(buffer.reshape(-1, wide))
    return whole[0], whole[1]


def scatter_columns(gate_grad, up_grad, rows):
    wide = gate_grad.shape[1]
    nz, ny, nx, nc = (lax.axis_size(a) for a in ("z", "y", "x", "c"))
    z, y, x, c = (lax.axis_index(a) for a in ("z", "y", "x", "c"))
    if ny != 2 or nx != 2:
        both = jnp.stack([gate_grad, up_grad]).reshape(2, nz, ny * nx, nc, rows, wide)
        both = lax.psum_scatter(both, ("y", "x"), scatter_dimension=2, tiled=False)
    else:
        sums = []
        for grad, order in ((gate_grad, "yx"), (up_grad, "xy")):
            left = grad.reshape(nz, ny, nx, nc, rows, wide)
            for axis in order:
                at = lax.axis_index(axis)
                dim = 1 if axis == "y" or left.ndim == 5 else 2
                came = swapped(pick(left, 1 - at, dim), axis)
                left = (
                    pick(left, at, dim).astype(jnp.float32) + came.astype(jnp.float32)
                ).astype(jnp.bfloat16)
            sums.append(left)
        both = jnp.stack(sums)
    kept = pick(both, c, 2)
    came = swapped(pick(both, 1 - c, 2), "c")
    cores = jnp.where(c == 0, jnp.stack([kept, came]), jnp.stack([came, kept]))
    cores = cores.transpose(2, 0, 1, 3, 4)
    shares = jnp.zeros((nz, nc, 2, rows, wide), both.dtype)
    for k in range(nz):
        piece = pick(cores, (z + k) % nz, 0)
        if k:
            piece = shifted(piece, k)
        shares = place(shares, piece, ((z - k) % nz,))
    unit = wide // (ny * nx)
    shares = shares.reshape(nz, nc, 2, rows, ny, nx, unit).transpose(2, 3, 0, 4, 5, 1, 6)
    shares = shares.reshape(2, rows, -1).astype(jnp.float32)
    return shares[0], shares[1]


def gather_rows(down_weight):
    rows, width = down_weight.shape
    ny, nx = (lax.axis_size(a) for a in ("y", "x"))
    y, x = (lax.axis_index(a) for a in ("y", "x"))
    if ny != 2 or nx != 2:
        return lax.all_gather(down_weight, ("y", "x"), axis=0, tiled=True)
    cut = rows // 32 * 16
    from_x = swapped(down_weight, "x")
    from_y = swapped(down_weight, "y")
    far = jnp.concatenate([swapped(from_x[:cut], "y"), swapped(from_y[cut:], "x")], axis=0)
    buffer = jnp.zeros((ny, nx, rows, width), down_weight.dtype)
    buffer = place(buffer, down_weight, (y, x))
    buffer = place(buffer, from_x, (y, 1 - x))
    buffer = place(buffer, from_y, (1 - y, x))
    buffer = place(buffer, far, (1 - y, 1 - x))
    return buffer.reshape(-1, width)


def scatter_rows(down_grad, rows):
    width = down_grad.shape[1]
    ny, nx = (lax.axis_size(a) for a in ("y", "x"))
    if ny != 2 or nx != 2:
        return lax.psum_scatter(down_grad, ("y", "x"), scatter_dimension=0, tiled=True)
    cut = rows // 32 * 16
    shaped = down_grad.reshape(ny, nx, rows, width)
    sums = []
    for part, order in ((shaped[:, :, :cut], "yx"), (shaped[:, :, cut:], "xy")):
        left = part
        for axis in order:
            at = lax.axis_index(axis)
            dim = 0 if axis == "y" or left.ndim == 3 else 1
            came = swapped(pick(left, 1 - at, dim), axis)
            left = pick(left, at, dim).astype(jnp.float32) + came.astype(jnp.float32)
            if left.ndim == 3:
                left = left.astype(jnp.bfloat16)
        sums.append(left)
    return jnp.concatenate(sums, axis=0)


def column_pack(columns, rows):
    padded = [jnp.pad(v, (0, rows - v.shape[0])) for v in columns]
    packed = jnp.stack(padded, axis=1)
    return jnp.pad(packed, ((0, 0), (0, 128 - len(columns))))


EVERY = ("z", "y", "x", "c")
ROW = ("y", "x", "c")


def shards(
    tokens,
    doc_lengths,
    query_weight,
    key_weight,
    value_weight,
    query_bias,
    key_bias,
    value_bias,
    output_weight,
    attention_norm_gain,
    feedforward_norm_gain,
    gate_weight,
    up_weight,
    down_weight,
    cotangent,
):
    local_rows, shard_tokens, width = tokens.shape
    devices = lax.axis_size(EVERY)
    row_length = shard_tokens * lax.axis_size(ROW)
    flat_count = local_rows * shard_tokens
    scaling = 1.0 / math.sqrt(HD)
    owned = query_weight.shape[0]
    query_width = query_weight.shape[1]
    key_width = key_weight.shape[1]
    owned_key = key_bias.shape[0]
    vectors = column_pack(
        (
            query_bias,
            attention_norm_gain,
            feedforward_norm_gain,
            jnp.concatenate([key_bias, value_bias]),
        ),
        owned,
    )
    packed = jnp.concatenate([query_weight, key_weight, value_weight, vectors], axis=1)
    packed = lax.all_gather(packed, EVERY, axis=0, tiled=True)
    weight_output = lax.all_gather(output_weight, EVERY, axis=0, tiled=True)
    projections = packed[:, : query_width + 2 * key_width]
    lines = packed[:, query_width + 2 * key_width :].T[:4].astype(jnp.float32)
    bias_query, input_gain, post_gain = lines[0], lines[1], lines[2]
    small = lines[3].reshape(devices, owned)
    bias_key = small[:, :owned_key].reshape(-1)
    bias_value = small[:, owned_key : 2 * owned_key].reshape(-1)
    bias_all = jnp.concatenate([bias_query, bias_key, bias_value])

    weight_gate, weight_up = gather_columns(gate_weight, up_weight)
    weight_down = gather_rows(down_weight)
    upstream = cotangent.reshape(flat_count, width)
    upstream_group = gather_group(upstream)

    local_pos = lax.axis_index(ROW) * shard_tokens + jnp.arange(shard_tokens, dtype=jnp.int32)
    all_pos = jnp.arange(row_length, dtype=jnp.int32)
    doc_ends = jnp.cumsum(doc_lengths, axis=1)
    query_doc, query_within = doc_tables(doc_ends, doc_lengths, local_pos)
    key_doc, unused_within = doc_tables(doc_ends, doc_lengths, all_pos)
    cosine, sine = rope_tables(query_within.reshape(flat_count))
    flattened_input = tokens.reshape(flat_count, width).astype(jnp.float32)
    first_inverse_norm = root_mean_square_scale(flattened_input)
    first_normalized = flattened_input * first_inverse_norm
    first_normed = (first_normalized * input_gain).astype(jnp.bfloat16)
    pre = jnp.dot(first_normed, projections, preferred_element_type=jnp.float32) + bias_all
    queries = rotate(pre[:, :query_width].reshape(flat_count, H, HD), cosine, sine).astype(
        jnp.bfloat16
    )
    key_pre = pre[:, query_width : query_width + key_width]
    key_rows = rotate(key_pre.reshape(flat_count, KV, HD), cosine, sine).astype(jnp.bfloat16)
    value_rows = pre[:, query_width + key_width :].astype(jnp.bfloat16)
    both_rows = jnp.concatenate([key_rows.reshape(flat_count, key_width), value_rows], axis=1)
    both_rows = lax.all_gather(
        both_rows.reshape(local_rows, shard_tokens, 2 * key_width), ROW, axis=1, tiled=True
    )
    both_heads = both_rows.reshape(local_rows, row_length, 2, KV, HD).transpose(2, 0, 3, 1, 4)
    key_heads, value_heads = both_heads[0], both_heads[1]
    query_groups = to_groups(queries.reshape(flat_count, H * HD), local_rows, shard_tokens)
    query_doc_rows = jnp.tile(query_doc, (1, HPG))
    query_pos_rows = jnp.tile(local_pos, (HPG,))
    scores = (
        jnp.einsum("rgmd,rgkd->rgmk", query_groups, key_heads, preferred_element_type=jnp.float32)
        * scaling
    )
    allowed = (query_doc_rows[:, None, :, None] == key_doc[:, None, None, :]) & (
        all_pos[None, None, None, :] <= query_pos_rows[None, None, :, None]
    )
    scores = jnp.where(allowed, scores, masked_value)
    row_top = jnp.max(scores, axis=-1, keepdims=True)
    log_total = row_top + jnp.log(jnp.sum(jnp.exp(scores - row_top), axis=-1, keepdims=True))
    probs = jnp.exp(scores - log_total)
    probs_low = probs.astype(jnp.bfloat16)
    mixed = jnp.einsum(
        "rgmk,rgkd->rgmd", probs_low, value_heads, preferred_element_type=jnp.float32
    )
    attended = from_groups(mixed, local_rows, shard_tokens).astype(jnp.bfloat16)
    first_hidden = flattened_input + jnp.dot(
        attended, weight_output, preferred_element_type=jnp.float32
    )
    second_inverse_norm = root_mean_square_scale(first_hidden)
    second_normalized = first_hidden * second_inverse_norm
    second_normed = (second_normalized * post_gain).astype(jnp.bfloat16)

    second_group = gather_group(second_normed)
    gate_pre = jnp.dot(second_group, weight_gate, preferred_element_type=jnp.float32)
    up_pre = jnp.dot(second_group, weight_up, preferred_element_type=jnp.float32)
    sigmoid_gate = jax.nn.sigmoid(gate_pre)
    silu_gate = gate_pre * sigmoid_gate
    hidden = (silu_gate * up_pre).astype(jnp.bfloat16)
    hidden_grad = contract_cols(upstream_group, weight_down)
    gate_grad = (
        hidden_grad * up_pre * sigmoid_gate * (1.0 + gate_pre * (1.0 - sigmoid_gate))
    ).astype(jnp.bfloat16)
    up_grad = (hidden_grad * silu_gate).astype(jnp.bfloat16)
    normed_partial = (
        contract_cols(gate_grad, weight_gate) + contract_cols(up_grad, weight_up)
    ).astype(jnp.bfloat16)
    second_normed_grad = scatter_group(normed_partial, flat_count)
    output_partial = jnp.dot(hidden, weight_down, preferred_element_type=jnp.float32)
    mlp_out = scatter_group(output_partial.astype(jnp.bfloat16), flat_count)
    layer_output = (first_hidden + mlp_out).astype(jnp.bfloat16)
    gate_sum, up_sum = scatter_columns(
        contract_rows(second_group, gate_grad).astype(jnp.bfloat16),
        contract_rows(second_group, up_grad).astype(jnp.bfloat16),
        owned,
    )
    down_sum = scatter_rows(
        contract_rows(hidden, upstream_group).astype(jnp.bfloat16), down_weight.shape[0]
    ).astype(jnp.float32)

    post_gain_term = jnp.sum(second_normed_grad * second_normalized, axis=0)
    second_scaled = second_normed_grad * post_gain
    hidden_one_grad = upstream.astype(jnp.float32) + second_inverse_norm * (
        second_scaled
        - second_normalized * jnp.mean(second_scaled * second_normalized, axis=-1, keepdims=True)
    )
    proj_grad = hidden_one_grad.astype(jnp.bfloat16)
    output_term = contract_rows(attended, proj_grad).astype(jnp.bfloat16)
    attended_grad = contract_cols(proj_grad, weight_output).astype(jnp.bfloat16)
    grad_groups = to_groups(attended_grad, local_rows, shard_tokens)
    prob_grad = jnp.einsum(
        "rgmd,rgkd->rgmk", grad_groups, value_heads, preferred_element_type=jnp.float32
    )
    prob_delta = jnp.sum(probs * prob_grad, axis=-1, keepdims=True)
    score_grad = (probs * (prob_grad - prob_delta)).astype(jnp.bfloat16)
    query_sum = jnp.einsum(
        "rgmk,rgkd->rgmd", score_grad, key_heads, preferred_element_type=jnp.float32
    )
    key_part = jnp.einsum(
        "rgmk,rgmd->rkgd", score_grad, query_groups, preferred_element_type=jnp.float32
    )
    value_part = jnp.einsum(
        "rgmk,rgmd->rkgd", probs_low, grad_groups, preferred_element_type=jnp.float32
    )
    both_terms = jnp.concatenate(
        [
            (key_part * scaling).reshape(local_rows, row_length, key_width),
            value_part.reshape(local_rows, row_length, key_width),
        ],
        axis=2,
    ).astype(jnp.bfloat16)
    both_sums = lax.psum_scatter(both_terms, ROW, scatter_dimension=1, tiled=True)
    both_sums = both_sums.reshape(flat_count, 2 * key_width).astype(jnp.float32)
    queries_grad = from_groups(query_sum, local_rows, shard_tokens) * scaling
    query_grad = (
        rotate_back(queries_grad.reshape(flat_count, H, HD), cosine, sine)
        .reshape(flat_count, H * HD)
        .astype(jnp.bfloat16)
    )
    key_grad = (
        rotate_back(both_sums[:, :key_width].reshape(flat_count, KV, HD), cosine, sine)
        .reshape(flat_count, key_width)
        .astype(jnp.bfloat16)
    )
    value_grad = both_sums[:, key_width:].astype(jnp.bfloat16)
    pair_grad = jnp.concatenate([key_grad, value_grad], axis=1)
    query_term = contract_rows(first_normed, query_grad).astype(jnp.bfloat16)
    pair_term = contract_rows(first_normed, pair_grad).astype(jnp.bfloat16)
    query_bias_term = jnp.sum(query_grad.astype(jnp.float32), axis=0)
    pair_bias_term = jnp.sum(pair_grad.astype(jnp.float32), axis=0)
    first_normed_grad = contract_cols(query_grad, projections[:, :query_width]) + contract_cols(
        pair_grad, projections[:, query_width:]
    )
    input_gain_term = jnp.sum(first_normed_grad * first_normalized, axis=0)
    first_scaled = first_normed_grad * input_gain
    input_grad = hidden_one_grad + first_inverse_norm * (
        first_scaled
        - first_normalized * jnp.mean(first_scaled * first_normalized, axis=-1, keepdims=True)
    )
    small_terms = jnp.concatenate(
        [
            pair_bias_term[:key_width].reshape(devices, owned_key),
            pair_bias_term[key_width:].reshape(devices, owned_key),
            jnp.zeros((devices, owned - 2 * owned_key), jnp.float32),
        ],
        axis=1,
    ).reshape(-1)
    vector_terms = column_pack(
        (query_bias_term, input_gain_term, post_gain_term, small_terms), width
    ).astype(jnp.bfloat16)
    output_sum = lax.psum_scatter(output_term, EVERY, scatter_dimension=0, tiled=True)
    query_sum_out = lax.psum_scatter(query_term, EVERY, scatter_dimension=0, tiled=True)
    last = lax.psum_scatter(
        jnp.concatenate([pair_term, vector_terms], axis=1), EVERY, scatter_dimension=0, tiled=True
    ).astype(jnp.float32)
    vector_sums = last[:, 2 * key_width :]
    return (
        layer_output.reshape(local_rows, shard_tokens, width),
        input_grad.astype(jnp.bfloat16).reshape(local_rows, shard_tokens, width),
        query_sum_out.astype(jnp.float32),
        last[:, :key_width],
        last[:, key_width : 2 * key_width],
        vector_sums[:, 0],
        vector_sums[:owned_key, 3],
        vector_sums[owned_key : 2 * owned_key, 3],
        output_sum.astype(jnp.float32),
        vector_sums[:, 1],
        vector_sums[:, 2],
        gate_sum,
        up_sum,
        down_sum,
    )


def solution(mesh):
    depth, across = mesh.devices.shape
    plane = across // 2
    side = math.isqrt(plane)
    inner = Mesh(mesh.devices.reshape(depth, plane // side, side, 2), EVERY)
    over_rows = P("z", ROW, None)
    whole, flat = P(EVERY, None), P(EVERY)
    in_specs = (
        (over_rows, P("z", None))
        + (whole,) * 3
        + (flat,) * 3
        + (whole, flat, flat)
        + (whole,) * 3
        + (over_rows,)
    )
    out_specs = (
        (over_rows,) * 2 + (whole,) * 3 + (flat,) * 3 + (whole, flat, flat) + (whole,) * 3
    )
    return jax.shard_map(
        shards, mesh=inner, in_specs=in_specs, out_specs=out_specs, check_vma=False
    )
```

```python
import math

import jax
import jax.numpy as jnp
from jax import lax
from jax.experimental import pallas as pl
from jax.experimental.pallas import tpu as pltpu
from jax.sharding import Mesh
from jax.sharding import PartitionSpec as P

H = 12
KV = 2
HD = 128
HPG = 6


epsilon = 1e-06
rope_base = 10000.0
masked_value = -1e30


def root_mean_square_scale(values):
    return lax.rsqrt(jnp.mean(values * values, axis=-1, keepdims=True) + epsilon)


def rope_tables(within):
    steps_even = jnp.arange(0, HD, 2).astype(jnp.float32)
    inverse = rope_base ** (-steps_even / HD)
    phase = within.astype(jnp.float32)[:, None] * inverse[None, :]
    phase = jnp.concatenate([phase, phase], axis=-1)
    return (jnp.cos(phase)[:, None, :], jnp.sin(phase)[:, None, :])


def rotate(values, cosine, sine):
    halfway = values.shape[-1] // 2
    return (
        values * cosine
        + jnp.concatenate([-values[..., halfway:], values[..., :halfway]], axis=-1) * sine
    )


def rotate_back(grads, cosine, sine):
    halfway = grads.shape[-1] // 2
    turned = grads * sine
    return grads * cosine + jnp.concatenate(
        [turned[..., halfway:], -turned[..., :halfway]], axis=-1
    )


def doc_tables(doc_ends, doc_lengths, positions):
    passed = doc_ends[:, None, :] <= positions[None, :, None]
    doc_index = jnp.sum(passed.astype(jnp.int32), axis=-1)
    starts = jnp.sum(jnp.where(passed, doc_lengths[:, None, :], 0), axis=-1)
    return (doc_index, positions[None, :] - starts)


def contract_rows(left, right):
    return lax.dot_general(
        left, right, (((0,), (0,)), ((), ())), preferred_element_type=jnp.float32
    )


def contract_cols(left, right):
    return lax.dot_general(
        left, right, (((1,), (1,)), ((), ())), preferred_element_type=jnp.float32
    )


EVERY = ("z", "y", "x", "c")
ROW = ("y", "x", "c")
PLANE = ("y", "x")


def low(values):
    return values.astype(jnp.bfloat16)


def wide(values):
    return values.astype(jnp.float32)


def after(values, *others):
    return lax.optimization_barrier((values, others))[0]


def swapped(values, axis):
    return lax.ppermute(values, axis, [(0, 1), (1, 0)])


def shifted(values, amount):
    count = lax.axis_size("z")
    return lax.ppermute(values, "z", [(i, (i + amount) % count) for i in range(count)])


def square():
    return lax.axis_size("y") == 2 and lax.axis_size("x") == 2


def pick(values, index, axis):
    return lax.dynamic_index_in_dim(values, index, axis, keepdims=False)


def put(buffer, block, index, axis=0):
    index = tuple(index)
    shape = buffer.shape[:axis] + (1,) * len(index) + buffer.shape[axis + len(index) :]
    start = (0,) * axis + index + (0,) * (buffer.ndim - axis - len(index))
    return lax.dynamic_update_slice(buffer, block.reshape(shape), start)


def by_core_pair(own, other):
    first = lax.axis_index("c") == 0
    return jnp.where(first, own, other), jnp.where(first, other, own)


def side_by_side(own, other):
    return jnp.where(
        lax.axis_index("c") == 0,
        jnp.concatenate([own, other], axis=-1),
        jnp.concatenate([other, own], axis=-1),
    )


def other_first(rows):
    half = rows.shape[0] // 2
    return jnp.concatenate([rows[half:], rows[:half]], axis=0)


def near_shifts():
    return sorted({1, lax.axis_size("z") - 1})


def far_shifts():
    return range(2, lax.axis_size("z") - 1)


def depth_sent(blocks, shifts):
    nz, z = lax.axis_size("z"), lax.axis_index("z")
    return {k: shifted(pick(blocks, (z + k) % nz, 0), k) for k in shifts}


def own_block(blocks):
    return {0: pick(blocks, lax.axis_index("z"), 0)}


def depth_gathered(rows, shifts):
    return {k: shifted(rows, k) for k in shifts}


def depth_returned(blocks, shifts):
    return {k: shifted(low(blocks[k]), -k) for k in shifts}


def depth_placed(pieces):
    nz, z = lax.axis_size("z"), lax.axis_index("z")
    buffer = jnp.zeros((nz,) + pieces[0].shape, pieces[0].dtype)
    for k in range(nz):
        buffer = put(buffer, pieces[k], ((z - k) % nz,))
    return buffer


def in_order(pieces):
    return [pieces[k] for k in sorted(pieces)]


def sync(*values):
    return lax.optimization_barrier(values)


def nn(left, right):
    return jnp.dot(left, right, preferred_element_type=jnp.float32)


SPACE = pltpu.CompilerParams(vmem_limit_bytes=48 << 20)


def spread_columns(gate_weight, up_weight, sizes, unit, lane):
    nz, ny, nx, nc = sizes
    rows = gate_weight.shape[0]

    def kernel(gate_ref, up_ref, out_ref):
        out_ref[...] = jnp.zeros_like(out_ref)
        for m, ref in enumerate((gate_ref, up_ref)):
            for d in range(nz * ny * nx * nc):
                z, p, c = d // (ny * nx * nc), d // nc % (ny * nx), d % nc
                out_ref[c, z, m, :, lane * p : lane * p + unit] = ref[:, unit * d : unit * d + unit]

    shape = (nc, nz, 2, rows, lane * ny * nx)
    return pl.pallas_call(
        kernel,
        out_shape=jax.ShapeDtypeStruct(shape, jnp.bfloat16),
        compiler_params=SPACE,
        cost_estimate=LITTLE,
    )(gate_weight, up_weight)


def collect_columns(blocks, sizes, unit, lane):
    nz, ny, nx, nc = sizes
    rows = blocks.shape[3]

    def kernel(blocks_ref, gate_ref, up_ref):
        for m, ref in enumerate((gate_ref, up_ref)):
            for d in range(nz * ny * nx * nc):
                z, p, c = d // (ny * nx * nc), d // nc % (ny * nx), d % nc
                ref[:, unit * d : unit * d + unit] = wide(
                    blocks_ref[z, c, m, :, lane * p : lane * p + unit]
                )

    shape = jax.ShapeDtypeStruct((rows, unit * nz * ny * nx * nc), jnp.float32)
    return pl.pallas_call(
        kernel, out_shape=(shape, shape), compiler_params=SPACE, cost_estimate=LITTLE
    )(blocks)


def feed_forward(normed, upstream, weight_gate, weight_up, weight_down):
    count, width = normed.shape
    hidden_width = weight_gate.shape[1]
    tile = min(256, count)

    def kernel(normed_ref, up_ref, wg, wu, wd, grad_ref, hidden_ref, gate_ref, upg_ref):
        normed = normed_ref[...]
        gate = nn(normed, wg[...])
        up = nn(normed, wu[...])
        back = contract_cols(up_ref[...], wd[...])
        sigmoid = jax.nn.sigmoid(gate)
        silu = gate * sigmoid
        hidden = low(silu * up)
        gate_grad = low(back * up * sigmoid * (1.0 + gate * (1.0 - sigmoid)))
        up_grad = low(back * silu)
        hidden_ref[...] = hidden
        gate_ref[...] = gate_grad
        upg_ref[...] = up_grad
        grad_ref[...] = low(contract_cols(gate_grad, wg[...]) + contract_cols(up_grad, wu[...]))

    def rows(columns):
        return pl.BlockSpec((tile, columns), lambda i: (i, 0))

    def whole(array):
        return pl.BlockSpec(array.shape, lambda i: (0, 0))

    columns = (width, hidden_width, hidden_width, hidden_width)
    return pl.pallas_call(
        kernel,
        grid=(count // tile,),
        in_specs=[rows(width), rows(width), whole(weight_gate), whole(weight_up), whole(weight_down)],
        out_specs=[rows(n) for n in columns],
        out_shape=[jax.ShapeDtypeStruct((count, n), jnp.bfloat16) for n in columns],
        compiler_params=SPACE,
        cost_estimate=LITTLE,
    )(normed, upstream, weight_gate, weight_up, weight_down)


LITTLE = pl.CostEstimate(flops=1, bytes_accessed=1, transcendentals=0)


def turn(values, cosine, sine):
    return values * cosine + pltpu.roll(values, HD // 2, 1) * sine


def inner_projections(tokens, weight, vectors, cosine, sine, core, owned, owned_key):
    cores, local_rows, count, width = tokens.shape
    total = cores * local_rows * count
    half = width // 2

    def kernel(core_ref, tokens_ref, weight_ref, vectors_ref, cos_ref, sin_ref, n_ref, q_ref, pair_ref, line_ref):
        lines = wide(vectors_ref[...]).T
        at = core_ref[0]
        values = wide(tokens_ref[...].reshape(total, width))
        scale = lax.rsqrt(jnp.mean(values * values, axis=-1, keepdims=True) + epsilon)
        normed = low(values * scale * lines[1:2])
        n_ref[...] = normed
        line_ref[...] = lines[:8]
        source = lax.broadcasted_iota(jnp.int32, (width, HD), 0)
        feature = lax.broadcasted_iota(jnp.int32, (width, HD), 1) + at * HD
        place = feature // owned_key * owned + feature % owned_key
        small = low(lines[3:4])
        key_bias = nn(small, low(wide(source == place)))
        value_bias = nn(small, low(wide(source == place + owned_key)))
        bias = jnp.where(at == 0, lines[0:1, :half], lines[0:1, half:])
        pre = nn(normed, weight_ref[...])
        cosine, sine = cos_ref[...], sin_ref[...]
        for h in range(HPG):
            block = slice(h * HD, (h + 1) * HD)
            query = low(turn(pre[:, block] + bias[:, block], cosine, sine))
            query = query.reshape(cores, local_rows, count, HD)
            for r in range(local_rows):
                q_ref[r, h] = query[:, r]
        key = low(turn(pre[:, half : half + HD] + key_bias, cosine, sine))
        value = low(pre[:, half + HD :] + value_bias)
        shape = (cores, local_rows, count, HD)
        pair_ref[..., :HD] = key.reshape(shape)
        pair_ref[..., HD:] = value.reshape(shape)

    vmem = pl.BlockSpec(memory_space=pltpu.VMEM)
    return pl.pallas_call(
        kernel,
        in_specs=[pl.BlockSpec(memory_space=pltpu.SMEM)] + [vmem] * 5,
        out_specs=[vmem] * 4,
        out_shape=[
            jax.ShapeDtypeStruct((total, width), jnp.bfloat16),
            jax.ShapeDtypeStruct((local_rows, HPG, cores, count, HD), jnp.bfloat16),
            jax.ShapeDtypeStruct((cores, local_rows, count, 2 * HD), jnp.bfloat16),
            jax.ShapeDtypeStruct((8, width), jnp.float32),
        ],
        compiler_params=SPACE,
        cost_estimate=LITTLE,
    )(core.reshape(1), tokens, weight, vectors, cosine, sine)


def row_scores(query, keys, allowed):
    scores = contract_cols(query, keys) * (1.0 / math.sqrt(HD))
    return jnp.where(allowed, scores, masked_value)


def row_specs(pairs, cores, count):
    keys = pl.BlockSpec((pairs.shape[0], cores, 1, count, 2 * HD), lambda r: (0, 0, r, 0, 0))
    queries = pl.BlockSpec((1, HPG, cores, count, HD), lambda r: (r, 0, 0, 0, 0))
    flat = pl.BlockSpec((cores, 1, count, HPG * HD), lambda r: (0, r, 0, 0))
    stats = pl.BlockSpec((1, HPG, cores * count, HD), lambda r: (r, 0, 0, 0))
    allowed = pl.BlockSpec((1, cores * count, pairs.shape[0] * cores * count), lambda r: (r, 0, 0))
    return keys, queries, flat, stats, allowed


def attend(queries, pairs, allowed):
    local_rows, heads, cores, count, hd = queries.shape
    total = cores * count
    keys, query_spec, flat, stats, allowed_spec = row_specs(pairs, cores, count)

    def kernel(q_ref, pair_ref, allowed_ref, out_ref, stat_ref):
        pair = pair_ref[...].reshape(-1, 2 * HD)
        key, value = pair[:, :HD], pair[:, HD:]
        seen = allowed_ref[0] > 0
        for h in range(heads):
            scores = row_scores(q_ref[0, h].reshape(total, HD), key, seen)
            top = jnp.max(scores, axis=-1, keepdims=True)
            log_total = top + jnp.log(jnp.sum(jnp.exp(scores - top), axis=-1, keepdims=True))
            mixed = low(nn(low(jnp.exp(scores - log_total)), value))
            out_ref[:, 0, :, h * HD : (h + 1) * HD] = mixed.reshape(cores, count, HD)
            stat_ref[0, h] = jnp.broadcast_to(log_total, (total, HD))

    return pl.pallas_call(
        kernel,
        grid=(local_rows,),
        in_specs=[query_spec, keys, allowed_spec],
        out_specs=[flat, stats],
        out_shape=[
            jax.ShapeDtypeStruct((cores, local_rows, count, heads * HD), jnp.bfloat16),
            jax.ShapeDtypeStruct((local_rows, heads, total, HD), jnp.float32),
        ],
        compiler_params=SPACE,
        cost_estimate=LITTLE,
    )(queries, pairs, allowed)


def attend_back(queries, pairs, allowed, stats, grads, cosine, sine):
    local_rows, heads, cores, count, hd = queries.shape
    total = cores * count
    scaling = 1.0 / math.sqrt(HD)
    keys, query_spec, flat, stat_spec, allowed_spec = row_specs(pairs, cores, count)
    table = pl.BlockSpec((cores, 1, count, HD), lambda r: (0, r, 0, 0))

    def kernel(q_ref, pair_ref, allowed_ref, stat_ref, grad_ref, cos_ref, sin_ref, out_ref, part_ref):
        pair = pair_ref[...].reshape(-1, 2 * HD)
        key, value = pair[:, :HD], pair[:, HD:]
        seen = allowed_ref[0] > 0
        cosine, sine = (ref[...].reshape(total, HD) for ref in (cos_ref, sin_ref))
        key_part = jnp.zeros(key.shape, jnp.float32)
        value_part = jnp.zeros(key.shape, jnp.float32)
        for h in range(heads):
            query = q_ref[0, h].reshape(total, HD)
            grad = grad_ref[:, 0, :, h * HD : (h + 1) * HD].reshape(total, HD)
            probs = jnp.exp(row_scores(query, key, seen) - stat_ref[0, h][:, :1])
            back = contract_cols(grad, value)
            delta = jnp.sum(probs * back, axis=-1, keepdims=True)
            score_grad = low(probs * (back - delta))
            key_part = key_part + contract_rows(score_grad, query)
            value_part = value_part + contract_rows(low(probs), grad)
            query_sum = nn(score_grad, key) * scaling
            turned = query_sum * cosine + pltpu.roll(query_sum * sine, HD // 2, 1)
            out_ref[:, 0, :, h * HD : (h + 1) * HD] = low(turned).reshape(cores, count, HD)
        shape = (pair_ref.shape[0], cores, count, HD)
        part_ref[:, :, 0, :, :HD] = low(key_part * scaling).reshape(shape)
        part_ref[:, :, 0, :, HD:] = low(value_part).reshape(shape)

    return pl.pallas_call(
        kernel,
        grid=(local_rows,),
        in_specs=[query_spec, keys, allowed_spec, stat_spec, flat, table, table],
        out_specs=[flat, keys],
        out_shape=[
            jax.ShapeDtypeStruct((cores, local_rows, count, heads * HD), jnp.bfloat16),
            jax.ShapeDtypeStruct(pairs.shape, jnp.bfloat16),
        ],
        compiler_params=SPACE,
        cost_estimate=LITTLE,
    )(queries, pairs, allowed, stats, grads, cosine, sine)


def weight_grads(left, rights):
    count, rows = left.shape
    tile = 256 if rows % 256 == 0 else 128

    def kernel(left_ref, *refs):
        turned = left_ref[...].T
        for right_ref, out_ref in zip(refs[: len(rights)], refs[len(rights) :]):
            out_ref[...] = low(nn(turned, right_ref[...]))

    return pl.pallas_call(
        kernel,
        grid=(rows // tile,),
        in_specs=[pl.BlockSpec((count, tile), lambda i: (0, i))]
        + [pl.BlockSpec(r.shape, lambda i: (0, 0)) for r in rights],
        out_specs=[pl.BlockSpec((tile, r.shape[1]), lambda i: (i, 0)) for r in rights],
        out_shape=[jax.ShapeDtypeStruct((rows, r.shape[1]), jnp.bfloat16) for r in rights],
        compiler_params=SPACE,
        cost_estimate=LITTLE,
    )(left, *rights)


def plane_near(values):
    if not square():
        return ()
    return swapped(values, "x"), swapped(values, "y")


def plane_far(near, first, second):
    if not square():
        return ()
    return swapped(first(near[0]), "y"), swapped(second(near[1]), "x")


def plane_place(pieces, axis):
    y, x = lax.axis_index("y"), lax.axis_index("x")
    shape = pieces[0].shape
    buffer = jnp.zeros(shape[:axis] + (2, 2) + shape[axis:], pieces[0].dtype)
    for piece, index in zip(pieces, ((y, x), (y, 1 - x), (1 - y, x), (1 - y, 1 - x))):
        buffer = put(buffer, piece, index, axis)
    return buffer


def gather_plane(own, near, far, axis):
    if square():
        return plane_place((own, *near, far), axis)
    whole = lax.all_gather(own, PLANE, axis=axis, tiled=False)
    ny, nx = lax.axis_size("y"), lax.axis_size("x")
    return whole.reshape(own.shape[:axis] + (ny, nx) + own.shape[axis:])


def plane_reduced(pair, axis, step):
    if not square():
        if step:
            return pair
        out = []
        for v in pair:
            flat = v.reshape(v.shape[:axis] + (-1,) + v.shape[axis + 2 :])
            out.append(lax.psum_scatter(flat, PLANE, scatter_dimension=axis, tiled=False))
        return out
    out = []
    for left, name in zip(pair, ("yx", "xy")[step]):
        at = lax.axis_index(name)
        dim = axis if step or name == "y" else axis + 1
        came = swapped(pick(left, 1 - at, dim), name)
        out.append(low(wide(pick(left, at, dim)) + wide(came)))
    return out


def plane_gathered(rows):
    if not square():
        return lax.all_gather(rows, PLANE, axis=0)
    pair = jnp.stack([rows, swapped(rows, "x")])
    return jnp.concatenate([pair, swapped(pair, "y")], axis=0)


def plane_summed(blocks):
    if not square():
        return wide(lax.psum_scatter(blocks, PLANE, scatter_dimension=0, tiled=False))
    pair = low(wide(blocks[:2]) + wide(swapped(blocks[2:], "y")))
    return wide(pair[0]) + wide(swapped(pair[1], "x"))


def places():
    y, x = lax.axis_index("y"), lax.axis_index("x")
    if square():
        return [(y, x), (y, 1 - x), (1 - y, x), (1 - y, 1 - x)]
    return [(i, j) for i in range(lax.axis_size("y")) for j in range(lax.axis_size("x"))]


def chip_positions(y, x, shard_tokens):
    core = lax.axis_index("c")
    place = (y * lax.axis_size("x") + x) * 2
    lanes = jnp.arange(shard_tokens, dtype=jnp.int32)
    return [(place + k) * shard_tokens + lanes for k in (core, 1 - core)]


def position_tables(doc_lengths, shard_tokens):
    local_rows = doc_lengths.shape[0]
    query_pos = jnp.concatenate(
        chip_positions(lax.axis_index("y"), lax.axis_index("x"), shard_tokens)
    )
    key_pos = jnp.concatenate(
        [p for place in places() for p in chip_positions(*place, shard_tokens)]
    )
    doc_ends = jnp.cumsum(doc_lengths, axis=1)
    query_doc, query_within = doc_tables(doc_ends, doc_lengths, query_pos)
    key_doc, unused_within = doc_tables(doc_ends, doc_lengths, key_pos)
    allowed = (query_doc[:, :, None] == key_doc[:, None, :]) & (
        key_pos[None, None, :] <= query_pos[None, :, None]
    )
    query_within = query_within.reshape(local_rows, 2, shard_tokens).transpose(1, 0, 2)
    cosine, sine = rope_tables(query_within.reshape(-1))
    sign = jnp.where(jnp.arange(HD) < HD // 2, -1.0, 1.0)
    return cosine[:, 0], sine[:, 0] * sign, wide(allowed)


def column_pack(columns, rows):
    padded = [jnp.pad(v, (0, rows - v.shape[0])) for v in columns]
    packed = jnp.stack(padded, axis=1)
    return jnp.pad(packed, ((0, 0), (0, 128 - len(columns))))


def shards(
    tokens,
    doc_lengths,
    query_weight,
    key_weight,
    value_weight,
    query_bias,
    key_bias,
    value_bias,
    output_weight,
    attention_norm_gain,
    feedforward_norm_gain,
    gate_weight,
    up_weight,
    down_weight,
    cotangent,
):
    local_rows, shard_tokens, width = tokens.shape
    nz, ny, nx, nc = (lax.axis_size(a) for a in EVERY)
    core = lax.axis_index("c")
    devices = nz * ny * nx * nc
    flat_count = local_rows * shard_tokens
    chip_count = 2 * flat_count
    row_length = shard_tokens * ny * nx * nc
    scaling = 1.0 / math.sqrt(HD)
    owned, query_width = query_weight.shape
    key_width = key_weight.shape[1]
    owned_key = key_bias.shape[0]
    half = query_width // 2

    unit = gate_weight.shape[1] // devices
    sizes = (nz, ny, nx, nc)
    lane = -(-ny * nx * unit // 128) * 128 // (ny * nx)
    hidden_width = ny * nx * lane
    own_tokens = tokens.reshape(flat_count, width)
    upstream = cotangent.reshape(flat_count, width)

    down_near = plane_near(down_weight)
    vectors = column_pack(
        (
            query_bias,
            attention_norm_gain,
            feedforward_norm_gain,
            jnp.concatenate([key_bias, value_bias]),
        ),
        owned,
    )
    packed = jnp.concatenate([query_weight, key_weight, value_weight, vectors], axis=1)
    every_shift = range(1, nz)
    pieces = depth_gathered(packed, every_shift)
    pieces[0] = packed
    both = spread_columns(gate_weight, up_weight, sizes, unit, lane)
    cosine, sine, allowed = position_tables(doc_lengths, shard_tokens)
    pieces, down_near, both, cosine, sine, allowed = sync(
        pieces, down_near, both, cosine, sine, allowed
    )

    def core_columns(of):
        return jnp.concatenate(
            [
                lax.dynamic_slice_in_dim(whole, of * half, half, 2),
                lax.dynamic_slice_in_dim(whole, query_width + of * HD, HD, 2),
                lax.dynamic_slice_in_dim(whole, query_width + key_width + of * HD, HD, 2),
                whole[..., query_width + 2 * key_width :],
            ],
            axis=2,
        )

    whole = depth_placed(pieces)
    mine, came = core_columns(core), swapped(core_columns(1 - core), "c")
    both_came = swapped(pick(both, 1 - core, 0), "c")
    both = pick(both, core, 0)
    output_weight = after(output_weight, pieces)
    output_pieces = depth_gathered(output_weight, every_shift)
    output_pieces[0] = output_weight
    mine, came, both, both_came, output_pieces = sync(mine, came, both, both_came, output_pieces)

    inner_own = jnp.stack(by_core_pair(mine, came), axis=1)
    inner_near = plane_near(inner_own)
    both_all = jnp.stack(by_core_pair(both, both_came), axis=2)
    both = depth_sent(both_all, near_shifts())
    both |= own_block(both_all)
    chip_tokens = jnp.concatenate([own_tokens, swapped(own_tokens, "c")], axis=0)
    output_all = depth_placed(output_pieces)
    output_mine = lax.dynamic_slice_in_dim(output_all, core * (width // 2), width // 2, 2)
    output_other = lax.dynamic_slice_in_dim(output_all, (1 - core) * (width // 2), width // 2, 2)
    inner_own, inner_near, output_mine, output_other, both, both_all, chip_tokens = sync(
        inner_own, inner_near, output_mine, output_other, both, both_all, chip_tokens
    )
    middle = 512
    inner_far = plane_far(inner_near, lambda v: v[..., :middle], lambda v: v[..., middle:])
    both |= depth_sent(both_all, far_shifts())
    down_far = plane_far(down_near, lambda v: v[: unit // 2], lambda v: v[unit // 2 :])
    inner_own, inner_near, inner_far, output_mine, output_other, both, down_far = sync(
        inner_own, inner_near, inner_far, output_mine, output_other, both, down_far
    )

    output_came = swapped(output_other, "c")
    output_own = jnp.stack(by_core_pair(output_mine, output_came), axis=1)
    output_near = plane_near(output_own)
    upstream_pieces = depth_gathered(after(upstream, both), near_shifts())
    both = depth_placed(both)
    if square():
        inner_far = jnp.concatenate(inner_far, axis=-1)
    attention = gather_plane(inner_own, inner_near, inner_far, 1).reshape(width, -1)
    at = half + 2 * HD
    weight_inner = attention[:, :at]
    chip_shape = (2, local_rows, shard_tokens)
    cosine = cosine.reshape(chip_shape + (HD,))
    sine = sine.reshape(chip_shape + (HD,))
    first_normed, queries, own_pair, lines = inner_projections(
        chip_tokens.reshape(chip_shape + (width,)),
        weight_inner,
        attention[:, at:],
        cosine.reshape(chip_count, HD),
        sine.reshape(chip_count, HD),
        core,
        owned,
        owned_key,
    )
    input_gain, post_gain = lines[1], lines[2]
    own_pair, output_own, output_near, upstream_pieces, both = sync(
        own_pair, output_own, output_near, upstream_pieces, both
    )
    upstream_pieces |= depth_gathered(after(upstream, own_pair), far_shifts())
    upstream_pieces[0] = upstream
    output_far = plane_far(
        output_near, lambda v: v[..., : width // 4], lambda v: v[..., width // 4 :]
    )

    pairs = plane_gathered(own_pair)
    pairs, output_far, upstream_pieces, both = sync(pairs, output_far, upstream_pieces, both)
    gate_near = plane_near(both[:, 0])
    attended, log_sums = attend(queries, pairs, allowed)
    attended = attended.reshape(chip_count, half)
    attended, gate_near, both = sync(attended, gate_near, both)
    up_near = plane_near(both[:, 1])
    if square():
        output_far = jnp.concatenate(output_far, axis=-1)
    weight_output = gather_plane(output_own, output_near, output_far, 1).reshape(width, -1)
    attended = side_by_side(attended, swapped(other_first(attended), "c"))
    output_part = nn(attended, weight_output)
    output_sum = side_by_side(
        output_part[:flat_count], swapped(output_part[flat_count:], "c")
    )
    own_wide = wide(own_tokens)
    first_hidden = own_wide + output_sum
    second_inverse_norm = root_mean_square_scale(first_hidden)
    second_normalized = first_hidden * second_inverse_norm
    second_normed = low(second_normalized * post_gain)

    second_normed, up_near = sync(second_normed, up_near)
    second_pieces = depth_gathered(second_normed, every_shift)
    second_pieces[0] = second_normed
    upstream_mine = jnp.concatenate(in_order(upstream_pieces), axis=0)
    upstream_other = swapped(upstream_mine, "c")
    gate_far = up_far = None
    if square():
        gate_far, up_far = swapped(gate_near[0], "y"), swapped(up_near[1], "x")
    second_pieces, gate_far, up_far, upstream_other = sync(
        second_pieces, gate_far, up_far, upstream_other
    )
    weight_gate = gather_plane(both[:, 0], gate_near, gate_far, 1).reshape(width, hidden_width)
    weight_up = gather_plane(both[:, 1], up_near, up_far, 1).reshape(width, hidden_width)
    if square():
        down_far = jnp.concatenate(down_far, axis=0)
    weight_down = gather_plane(down_weight, down_near, down_far, 0)
    weight_down = jnp.pad(weight_down, ((0, 0), (0, 0), (0, lane - unit), (0, 0)))
    weight_down = weight_down.reshape(hidden_width, width)

    second_mine = jnp.concatenate(in_order(second_pieces), axis=0)
    second_group = jnp.concatenate([swapped(second_mine, "c"), second_mine], axis=0)
    upstream_group = jnp.concatenate([upstream_other, upstream_mine], axis=0)
    normed_part, hidden, gate_grad, up_grad = feed_forward(
        second_group, upstream_group, weight_gate, weight_up, weight_down
    )
    group = second_mine.shape[0]
    normed_came = swapped(normed_part[:group], "c")
    gate_term, up_term = weight_grads(second_group, (gate_grad, up_grad))
    normed_came, gate_term, up_term = sync(normed_came, gate_term, up_term)
    normed_sum = (wide(normed_part[group:]) + wide(normed_came)).reshape(nz, flat_count, width)
    normed_pieces = depth_returned(normed_sum, every_shift)
    six = (nz, ny, nx, nc, owned, hidden_width)
    both = plane_reduced((gate_term.reshape(six), up_term.reshape(six)), 1, 0)
    hidden, weight_down = after((hidden, weight_down), normed_sum)
    (down_term,) = weight_grads(hidden, (upstream_group,))
    output_part = low(nn(hidden, weight_down))
    normed_pieces, down_term, output_part, normed_sum, both = sync(
        normed_pieces, down_term, output_part, normed_sum, both
    )
    second_normed_grad = normed_sum[0] + sum(wide(v) for v in in_order(normed_pieces))

    post_gain_term = jnp.sum(second_normed_grad * second_normalized, axis=0)
    second_scaled = second_normed_grad * post_gain
    hidden_one_grad = wide(upstream) + second_inverse_norm * (
        second_scaled
        - second_normalized * jnp.mean(second_scaled * second_normalized, axis=-1, keepdims=True)
    )
    proj_halves = low(hidden_one_grad).reshape(flat_count, 2, width // 2)
    proj_grad = jnp.concatenate(
        [pick(proj_halves, core, 1), swapped(pick(proj_halves, 1 - core, 1), "c")], axis=0
    )
    part = contract_cols(proj_grad, weight_output).reshape(chip_count, 2, half)
    came = swapped(other_first(pick(part, 1 - core, 1)), "c")
    attended_grad = low(pick(part, core, 1) + came)
    output_came = swapped(output_part[:group], "c")
    attended_grad, both, output_came = sync(attended_grad, both, output_came)
    output_sum = (wide(output_part[group:]) + wide(output_came)).reshape(nz, flat_count, width)
    both = plane_reduced(both, 1, 1)
    output_pieces = depth_returned(output_sum, near_shifts())
    query_grad, pair_part = attend_back(
        queries,
        pairs,
        allowed,
        log_sums,
        attended_grad.reshape(chip_shape + (half,)),
        cosine,
        sine,
    )
    query_grad = query_grad.reshape(chip_count, half)
    pair_part, both, output_pieces, output_sum = sync(pair_part, both, output_pieces, output_sum)
    pair_sum = plane_summed(pair_part)
    output_pieces |= depth_returned(output_sum, far_shifts())
    pair_sum = pair_sum.reshape(chip_count, 2 * HD)
    both = jnp.stack(both, axis=2)
    both_came = swapped(pick(both, 1 - core, 1), "c")
    both = jnp.stack(by_core_pair(pick(both, core, 1), both_came), axis=1)
    pair_sum, both, output_pieces = sync(pair_sum, both, output_pieces)
    down_term = after(down_term, pair_sum).reshape(ny, nx, lane, width)
    down_sum = plane_reduced((down_term[:, :, : lane // 2], down_term[:, :, lane // 2 :]), 0, 0)
    key_sum = pair_sum[:, :HD]
    turned = jnp.roll(key_sum * sine.reshape(chip_count, HD), HD // 2, axis=1)
    key_grad = low(key_sum * cosine.reshape(chip_count, HD) + turned)
    pair_grad = jnp.concatenate([key_grad, low(pair_sum[:, HD:])], axis=1)

    first_normed_grad = (
        contract_cols(jnp.concatenate([query_grad, pair_grad], axis=1), weight_inner)
    )
    first_normed_grad = first_normed_grad[:flat_count] + swapped(
        first_normed_grad[flat_count:], "c"
    )
    first_inverse_norm = root_mean_square_scale(own_wide)
    own_normalized = own_wide * first_inverse_norm
    input_gain_term = jnp.sum(first_normed_grad * own_normalized, axis=0)
    first_scaled = first_normed_grad * input_gain
    input_grad = hidden_one_grad + first_inverse_norm * (
        first_scaled
        - own_normalized * jnp.mean(first_scaled * own_normalized, axis=-1, keepdims=True)
    )

    query_bias_term = jnp.sum(wide(query_grad), axis=0)
    pair_bias_term = jnp.sum(wide(pair_grad), axis=0)
    inner_grad = jnp.concatenate([query_grad, pair_grad], axis=1)
    (output_term,) = weight_grads(attended, (proj_grad,))
    (inner_term,) = weight_grads(first_normed, (inner_grad,))

    def spread(term, size):
        return lax.dynamic_update_slice(jnp.zeros((size,), term.dtype), term, (core * term.shape[0],))

    small_terms = jnp.concatenate(
        [
            spread(pair_bias_term[:HD], key_width).reshape(devices, owned_key),
            spread(pair_bias_term[HD:], key_width).reshape(devices, owned_key),
            jnp.zeros((devices, owned - 2 * owned_key), jnp.float32),
        ],
        axis=1,
    ).reshape(-1)
    vector_terms = column_pack(
        (spread(query_bias_term, width), input_gain_term, post_gain_term, small_terms), width
    )
    five = (nz, ny, nx, nc, owned, -1)
    inner = (
        jnp.concatenate([output_term, low(vector_terms)], axis=1).reshape(five),
        inner_term.reshape(five),
    )
    inner, both, down_sum, output_pieces = sync(inner, both, down_sum, output_pieces)
    layer_output = low(
        first_hidden + output_sum[0] + sum(wide(v) for v in in_order(output_pieces))
    )
    inner = plane_reduced(inner, 1, 0)
    both_sent = depth_sent(both, every_shift) | own_block(both)
    inner, both_sent, down_sum = sync(inner, both_sent, down_sum)
    inner = plane_reduced(inner, 1, 1)
    gate_sum, up_sum = collect_columns(depth_placed(both_sent), sizes, unit, lane)
    inner, down_sum = sync(inner, down_sum)
    inner = jnp.concatenate(inner, axis=-1)
    pieces = depth_sent(inner, every_shift) | own_block(inner)
    down_sum = plane_reduced(down_sum, 0, 1)
    inner = sum(wide(v) for v in in_order(pieces))
    mine, came = pick(inner, core, 0), wide(swapped(low(pick(inner, 1 - core, 0)), "c"))
    ends = [width // 2, width // 2 + 128]
    ends += [ends[1] + half, ends[1] + half + HD]
    mine, came = (jnp.split(v, ends, axis=1) for v in (mine, came))
    output_term, query_term, key_term, value_term = (
        side_by_side(mine[i], came[i]) for i in (0, 2, 3, 4)
    )
    vector_sums = mine[1] + came[1]
    down_sum = wide(jnp.concatenate(down_sum, axis=0))[:unit]
    return (
        layer_output.reshape(local_rows, shard_tokens, width),
        low(input_grad).reshape(local_rows, shard_tokens, width),
        query_term,
        key_term,
        value_term,
        vector_sums[:, 0],
        vector_sums[:owned_key, 3],
        vector_sums[owned_key : 2 * owned_key, 3],
        output_term,
        vector_sums[:, 1],
        vector_sums[:, 2],
        gate_sum,
        up_sum,
        down_sum,
    )


def solution(mesh):
    depth, across = mesh.devices.shape
    plane = across // 2
    side = math.isqrt(plane)
    inner = Mesh(mesh.devices.reshape(depth, plane // side, side, 2), EVERY)
    over_rows = P("z", ROW, None)
    whole, flat = P(EVERY, None), P(EVERY)
    in_specs = (
        (over_rows, P("z", None))
        + (whole,) * 3
        + (flat,) * 3
        + (whole, flat, flat)
        + (whole,) * 3
        + (over_rows,)
    )
    out_specs = (
        (over_rows,) * 2 + (whole,) * 3 + (flat,) * 3 + (whole, flat, flat) + (whole,) * 3
    )
    return jax.shard_map(
        shards, mesh=inner, in_specs=in_specs, out_specs=out_specs, check_vma=False
    )
```

```python
import math

import jax
import jax.numpy as jnp
from jax import lax
from jax.experimental import pallas as pl
from jax.experimental.pallas import tpu as pltpu
from jax.sharding import Mesh
from jax.sharding import PartitionSpec as P

H = 12
KV = 2
HD = 128
HPG = 6

epsilon = 1e-06
rope_base = 10000.0
masked_value = -1e30

EVERY = ("z", "y", "x", "c")
ROW = ("y", "x", "c")
PLANE = ("y", "x")


def low(values):
    return values.astype(jnp.bfloat16)


def wide(values):
    return values.astype(jnp.float32)


def nn(left, right):
    return jnp.dot(left, right, preferred_element_type=jnp.float32)


def nt(left, right):
    return lax.dot_general(
        left, right, (((1,), (1,)), ((), ())), preferred_element_type=jnp.float32
    )


def tn(left, right):
    return lax.dot_general(
        left, right, (((0,), (0,)), ((), ())), preferred_element_type=jnp.float32
    )


def doc_tables(doc_ends, doc_lengths, positions):
    passed = doc_ends[:, None, :] <= positions[None, :, None]
    doc_index = jnp.sum(passed.astype(jnp.int32), axis=-1)
    starts = jnp.sum(jnp.where(passed, doc_lengths[:, None, :], 0), axis=-1)
    return (doc_index, positions[None, :] - starts)


def rope_tables(within):
    steps_even = jnp.arange(0, HD, 2).astype(jnp.float32)
    inverse = rope_base ** (-steps_even / HD)
    phase = within.astype(jnp.float32)[:, None] * inverse[None, :]
    phase = jnp.concatenate([phase, phase], axis=-1)
    return jnp.cos(phase), jnp.sin(phase)


def square():
    return lax.axis_size("y") == 2 and lax.axis_size("x") == 2


def places():
    y, x = lax.axis_index("y"), lax.axis_index("x")
    if square():
        return [(y, x), (y, 1 - x), (1 - y, x), (1 - y, 1 - x)]
    return [(i, j) for i in range(lax.axis_size("y")) for j in range(lax.axis_size("x"))]


def chip_positions(y, x, shard_tokens):
    core = lax.axis_index("c")
    place = (y * lax.axis_size("x") + x) * 2
    lanes = jnp.arange(shard_tokens, dtype=jnp.int32)
    return [(place + k) * shard_tokens + lanes for k in (core, 1 - core)]


def position_tables(doc_lengths, shard_tokens):
    local_rows = doc_lengths.shape[0]
    query_pos = jnp.concatenate(
        chip_positions(lax.axis_index("y"), lax.axis_index("x"), shard_tokens)
    )
    key_pos = jnp.concatenate(
        [p for place in places() for p in chip_positions(*place, shard_tokens)]
    )
    doc_ends = jnp.cumsum(doc_lengths, axis=1)
    query_doc, query_within = doc_tables(doc_ends, doc_lengths, query_pos)
    key_doc, unused_within = doc_tables(doc_ends, doc_lengths, key_pos)
    allowed = (query_doc[:, :, None] == key_doc[:, None, :]) & (
        key_pos[None, None, :] <= query_pos[None, :, None]
    )
    query_within = query_within.reshape(local_rows, 2, shard_tokens).transpose(1, 0, 2)
    cosine, sine = rope_tables(query_within.reshape(-1))
    sign = jnp.where(jnp.arange(HD) < HD // 2, -1.0, 1.0)
    return cosine, sine * sign, wide(allowed)


def sync(*values):
    return lax.optimization_barrier(values)


def after(values, *others):
    return lax.optimization_barrier((values, others))[0]


def swapped(values, axis):
    return lax.ppermute(values, axis, [(0, 1), (1, 0)])


def shifted(values, amount):
    count = lax.axis_size("z")
    return lax.ppermute(values, "z", [(i, (i + amount) % count) for i in range(count)])


def every_shift():
    return range(1, lax.axis_size("z"))


def near_shifts():
    return sorted({1, lax.axis_size("z") - 1})


def far_shifts():
    return range(2, lax.axis_size("z") - 1)


def depth_gathered(rows, shifts):
    return {k: shifted(rows, k) for k in shifts}


def depth_sent(blocks, shifts):
    return {k: shifted(blocks[k], k) for k in shifts}


def in_order(pieces):
    return [pieces[k] for k in sorted(pieces)]


def plane_near(values):
    return swapped(values, "x"), swapped(values, "y")


def plane_gathered(rows):
    if not square():
        return lax.all_gather(rows, PLANE, axis=0)
    pair = jnp.stack([rows, swapped(rows, "x")])
    return jnp.concatenate([pair, swapped(pair, "y")], axis=0)


def plane_summed(blocks):
    if not square():
        return wide(lax.psum_scatter(blocks, PLANE, scatter_dimension=0, tiled=False))
    pair = low(wide(blocks[:2]) + wide(swapped(blocks[2:], "y")))
    return wide(pair[0]) + wide(swapped(pair[1], "x"))


def plane_whole(own):
    own = jnp.where(lax.axis_index("c") == 0, own, own[:, ::-1])
    whole = lax.all_gather(own, PLANE, axis=1, tiled=False)
    ny, nx = lax.axis_size("y"), lax.axis_size("x")
    return whole.reshape(own.shape[:1] + (ny, nx) + own.shape[1:])


LITTLE = pl.CostEstimate(flops=1, bytes_accessed=1, transcendentals=0)
SPACE = pltpu.CompilerParams(vmem_limit_bytes=48 << 20)
VMEM = pl.BlockSpec(memory_space=pltpu.VMEM)
SMEM = pl.BlockSpec(memory_space=pltpu.SMEM)


def shape_of(dims, kind=jnp.bfloat16):
    return jax.ShapeDtypeStruct(tuple(dims), kind)


def run(kernel, shapes, here, *arrays):
    return pl.pallas_call(
        kernel,
        in_specs=[SMEM] + [VMEM] * len(arrays),
        out_specs=[VMEM] * len(shapes),
        out_shape=list(shapes),
        compiler_params=SPACE,
        cost_estimate=LITTLE,
    )(here, *arrays)


def run_grid(kernel, grid, specs, outs, here, *arrays):
    return pl.pallas_call(
        kernel,
        grid=(grid,),
        in_specs=[SMEM] + list(specs),
        out_specs=[spec for spec, shape in outs],
        out_shape=[shape for spec, shape in outs],
        compiler_params=SPACE,
        cost_estimate=LITTLE,
    )(here, *arrays)


def whole_block(array):
    dims = len(array.shape)
    return pl.BlockSpec(array.shape, lambda i: (0,) * dims)


def lead_block(shape):
    dims = len(shape)
    return pl.BlockSpec((1,) + tuple(shape[1:]), lambda i: (i,) + (0,) * (dims - 1))


def around(z, k, count):
    return lax.rem(z + (k + count), count)


def split_shares(here, pieces, gate_weight, up_weight, sizes, unit, lane, query_width, key_width):
    nz, ny, nx, nc = sizes
    rows = gate_weight.shape[0]
    half = query_width // 2
    hidden_width = lane * ny * nx
    inner_width = half + 2 * HD + 128
    count = len(pieces)

    def columns(piece, of):
        first, second = query_width + of * HD, query_width + key_width + of * HD
        return jnp.concatenate(
            [
                piece[:, of * half : (of + 1) * half],
                piece[:, first : first + HD],
                piece[:, second : second + HD],
                piece[:, query_width + 2 * key_width :],
            ],
            axis=1,
        )

    def kernel(here_ref, *refs):
        piece_refs, (gate_ref, up_ref) = refs[:count], refs[count : count + 2]
        mine_ref, share_ref, send_ref, send_share_ref = refs[count + 2 :]
        core = here_ref[3]
        for k, ref in enumerate(piece_refs):
            at = around(here_ref[0], -k, nz)
            piece = ref[...]
            zero, one = columns(piece, 0), columns(piece, 1)
            mine_ref[at] = jnp.where(core == 0, zero, one)
            send_ref[at] = jnp.where(core == 0, one, zero)
        share_ref[...] = jnp.zeros_like(share_ref)
        send_share_ref[...] = jnp.zeros_like(send_share_ref)
        for own in range(nc):

            @pl.when(core == own)
            def _():
                for m, ref in enumerate((gate_ref, up_ref)):
                    for d in range(nz * ny * nx * nc):
                        z, p, c = d // (ny * nx * nc), d // nc % (ny * nx), d % nc
                        out = share_ref if c == own else send_share_ref
                        out[z, m, :, lane * p : lane * p + unit] = ref[
                            :, unit * d : unit * d + unit
                        ]

    return run(
        kernel,
        (
            shape_of((nz, rows, inner_width)),
            shape_of((nz, 2, rows, hidden_width)),
            shape_of((nz, rows, inner_width)),
            shape_of((nz, 2, rows, hidden_width)),
        ),
        here,
        *pieces,
        gate_weight,
        up_weight,
    )


def share_blocks(here, mine, came):
    nz = mine.shape[0]

    def kernel(here_ref, mine_ref, came_ref, *outs):
        for k, out in enumerate(outs):
            at = around(here_ref[0], k, nz)
            out[0] = mine_ref[at]
            out[1] = came_ref[at]

    return run(kernel, [shape_of((2,) + mine.shape[1:])] * nz, here, mine, came)


def split_output(here, pieces):
    nz = len(pieces)
    rows, width = pieces[0].shape
    half = width // 2

    def kernel(here_ref, *refs):
        mine_ref, other_ref = refs[nz:]
        first = here_ref[3] == 0
        for k, ref in enumerate(refs[:nz]):
            at = around(here_ref[0], -k, nz)
            left, right = ref[:, :half], ref[:, half:]
            mine_ref[at] = jnp.where(first, left, right)
            other_ref[at] = jnp.where(first, right, left)

    return run(kernel, [shape_of((nz, rows, half))] * 2, here, *pieces)


def place_shares(here, pieces):
    nz = len(pieces)

    def kernel(here_ref, *refs):
        gate_ref, up_ref = refs[nz:]
        for k, ref in enumerate(refs[:nz]):
            at = around(here_ref[0], -k, nz)
            for i in range(2):
                gate_ref[at, i] = ref[i, 0]
                up_ref[at, i] = ref[i, 1]

    return run(kernel, [shape_of((nz, 2) + pieces[0].shape[2:])] * 2, here, *pieces)


def assemble(here_ref, refs, out):
    y, x, c = here_ref[1], here_ref[2], here_ref[3]
    own, from_x, from_y, *far = refs
    for ref, at_y, at_x in ((own, y, x), (from_x, y, 1 - x), (from_y, 1 - y, x)):
        for z in range(out.shape[0]):
            for i in range(2):
                out[z, at_y, at_x, c if i == 0 else 1 - c] = ref[z, i]
    for z in range(out.shape[0]):
        for i in range(2):
            block = [ref[z, i] for ref in far]
            block = block[0] if len(block) == 1 else jnp.concatenate(block, axis=1)
            out[z, 1 - y, 1 - x, c if i == 0 else 1 - c] = block


def six(own):
    return (own.shape[0], lax.axis_size("y"), lax.axis_size("x")) + own.shape[1:]


def turn(values, cosine, sine):
    return values * cosine + pltpu.roll(values, HD // 2, 1) * sine


def turn_back(values, cosine, sine):
    return values * cosine + pltpu.roll(values * sine, HD // 2, 1)


def key_places(core, width, owned, owned_key, shift):
    source = lax.broadcasted_iota(jnp.int32, (width, HD), 0)
    feature = lax.broadcasted_iota(jnp.int32, (width, HD), 1) + core * HD
    place = feature // owned_key * owned + feature % owned_key + shift
    return low(wide(source == place))


def inner_projections(here, own, other, weights, cosine, sine, owned, owned_key):
    local_rows, count, width = own.shape
    total = 2 * local_rows * count
    half = width // 2
    tables = len(weights)
    pieces = tables > 1
    dims = six(weights[0]) if pieces else weights[0].shape
    columns = dims[-1]

    def kernel(here_ref, own_ref, other_ref, cos_ref, sin_ref, *refs):
        weight_refs = refs[:tables]
        n_ref, q_ref, pair_ref, line_ref = refs[tables : tables + 4]
        if pieces:
            assemble(here_ref, weight_refs, refs[-1])
            weight = refs[-1][...].reshape(width, columns)
        else:
            weight = weight_refs[0][...]
        lines = wide(weight[:, columns - 128 :]).T
        core = here_ref[3]
        values = jnp.concatenate([own_ref[...], other_ref[...]], axis=0)
        values = wide(values.reshape(total, width))
        scale = lax.rsqrt(jnp.mean(values * values, axis=-1, keepdims=True) + epsilon)
        normed = low(values * scale * lines[1:2])
        n_ref[...] = normed
        line_ref[...] = lines[:8]
        small = low(lines[3:4])
        key_bias = nn(small, key_places(core, width, owned, owned_key, 0))
        value_bias = nn(small, key_places(core, width, owned, owned_key, owned_key))
        bias = jnp.where(core == 0, lines[0:1, :half], lines[0:1, half:])
        pre = nn(normed, weight[:, : half + 2 * HD])
        cosine, sine = cos_ref[...], sin_ref[...]
        for h in range(HPG):
            block = slice(h * HD, (h + 1) * HD)
            query = low(turn(pre[:, block] + bias[:, block], cosine, sine))
            query = query.reshape(2, local_rows, count, HD)
            for r in range(local_rows):
                q_ref[r, h] = query[:, r]
        key = low(turn(pre[:, half : half + HD] + key_bias, cosine, sine))
        value = low(pre[:, half + HD : half + 2 * HD] + value_bias)
        shape = (2, local_rows, count, HD)
        pair_ref[..., :HD] = key.reshape(shape)
        pair_ref[..., HD:] = value.reshape(shape)

    shapes = [
        shape_of((total, width)),
        shape_of((local_rows, HPG, 2, count, HD)),
        shape_of((2, local_rows, count, 2 * HD)),
        shape_of((8, width), jnp.float32),
    ]
    if pieces:
        shapes.append(shape_of(dims))
    out = run(kernel, shapes, here, own, other, cosine, sine, *weights)
    return out if pieces else list(out) + [weights[0]]


def row_scores(query, keys, allowed):
    return jnp.where(allowed, nt(query, keys) * (1.0 / math.sqrt(HD)), masked_value)


def row_specs(pairs, count):
    keys = pl.BlockSpec((pairs.shape[0], 2, 1, count, 2 * HD), lambda r: (0, 0, r, 0, 0))
    queries = pl.BlockSpec((1, HPG, 2, count, HD), lambda r: (r, 0, 0, 0, 0))
    flat = pl.BlockSpec((2, 1, count, HPG * HD), lambda r: (0, r, 0, 0))
    stats = pl.BlockSpec((1, HPG, 2 * count, HD), lambda r: (r, 0, 0, 0))
    allowed = pl.BlockSpec((1, 2 * count, pairs.shape[0] * 2 * count), lambda r: (r, 0, 0))
    return keys, queries, flat, stats, allowed


def attend(here, queries, pairs, allowed):
    local_rows, heads, cores, count, hd = queries.shape
    total = 2 * count
    keys, query_spec, flat, stats, allowed_spec = row_specs(pairs, count)

    def kernel(here_ref, q_ref, pair_ref, allowed_ref, out_ref, other_ref, stat_ref):
        pair = pair_ref[...].reshape(-1, 2 * HD)
        key, value = pair[:, :HD], pair[:, HD:]
        seen = allowed_ref[0] > 0
        for h in range(heads):
            scores = row_scores(q_ref[0, h].reshape(total, HD), key, seen)
            top = jnp.max(scores, axis=-1, keepdims=True)
            log_total = top + jnp.log(jnp.sum(jnp.exp(scores - top), axis=-1, keepdims=True))
            mixed = low(nn(low(jnp.exp(scores - log_total)), value)).reshape(2, count, HD)
            columns = slice(h * HD, (h + 1) * HD)
            for c in range(2):
                out_ref[c, 0, :, columns] = mixed[c]
                other_ref[1 - c, 0, :, columns] = mixed[c]
            stat_ref[0, h] = jnp.broadcast_to(log_total, (total, HD))

    flat_shape = shape_of((2, local_rows, count, heads * HD))
    stat_shape = shape_of((local_rows, heads, total, HD), jnp.float32)
    return run_grid(
        kernel,
        local_rows,
        [query_spec, keys, allowed_spec],
        [(flat, flat_shape), (flat, flat_shape), (stats, stat_shape)],
        here,
        queries,
        pairs,
        allowed,
    )


def attend_back(here, queries, pairs, allowed, stats, grads, came, cosine, sine):
    local_rows, heads, cores, count, hd = queries.shape
    total = 2 * count
    spots = pairs.shape[0]
    scaling = 1.0 / math.sqrt(HD)
    keys, query_spec, flat, stat_spec, allowed_spec = row_specs(pairs, count)
    table = pl.BlockSpec((2, 1, count, HD), lambda r: (0, r, 0, 0))
    half_keys = pl.BlockSpec((spots // 2, 2, 1, count, 2 * HD), lambda r: (0, 0, r, 0, 0))

    def kernel(here_ref, q_ref, pair_ref, allowed_ref, stat_ref, grad_ref, came_ref, cos_ref, sin_ref, out_ref, *parts):
        pair = pair_ref[...].reshape(-1, 2 * HD)
        key, value = pair[:, :HD], pair[:, HD:]
        seen = allowed_ref[0] > 0
        cosine, sine = (ref[...].reshape(total, HD) for ref in (cos_ref, sin_ref))
        key_part = jnp.zeros(key.shape, jnp.float32)
        value_part = jnp.zeros(key.shape, jnp.float32)
        for h in range(heads):
            columns = slice(h * HD, (h + 1) * HD)
            query = q_ref[0, h].reshape(total, HD)
            grad = low(grad_ref[:, 0, :, columns] + came_ref[:, 0, :, columns]).reshape(total, HD)
            probs = jnp.exp(row_scores(query, key, seen) - stat_ref[0, h][:, :1])
            back = nt(grad, value)
            delta = jnp.sum(probs * back, axis=-1, keepdims=True)
            score_grad = low(probs * (back - delta))
            key_part = key_part + tn(score_grad, query)
            value_part = value_part + tn(low(probs), grad)
            query_sum = nn(score_grad, key) * scaling
            turned = low(turn_back(query_sum, cosine, sine))
            out_ref[:, 0, :, columns] = turned.reshape(2, count, HD)
        shape = (2, spots // 2, 2, count, HD)
        key_part = low(key_part * scaling).reshape(shape)
        value_part = low(value_part).reshape(shape)
        for i, ref in enumerate(parts):
            ref[:, :, 0, :, :HD] = key_part[i]
            ref[:, :, 0, :, HD:] = value_part[i]

    part_shape = shape_of((spots // 2,) + pairs.shape[1:])
    return run_grid(
        kernel,
        local_rows,
        [query_spec, keys, allowed_spec, stat_spec, flat, flat, table, table],
        [
            (flat, shape_of((2, local_rows, count, heads * HD))),
            (half_keys, part_shape),
            (half_keys, part_shape),
        ],
        here,
        queries,
        pairs,
        allowed,
        stats,
        grads,
        came,
        cosine,
        sine,
    )


def output_projection(here, attended, came, weights):
    total, half = attended.shape
    width = 2 * half
    tables = len(weights)
    pieces = tables > 1
    dims = six(weights[0]) if pieces else weights[0].shape

    def kernel(here_ref, own_ref, came_ref, *refs):
        weight_refs = refs[:tables]
        part_ref, other_ref, all_ref = refs[tables : tables + 3]
        if pieces:
            assemble(here_ref, weight_refs, refs[-1])
            weight = refs[-1][...].reshape(width, half)
        else:
            weight = weight_refs[0][...]
        own, came = own_ref[...], came_ref[...]
        first = here_ref[3] == 0
        heads = jnp.concatenate([jnp.where(first, own, came), jnp.where(first, came, own)], axis=1)
        all_ref[...] = heads
        part = nn(heads, weight)
        part_ref[...] = part[: total // 2]
        other_ref[...] = part[total // 2 :]

    part_shape = shape_of((total // 2, half), jnp.float32)
    shapes = [part_shape, part_shape, shape_of((total, width))]
    if pieces:
        shapes.append(shape_of(dims))
    out = run(kernel, shapes, here, attended, came, *weights)
    return out if pieces else list(out) + [weights[0]]


def joined(first, own, came):
    return jnp.concatenate([jnp.where(first, own, came), jnp.where(first, came, own)], axis=1)


def second_norm(here, tokens, part, came, lines):
    count, width = tokens.shape

    def kernel(here_ref, tokens_ref, part_ref, came_ref, line_ref, hidden_ref, normed_ref):
        hidden = wide(tokens_ref[...]) + joined(here_ref[3] == 0, part_ref[...], came_ref[...])
        scale = lax.rsqrt(jnp.mean(hidden * hidden, axis=-1, keepdims=True) + epsilon)
        hidden_ref[...] = hidden
        normed_ref[...] = low(hidden * scale * line_ref[2:3])

    shapes = (shape_of((count, width), jnp.float32), shape_of((count, width)))
    return run(kernel, shapes, here, tokens, part, came, lines)


def halves_specs(width, tile, steps):
    first = pl.BlockSpec((tile, width), lambda i: (jnp.minimum(i, steps - 1), 0))
    second = pl.BlockSpec((tile, width), lambda i: (jnp.maximum(i - steps, 0), 0))
    return first, second


def feed_forward(here, normed, upstream, weights, weight_down):
    count, width = normed[0].shape
    hidden_width = weight_down.shape[0]
    tile = min(256, count)
    steps = count // tile
    tables = len(weights)
    pieces = tables > 2
    chunk = hidden_width // 3 if hidden_width % 384 == 0 else hidden_width
    spec_a, spec_b = halves_specs(width, tile, steps)

    def kernel(here_ref, na_ref, nb_ref, ua_ref, ub_ref, wd, *refs):
        weight_refs = refs[:tables]
        grad_a, grad_b, hidden_ref, gate_ref, up_ref = refs[tables : tables + 5]
        step = pl.program_id(0)
        if pieces:
            scratch = refs[-2:]

            @pl.when(step == 0)
            def _():
                assemble(here_ref, weight_refs[: tables // 2], scratch[0])
                assemble(here_ref, weight_refs[tables // 2 :], scratch[1])

            wg, wu = (ref[...].reshape(width, hidden_width) for ref in scratch)
        else:
            wg, wu = (ref[...] for ref in weight_refs)
        early = step < steps
        normed = jnp.where(early, na_ref[...], nb_ref[...])
        upstream = jnp.where(early, ua_ref[...], ub_ref[...])
        for k in range(0, hidden_width, chunk):
            columns = slice(k, k + chunk)
            gate = nn(normed, wg[:, columns])
            up = nn(normed, wu[:, columns])
            back = nt(upstream, wd[columns, :])
            sigmoid = jax.nn.sigmoid(gate)
            silu = gate * sigmoid
            hidden_ref[:, columns] = low(silu * up)
            gate_ref[:, columns] = low(back * up * sigmoid * (1.0 + gate * (1.0 - sigmoid)))
            up_ref[:, columns] = low(back * silu)
        grad = low(nt(gate_ref[...], wg) + nt(up_ref[...], wu))

        @pl.when(early)
        def _():
            grad_a[...] = grad

        @pl.when(jnp.logical_not(early))
        def _():
            grad_b[...] = grad

    rows = pl.BlockSpec((tile, hidden_width), lambda i: (i, 0))
    group = shape_of((count, width))
    wide_rows = shape_of((2 * count, hidden_width))
    scratch = [pltpu.VMEM(six(weights[0]), jnp.bfloat16)] * 2 if pieces else []
    return pl.pallas_call(
        kernel,
        grid=(2 * steps,),
        in_specs=[SMEM, spec_a, spec_b, spec_a, spec_b, whole_block(weight_down)]
        + [whole_block(w) for w in weights],
        out_specs=[spec_a, spec_b, rows, rows, rows],
        out_shape=[group, group, wide_rows, wide_rows, wide_rows],
        scratch_shapes=scratch,
        compiler_params=pltpu.CompilerParams(vmem_limit_bytes=56 << 20),
        cost_estimate=LITTLE,
    )(here, *normed, *upstream, weight_down, *weights)


def feed_forward_output(here, hidden, weight_down):
    count = hidden.shape[0] // 2
    width = weight_down.shape[1]
    tile = min(256, count)
    steps = count // tile
    specs = halves_specs(width, tile, steps)

    def kernel(here_ref, hidden_ref, weight_ref, out_a, out_b):
        part = low(nn(hidden_ref[...], weight_ref[...]))

        @pl.when(pl.program_id(0) < steps)
        def _():
            out_a[...] = part

        @pl.when(pl.program_id(0) >= steps)
        def _():
            out_b[...] = part

    rows = pl.BlockSpec((tile, hidden.shape[1]), lambda i: (i, 0))
    shape = shape_of((count, width))
    return run_grid(
        kernel,
        2 * steps,
        [rows, whole_block(weight_down)],
        [(spec, shape) for spec in specs],
        here,
        hidden,
        weight_down,
    )


def column_block(array, width):
    return pl.BlockSpec((array.shape[0], width), lambda i: (0, i))


def weight_grads(here, lefts, rights):
    counts = [v.shape[0] for v in lefts]
    rows = lefts[0].shape[1]
    tile = 384 if rows % 384 == 0 else 128
    number = len(lefts)

    def kernel(here_ref, *refs):
        turned = jnp.concatenate([ref[...] for ref in refs[:number]], axis=0).T
        for right, out in zip(refs[number : number + len(rights)], refs[number + len(rights) :]):
            out[...] = low(nn(turned, right[...]))

    return run_grid(
        kernel,
        rows // tile,
        [column_block(v, tile) for v in lefts] + [whole_block(v) for v in rights],
        [
            (pl.BlockSpec((tile, v.shape[1]), lambda i: (i, 0)), shape_of((rows, v.shape[1])))
            for v in rights
        ],
        here,
        *lefts,
        *rights,
    )


def split_by_plane(here_ref, first, second, refs, rows):
    y, x = here_ref[1], here_ref[2]
    first_send, first_keep, second_send, second_keep = refs
    first = first.reshape(2, 2, rows, first.shape[1])
    second = second.reshape(2, 2, rows, second.shape[1])
    first_send[0] = jnp.where(y == 0, first[1], first[0])
    first_keep[0] = jnp.where(y == 0, first[0], first[1])
    second_send[0] = jnp.where(x == 0, second[:, 1], second[:, 0])
    second_keep[0] = jnp.where(x == 0, second[:, 0], second[:, 1])


def plane_outs(nz, rows, first, second):
    shapes = [shape_of((nz, 2, rows, n)) for n in (first, first, second, second)]
    return [(lead_block(s.shape), s) for s in shapes]


def share_grads(here, lefts, first, second, nz, rows, vectors=None):
    width = lefts[0].shape[1]
    block = width // nz
    number = len(lefts)
    (first, first_from, first_to), (second, second_from, second_to) = first, second
    arrays = list(lefts) + [first, second] + ([] if vectors is None else [vectors])

    def kernel(here_ref, *refs):
        turned = jnp.concatenate([ref[...] for ref in refs[:number]], axis=0).T
        one = low(nn(turned, refs[number][:, first_from:first_to]))
        two = low(nn(turned, refs[number + 1][:, second_from:second_to]))
        if vectors is not None:
            filled = jnp.concatenate(
                [refs[number + 2][...], jnp.zeros((120, block), jnp.float32)], axis=0
            )
            two = jnp.concatenate([two, low(filled.T)], axis=1)
        split_by_plane(here_ref, one, two, refs[len(arrays) :], rows)

    extra = 0 if vectors is None else 128
    return run_grid(
        kernel,
        nz,
        [column_block(v, block) for v in lefts]
        + [whole_block(first), whole_block(second)]
        + ([] if vectors is None else [column_block(vectors, block)]),
        plane_outs(nz, rows, first_to - first_from, second_to - second_from + extra),
        here,
        *arrays,
    )


def plane_step(here, keeps, cames):
    nz = keeps[0].shape[0]

    def kernel(here_ref, first_ref, first_came, second_ref, second_came, *outs):
        y, x = here_ref[1], here_ref[2]
        first = low(wide(first_ref[0]) + wide(first_came[0]))
        second = low(wide(second_ref[0]) + wide(second_came[0]))
        for value, at, send, keep in ((first, x, *outs[:2]), (second, y, *outs[2:])):
            send[0] = jnp.where(at == 0, value[1], value[0])
            keep[0] = jnp.where(at == 0, value[0], value[1])

    shapes = []
    for v in keeps:
        shapes += [shape_of((nz,) + v.shape[2:])] * 2
    return run_grid(
        kernel,
        nz,
        [lead_block(v.shape) for v in (keeps[0], cames[0], keeps[1], cames[1])],
        [(lead_block(s.shape), s) for s in shapes],
        here,
        keeps[0],
        cames[0],
        keeps[1],
        cames[1],
    )


def share_sums(here, keeps, cames):
    nz, cores, rows, width = keeps[0].shape

    def kernel(here_ref, g_ref, g_came, u_ref, u_came, mine_ref, send_ref):
        core = here_ref[3]
        for m, (ref, came) in enumerate(((g_ref, g_came), (u_ref, u_came))):
            mine_ref[0, m] = low(wide(ref[0, core]) + wide(came[0, core]))
            send_ref[0, m] = low(wide(ref[0, 1 - core]) + wide(came[0, 1 - core]))

    shape = shape_of((nz, 2, rows, width))
    arrays = (keeps[0], cames[0], keeps[1], cames[1])
    return run_grid(
        kernel,
        nz,
        [lead_block(v.shape) for v in arrays],
        [(lead_block(shape.shape), shape)] * 2,
        here,
        *arrays,
    )


def collect_columns(here, pieces, sizes, unit, lane):
    nz, ny, nx, nc = sizes
    rows = pieces[0].shape[2]

    def kernel(here_ref, *refs):
        gate_ref, up_ref, placed = refs[nz:]
        core = here_ref[3]
        for k, ref in enumerate(refs[:nz]):
            at = around(here_ref[0], -k, nz)
            placed[at, core] = ref[0]
            placed[at, 1 - core] = ref[1]
        for m, ref in enumerate((gate_ref, up_ref)):
            for d in range(nz * ny * nx * nc):
                z, p, c = d // (ny * nx * nc), d // nc % (ny * nx), d % nc
                ref[:, unit * d : unit * d + unit] = wide(
                    placed[z, c, m, :, lane * p : lane * p + unit]
                )

    shape = shape_of((rows, unit * nz * ny * nx * nc), jnp.float32)
    return pl.pallas_call(
        kernel,
        in_specs=[SMEM] + [VMEM] * nz,
        out_specs=[VMEM] * 2,
        out_shape=[shape, shape],
        scratch_shapes=[pltpu.VMEM((nz,) + pieces[0].shape, jnp.bfloat16)],
        compiler_params=SPACE,
        cost_estimate=LITTLE,
    )(here, *pieces)


def down_grads(here, hidden, upstream, lane):
    hidden_width = hidden.shape[1]
    width = upstream[0].shape[1]
    count = upstream[0].shape[0]
    part = lane // 2

    def kernel(here_ref, hidden_ref, other_ref, own_ref, *outs):
        refs, turned_ref = outs[:4], outs[4]
        y, x = here_ref[1], here_ref[2]
        turned_ref[...] = hidden_ref[...].T
        for p in range(4):
            left = turned_ref[lane * p : lane * (p + 1), :]
            block = low(nn(left[:, :count], other_ref[...]) + nn(left[:, count:], own_ref[...]))
            for half, at, here_at, slot in ((0, p // 2, y, p % 2), (1, p % 2, x, p // 2)):
                value = block[half * part : (half + 1) * part]

                @pl.when(here_at == at)
                def _():
                    refs[2 * half + 1][slot] = value

                @pl.when(here_at != at)
                def _():
                    refs[2 * half][slot] = value

    shape = shape_of((2, part, width))
    return pl.pallas_call(
        kernel,
        in_specs=[SMEM] + [VMEM] * 3,
        out_specs=[VMEM] * 4,
        out_shape=[shape] * 4,
        scratch_shapes=[pltpu.VMEM((hidden_width, 2 * count), jnp.bfloat16)],
        compiler_params=SPACE,
        cost_estimate=LITTLE,
    )(here, hidden, *upstream)


def down_step(here, keeps, cames):
    def kernel(here_ref, first_ref, first_came, second_ref, second_came, *outs):
        for at, ref, came, send, keep in (
            (here_ref[2], first_ref, first_came, *outs[:2]),
            (here_ref[1], second_ref, second_came, *outs[2:]),
        ):
            send[...] = low(wide(ref[1 - at]) + wide(came[1 - at]))
            keep[...] = low(wide(ref[at]) + wide(came[at]))

    shape = shape_of(keeps[0].shape[1:])
    return run(kernel, [shape] * 4, here, keeps[0], cames[0], keeps[1], cames[1])


def depth_blocks(here, own, came):
    nz = lax.axis_size("z")
    shape = (own.shape[0] // nz, own.shape[1])
    own, came = (v.reshape((nz,) + shape) for v in (own, came))

    def kernel(here_ref, own_ref, came_ref, *outs):
        for k, out in enumerate(outs):
            at = (nz - k) % nz
            out[...] = (wide(own_ref[at]) + wide(came_ref[at])).astype(out.dtype)

    shapes = [shape_of(shape, jnp.float32)] + [shape_of(shape)] * (nz - 1)
    return run(kernel, shapes, here, own, came)


def first_backward(here, own, pieces, hidden, upstream, lines):
    count, width = hidden.shape
    half = width // 2
    number = len(pieces)

    def kernel(here_ref, own_ref, hidden_ref, up_ref, line_ref, *refs):
        out_ref, mine_ref, other_ref, term_ref = refs[number:]
        grad = own_ref[...]
        for ref in refs[:number]:
            grad = grad + wide(ref[...])
        hidden = hidden_ref[...]
        scale = lax.rsqrt(jnp.mean(hidden * hidden, axis=-1, keepdims=True) + epsilon)
        normalized = hidden * scale
        term_ref[...] = jnp.sum(grad * normalized, axis=0, keepdims=True)
        scaled = grad * line_ref[2:3]
        mean = jnp.mean(scaled * normalized, axis=-1, keepdims=True)
        result = wide(up_ref[...]) + scale * (scaled - normalized * mean)
        out_ref[...] = result
        proj = low(result)
        first = here_ref[3] == 0
        mine_ref[...] = jnp.where(first, proj[:, :half], proj[:, half:])
        other_ref[...] = jnp.where(first, proj[:, half:], proj[:, :half])

    shapes = (
        shape_of((count, width), jnp.float32),
        shape_of((count, half)),
        shape_of((count, half)),
        shape_of((1, width), jnp.float32),
    )
    return run(kernel, shapes, here, own, hidden, upstream, lines, *pieces)


def attended_backward(here, mine, came, weight):
    count, half = mine.shape

    def kernel(here_ref, mine_ref, came_ref, weight_ref, keep_ref, send_ref, proj_ref):
        proj = jnp.concatenate([mine_ref[...], came_ref[...]], axis=0)
        proj_ref[...] = proj
        part = nt(proj, weight_ref[...])
        first = here_ref[3] == 0
        keep_ref[...] = jnp.where(first, part[:, :half], part[:, half:])
        send = jnp.where(first, part[:, half:], part[:, :half])
        send_ref[:count] = send[count:]
        send_ref[count:] = send[:count]

    shape = shape_of((2 * count, half), jnp.float32)
    return run(kernel, (shape, shape, shape_of((2 * count, half))), here, mine, came, weight)


def inner_backward(here, query_grad, pair_sum, cosine, sine, weight, owned, owned_key):
    total, half = query_grad.shape
    width = 2 * half
    inner = half + 2 * HD

    def kernel(here_ref, q_ref, pair_ref, cos_ref, sin_ref, weight_ref, out_ref, own_ref, other_ref, line_ref):
        core = here_ref[3]
        pair = pair_ref[...]
        key = low(turn_back(pair[:, :HD], cos_ref[...], sin_ref[...]))
        value = low(pair[:, HD:])
        grad = jnp.concatenate([q_ref[...], key, value], axis=1)
        out_ref[...] = grad
        part = nt(grad, weight_ref[:, :inner])
        own_ref[...] = part[: total // 2]
        other_ref[...] = part[total // 2 :]
        terms = jnp.sum(wide(grad), axis=0, keepdims=True)
        query = terms[:, :half]
        nothing = jnp.zeros_like(query)
        first = core == 0
        line_ref[0:1] = jnp.concatenate(
            [jnp.where(first, query, nothing), jnp.where(first, nothing, query)], axis=1
        )
        line_ref[1:2] = nt(
            low(terms[:, half : half + HD]), key_places(core, width, owned, owned_key, 0)
        ) + nt(
            low(terms[:, half + HD :]), key_places(core, width, owned, owned_key, owned_key)
        )

    shapes = (
        shape_of((total, inner)),
        shape_of((total // 2, width), jnp.float32),
        shape_of((total // 2, width), jnp.float32),
        shape_of((2, width), jnp.float32),
    )
    return run(kernel, shapes, here, query_grad, pair_sum, cosine, sine, weight)


def input_backward(here, tokens, own, came, hidden_grad, lines, post_term, bias_terms):
    count, width = tokens.shape

    def kernel(here_ref, t_ref, own_ref, came_ref, h_ref, line_ref, post_ref, bias_ref, out_ref, term_ref):
        values = wide(t_ref[...])
        scale = lax.rsqrt(jnp.mean(values * values, axis=-1, keepdims=True) + epsilon)
        normalized = values * scale
        grad = own_ref[...] + came_ref[...]
        scaled = grad * line_ref[1:2]
        mean = jnp.mean(scaled * normalized, axis=-1, keepdims=True)
        out_ref[...] = low(h_ref[...] + scale * (scaled - normalized * mean))
        term_ref[...] = jnp.concatenate(
            [
                bias_ref[0:1],
                jnp.sum(grad * normalized, axis=0, keepdims=True),
                post_ref[...],
                bias_ref[1:2],
                jnp.zeros((4, width), jnp.float32),
            ],
            axis=0,
        )

    shapes = (shape_of((count, width)), shape_of((8, width), jnp.float32))
    return run(
        kernel, shapes, here, tokens, own, came, hidden_grad, lines, post_term, bias_terms
    )


def inner_blocks(here, keeps, cames):
    nz, cores, rows, columns = keeps[0].shape
    columns = sum(v.shape[3] for v in keeps)
    number = len(keeps)

    def kernel(here_ref, *refs):
        pairs = list(zip(refs[:number], refs[number : 2 * number]))
        for k, out in enumerate(refs[2 * number :]):
            at = around(here_ref[0], k, nz)
            for c in range(cores):
                sums = [wide(a[at, c]) + wide(b[at, c]) for a, b in pairs]
                out[c] = jnp.concatenate(sums, axis=1).astype(out.dtype)

    shape = (cores, rows, columns)
    shapes = [shape_of(shape, jnp.float32)] + [shape_of(shape)] * (nz - 1)
    return run(kernel, shapes, here, *keeps, *cames)


def inner_sums(here, own, pieces):
    cores, rows, columns = own.shape
    number = len(pieces)

    def kernel(here_ref, own_ref, *refs):
        mine_ref, send_ref = refs[number:]
        core = here_ref[3]
        for at, out in ((core, mine_ref), (1 - core, send_ref)):
            total = own_ref[at]
            for ref in refs[:number]:
                total = total + wide(ref[at])
            out[...] = total.astype(out.dtype)

    shapes = (shape_of((rows, columns), jnp.float32), shape_of((rows, columns)))
    return run(kernel, shapes, here, own, *pieces)


def inner_results(here, mine, came, width, key_width):
    rows = mine.shape[0]
    half = width // 2
    ends = (half, 2 * half, 2 * half + HD, 2 * half + 2 * HD)

    def kernel(here_ref, mine_ref, came_ref, output_ref, query_ref, key_ref, value_ref, line_ref):
        first = here_ref[3] == 0
        mine, came = mine_ref[...], wide(came_ref[...])
        line_ref[...] = mine[:, ends[-1] :] + came[:, ends[-1] :]
        output_ref[...] = joined(first, mine[:, :half], came[:, :half])
        for ref, a, b in zip((query_ref, key_ref, value_ref), ends, ends[1:]):
            ref[...] = joined(first, mine[:, a:b], came[:, a:b])

    shapes = [
        shape_of((rows, n), jnp.float32) for n in (width, width, key_width, key_width, 128)
    ]
    return run(kernel, shapes, here, mine, came)


def column_pack(columns, rows):
    padded = [jnp.pad(v, (0, rows - v.shape[0])) for v in columns]
    packed = jnp.stack(padded, axis=1)
    return jnp.pad(packed, ((0, 0), (0, 128 - len(columns))))


def shards(
    tokens,
    doc_lengths,
    query_weight,
    key_weight,
    value_weight,
    query_bias,
    key_bias,
    value_bias,
    output_weight,
    attention_norm_gain,
    feedforward_norm_gain,
    gate_weight,
    up_weight,
    down_weight,
    cotangent,
):
    local_rows, shard_tokens, width = tokens.shape
    sizes = nz, ny, nx, nc = tuple(lax.axis_size(a) for a in EVERY)
    here = jnp.stack([lax.axis_index(a) for a in EVERY]).astype(jnp.int32)
    devices = nz * ny * nx * nc
    flat_count = local_rows * shard_tokens
    chip_count = 2 * flat_count
    owned, query_width = query_weight.shape
    key_width = key_weight.shape[1]
    owned_key = key_bias.shape[0]
    half = query_width // 2
    unit = gate_weight.shape[1] // devices
    lane = -(-ny * nx * unit // 128) * 128 // (ny * nx)
    hidden_width = ny * nx * lane
    in_square = square()
    own_tokens = tokens.reshape(flat_count, width)
    upstream = cotangent.reshape(flat_count, width)
    chip_shape = (2, local_rows, shard_tokens)

    vectors = column_pack(
        (
            query_bias,
            attention_norm_gain,
            feedforward_norm_gain,
            jnp.concatenate([key_bias, value_bias]),
        ),
        owned,
    )
    packed = jnp.concatenate([query_weight, key_weight, value_weight, vectors], axis=1)
    pieces = depth_gathered(packed, every_shift()) | {0: packed}
    down_near = plane_near(down_weight) if in_square else ()
    cosine, sine, allowed = position_tables(doc_lengths, shard_tokens)
    pieces, down_near, cosine, sine, allowed = sync(pieces, down_near, cosine, sine, allowed)
    first_shift, *more_shifts = every_shift()

    mine, shares, send, send_shares = split_shares(
        here, in_order(pieces), gate_weight, up_weight, sizes, unit, lane, query_width, key_width
    )
    came, came_shares = swapped(send, "c"), swapped(send_shares, "c")
    late_output = after(output_weight, pieces)
    output_pieces = depth_gathered(late_output, [first_shift]) | {0: late_output}
    cut = down_weight.shape[0] // 32 * 16
    down_far = ()
    if in_square:
        down_far = swapped(down_near[0][:cut], "y"), swapped(down_near[1][cut:], "x")
    mine, came, shares, came_shares, output_pieces, down_far = sync(
        mine, came, shares, came_shares, output_pieces, down_far
    )

    inner_own = jnp.stack([mine, came], axis=1)
    share_parts = dict(enumerate(share_blocks(here, shares, came_shares)))
    if in_square:
        inner_near = plane_near(inner_own)
    else:
        inner_near = ()
    output_pieces |= depth_gathered(after(late_output, mine), more_shifts)
    share_pieces = depth_sent(share_parts, [first_shift]) | {0: share_parts[0]}
    inner_own, inner_near, output_pieces, share_parts, share_pieces = sync(
        inner_own, inner_near, output_pieces, share_parts, share_pieces
    )

    middle = 512
    if in_square:
        inner_far = (
            swapped(inner_near[0][..., :middle], "y"),
            swapped(inner_near[1][..., middle:], "x"),
        )
        inner_weights = (inner_own, *inner_near, *inner_far)
    else:
        inner_weights = (plane_whole(inner_own).reshape(width, -1),)
    output_mine, output_send = split_output(here, in_order(output_pieces))
    output_came = swapped(output_send, "c")
    other_tokens = swapped(after(own_tokens, inner_own), "c")
    share_pieces |= depth_sent(after(share_parts, inner_own), more_shifts[1:])
    inner_weights, output_mine, output_came, other_tokens, share_pieces = sync(
        inner_weights, output_mine, output_came, other_tokens, share_pieces
    )

    output_own = jnp.stack([output_mine, output_came], axis=1)
    share_pieces |= depth_sent(after(share_parts, output_mine), more_shifts[:1])
    output_near = plane_near(output_own) if in_square else ()
    first_normed, queries, own_pair, lines, weight_inner = inner_projections(
        here,
        own_tokens.reshape(chip_shape[1:] + (width,)),
        other_tokens.reshape(chip_shape[1:] + (width,)),
        inner_weights,
        cosine,
        sine,
        owned,
        owned_key,
    )
    weight_inner = weight_inner.reshape(width, -1)
    cosine_chip = cosine.reshape(chip_shape + (HD,))
    sine_chip = sine.reshape(chip_shape + (HD,))
    own_pair, output_own, output_near, share_pieces = sync(
        own_pair, output_own, output_near, share_pieces
    )

    middle = half // 2
    if in_square:
        pairs = jnp.stack([own_pair, swapped(own_pair, "x")])
        output_near = after(output_near, pairs)
        output_far = (
            swapped(output_near[0][..., :middle], "y"),
            swapped(output_near[1][..., middle:], "x"),
        )
        output_weights = (output_own, *output_near, *output_far)
        pairs = jnp.concatenate([pairs, swapped(pairs, "y")], axis=0)
    else:
        pairs = plane_gathered(own_pair)
        output_weights = (plane_whole(output_own).reshape(width, -1),)
    gate_own, up_own = place_shares(here, in_order(share_pieces))
    late_upstream = after(upstream, share_pieces)
    upstream_pieces = depth_gathered(late_upstream, near_shifts()) | {0: late_upstream}
    pairs, upstream_pieces, gate_own, up_own, output_weights = sync(
        pairs, upstream_pieces, gate_own, up_own, output_weights
    )

    gate_near = plane_near(gate_own) if in_square else ()
    upstream_pieces |= depth_gathered(after(late_upstream, pairs), far_shifts())
    attended, turned, log_sums = attend(here, queries, pairs, allowed)
    attended, turned, gate_near, upstream_pieces = sync(
        attended, turned, gate_near, upstream_pieces
    )

    up_near = plane_near(after(up_own, attended)) if in_square else ()
    upstream_mine = jnp.concatenate(in_order(upstream_pieces), axis=0)
    upstream_other = swapped(upstream_mine, "c")
    came = swapped(turned.reshape(chip_count, half), "c")
    part, send, attended_all, weight_output = output_projection(
        here, attended.reshape(chip_count, half), came, output_weights
    )
    weight_output = weight_output.reshape(width, half)
    first_hidden, second_normed = second_norm(here, own_tokens, part, swapped(send, "c"), lines)
    second_normed, up_near, upstream_other = sync(second_normed, up_near, upstream_other)

    second_pieces = depth_gathered(second_normed, every_shift()) | {0: second_normed}
    if in_square:
        gate_far, up_far = swapped(gate_near[0], "y"), swapped(up_near[1], "x")
        weights = (gate_own, *gate_near, gate_far, up_own, *up_near, up_far)
        second_pieces, weights = sync(second_pieces, weights)
        y, x = lax.axis_index("y"), lax.axis_index("x")
        weight_down = jnp.zeros((2, 2, lane, width), jnp.bfloat16)
        for block, index in (
            (down_weight, (y, x, 0, 0)),
            (down_near[0], (y, 1 - x, 0, 0)),
            (down_near[1], (1 - y, x, 0, 0)),
            (down_far[0], (1 - y, 1 - x, 0, 0)),
            (down_far[1], (1 - y, 1 - x, cut, 0)),
        ):
            weight_down = lax.dynamic_update_slice(weight_down, block[None, None], index)
    else:
        weights = tuple(plane_whole(v).reshape(width, -1) for v in (gate_own, up_own))
        weight_down = lax.all_gather(down_weight, PLANE, axis=0)
        weight_down = jnp.pad(weight_down, ((0, 0), (0, lane - unit), (0, 0)))
        second_pieces, weights, weight_down = sync(second_pieces, weights, weight_down)
    weight_down = weight_down.reshape(hidden_width, width)

    second_mine = jnp.concatenate(in_order(second_pieces), axis=0)
    second_group = (swapped(second_mine, "c"), second_mine)
    upstream_group = (upstream_other, upstream_mine)
    normed_send, normed_own, hidden, gate_grad, up_grad = feed_forward(
        here, second_group, upstream_group, weights, weight_down
    )
    normed_came = swapped(normed_send, "c")
    rows = nc * owned
    if in_square:
        send_gate, gate_sum, send_up, up_sum = share_grads(
            here,
            second_group,
            (gate_grad, 0, hidden_width),
            (up_grad, 0, hidden_width),
            nz,
            rows,
        )
    else:
        send_gate, send_up = weight_grads(here, second_group, (gate_grad, up_grad))
        gate_sum = up_sum = ()
    normed_own, *normed_parts = depth_blocks(here, normed_own, normed_came)
    normed_parts = dict(enumerate(normed_parts, 1))
    normed_own, normed_parts, send_gate, gate_sum, send_up, up_sum = sync(
        normed_own, normed_parts, send_gate, gate_sum, send_up, up_sum
    )

    normed_pieces = depth_sent(normed_parts, every_shift())
    if in_square:
        came_gate, came_up = swapped(send_gate, "y"), swapped(send_up, "x")
        down_parts = down_grads(here, after(hidden, normed_own), upstream_group, lane)
    else:
        blocks = (nz, ny * nx, nc, owned, hidden_width)
        gate_sum, up_sum = (
            lax.psum_scatter(v.reshape(blocks), PLANE, scatter_dimension=1, tiled=False)
            for v in (send_gate, send_up)
        )
        (down_parts,) = weight_grads(
            here, (hidden,), (jnp.concatenate(upstream_group, axis=0),)
        )
    output_send, output_own = feed_forward_output(here, after(hidden, normed_own), weight_down)
    normed_pieces, down_parts, output_send, output_own = sync(
        normed_pieces, down_parts, output_send, output_own
    )

    hidden_one_grad, proj_mine, proj_send, post_term = first_backward(
        here, normed_own, in_order(normed_pieces), first_hidden, upstream, lines
    )
    keep, send, proj_grad = attended_backward(
        here, proj_mine, swapped(proj_send, "c"), weight_output
    )
    attended_came = swapped(send, "c")
    output_came = swapped(after(output_send, proj_mine), "c")
    if in_square:
        keep, attended_came, output_own, output_came, came_gate, came_up = sync(
            keep, attended_came, output_own, output_came, came_gate, came_up
        )
        send_gate, gate_sum, send_up, up_sum = plane_step(
            here, (gate_sum, up_sum), (came_gate, came_up)
        )
    else:
        keep, attended_came = sync(keep, attended_came)
    output_own, *output_parts = depth_blocks(here, output_own, output_came)
    output_parts = dict(enumerate(output_parts, 1))

    four = (nz, nc, owned, hidden_width)
    if in_square:
        came_gate, came_up = swapped(send_gate, "x"), swapped(send_up, "y")
    output_pieces = depth_sent(output_parts, near_shifts())
    if in_square:
        send_a, keep_a, send_b, keep_b = share_grads(
            here,
            (attended_all,),
            (proj_grad, 0, half // 2),
            (proj_grad, half // 2, half),
            nz,
            rows,
        )
    query_grad, part_near, part_far = attend_back(
        here,
        queries,
        pairs,
        allowed,
        log_sums,
        keep.reshape(chip_shape + (half,)),
        attended_came.reshape(chip_shape + (half,)),
        cosine_chip,
        sine_chip,
    )
    if in_square:
        part_near, part_far, came_gate, came_up, output_pieces, send_a, send_b = sync(
            part_near, part_far, came_gate, came_up, output_pieces, send_a, send_b
        )
    else:
        came_gate = came_up = jnp.zeros(four, jnp.bfloat16)

    shares, send_shares = share_sums(
        here,
        (gate_sum.reshape(four), up_sum.reshape(four)),
        (came_gate.reshape(four), came_up.reshape(four)),
    )
    came_shares = swapped(send_shares, "c")
    output_pieces |= depth_sent(after(output_parts, part_near), far_shifts())
    if in_square:
        step = low(wide(part_near) + wide(swapped(part_far, "y")))
        send_a, send_b = after((send_a, send_b), step)
        pair_sum = wide(step[0]) + wide(swapped(step[1], "x"))
        came_a, came_b = swapped(send_a, "y"), swapped(send_b, "x")
    else:
        pair_sum = plane_summed(jnp.concatenate([part_near, part_far], axis=0))
    else_came = (came_a, came_b) if in_square else ()
    pair_sum, shares, came_shares, output_pieces, else_came = sync(
        pair_sum, shares, came_shares, output_pieces, else_came
    )
    layer_output = first_hidden + output_own + sum(wide(v) for v in in_order(output_pieces))

    share_parts = dict(enumerate(share_blocks(here, shares, came_shares)))
    share_pieces = depth_sent(share_parts, near_shifts()) | {0: share_parts[0]}
    if in_square:
        came_a, came_b = else_came
        first_send, first_keep, second_send, second_keep = after(down_parts, pair_sum)
        came_first, came_second = swapped(first_send, "y"), swapped(second_send, "x")
    else:
        down_sum = lax.psum_scatter(
            down_parts.reshape(ny * nx, lane, width), PLANE, scatter_dimension=0, tiled=False
        )
    inner_grad, own_part, send, bias_terms = inner_backward(
        here,
        query_grad.reshape(chip_count, half),
        pair_sum.reshape(chip_count, 2 * HD),
        cosine,
        sine,
        weight_inner,
        owned,
        owned_key,
    )
    input_grad, vector_terms = input_backward(
        here, own_tokens, own_part, swapped(send, "c"), hidden_one_grad, lines, post_term, bias_terms
    )
    share_parts = after(share_parts, inner_grad)
    if in_square:
        send_c, keep_c, send_d, keep_d = share_grads(
            here,
            (first_normed,),
            (inner_grad, 0, 512),
            (inner_grad, 512, half + 2 * HD),
            nz,
            rows,
            vector_terms,
        )
        send_c, keep_c, send_d, keep_d, came_first, came_second, share_parts, share_pieces = sync(
            send_c, keep_c, send_d, keep_d, came_first, came_second, share_parts, share_pieces
        )
        share_pieces |= depth_sent(share_parts, far_shifts())
        send_a, keep_a, send_b, keep_b = plane_step(here, (keep_a, keep_b), (came_a, came_b))
        came_a, came_b = swapped(send_a, "x"), swapped(send_b, "y")
        came_c, came_d = swapped(send_c, "y"), swapped(send_d, "x")
        came_a, came_b, came_c, came_d, share_pieces = sync(
            came_a, came_b, came_c, came_d, share_pieces
        )
        send_c, keep_c, send_d, keep_d = plane_step(here, (keep_c, keep_d), (came_c, came_d))
        came_c, came_d = swapped(send_c, "x"), swapped(send_d, "y")
        first_send, first_keep, second_send, second_keep = down_step(
            here, (first_keep, second_keep), (came_first, came_second)
        )
        came_c, came_d, first_send, second_send = sync(came_c, came_d, first_send, second_send)
        keeps, cames = (
            [v.reshape(nz, nc, owned, -1) for v in group]
            for group in ((keep_a, keep_b, keep_c, keep_d), (came_a, came_b, came_c, came_d))
        )
    else:
        share_pieces |= depth_sent(share_parts, far_shifts())
        (output_term,) = weight_grads(here, (attended_all,), (proj_grad,))
        (inner_term,) = weight_grads(here, (first_normed,), (inner_grad,))
        inner_term = jnp.concatenate(
            [inner_term, jnp.pad(low(vector_terms.T), ((0, 0), (0, 120)))], axis=1
        )
        blocks = (nz, ny * nx, nc, owned, -1)
        keeps = [
            lax.psum_scatter(v.reshape(blocks), PLANE, scatter_dimension=1, tiled=False)
            for v in (output_term, inner_term)
        ]
        cames = [jnp.zeros_like(v) for v in keeps]
    gate_sum, up_sum = collect_columns(here, in_order(share_pieces), sizes, unit, lane)

    own, *parts = inner_blocks(here, keeps, cames)
    parts = dict(enumerate(parts, 1))
    pieces = depth_sent(parts, every_shift())
    if in_square:
        came_first, came_second = swapped(first_send, "x"), swapped(second_send, "y")
        down_sum = jnp.concatenate(
            [
                wide(first_keep) + wide(came_first),
                wide(second_keep) + wide(came_second),
            ],
            axis=0,
        )
    pieces, down_sum = sync(pieces, down_sum)
    mine, send = inner_sums(here, own, in_order(pieces))
    output_sum, query_sum, key_sum, value_sum, vector_sums = inner_results(
        here, mine, swapped(send, "c"), width, key_width
    )
    return (
        low(layer_output).reshape(local_rows, shard_tokens, width),
        input_grad.reshape(local_rows, shard_tokens, width),
        query_sum,
        key_sum,
        value_sum,
        vector_sums[:, 0],
        vector_sums[:owned_key, 3],
        vector_sums[owned_key : 2 * owned_key, 3],
        output_sum,
        vector_sums[:, 1],
        vector_sums[:, 2],
        gate_sum,
        up_sum,
        wide(down_sum)[:unit],
    )


def solution(mesh):
    depth, across = mesh.devices.shape
    plane = across // 2
    side = math.isqrt(plane)
    inner = Mesh(mesh.devices.reshape(depth, plane // side, side, 2), EVERY)
    over_rows = P("z", ROW, None)
    whole, flat = P(EVERY, None), P(EVERY)
    in_specs = (
        (over_rows, P("z", None))
        + (whole,) * 3
        + (flat,) * 3
        + (whole, flat, flat)
        + (whole,) * 3
        + (over_rows,)
    )
    out_specs = (
        (over_rows,) * 2 + (whole,) * 3 + (flat,) * 3 + (whole, flat, flat) + (whole,) * 3
    )
    return jax.shard_map(
        shards, mesh=inner, in_specs=in_specs, out_specs=out_specs, check_vma=False
    )
```

```python
import math

import jax
import jax.numpy as jnp
from jax import lax
from jax.experimental import pallas as pl
from jax.experimental.pallas import tpu as pltpu
from jax.sharding import Mesh
from jax.sharding import PartitionSpec as P

H = 12
KV = 2
HD = 128
HPG = 6

epsilon = 1e-06
rope_base = 10000.0
masked_value = -1e30

EVERY = ("z", "y", "x", "c")
ROW = ("y", "x", "c")
PLANE = ("y", "x")


def low(values):
    return values.astype(jnp.bfloat16)


def wide(values):
    return values.astype(jnp.float32)


def nn(left, right):
    return jnp.dot(left, right, preferred_element_type=jnp.float32)


def nt(left, right):
    return lax.dot_general(
        left, right, (((1,), (1,)), ((), ())), preferred_element_type=jnp.float32
    )


def tn(left, right):
    return lax.dot_general(
        left, right, (((0,), (0,)), ((), ())), preferred_element_type=jnp.float32
    )


def doc_tables(doc_ends, doc_lengths, positions):
    passed = doc_ends[:, None, :] <= positions[None, :, None]
    doc_index = jnp.sum(passed.astype(jnp.int32), axis=-1)
    starts = jnp.sum(jnp.where(passed, doc_lengths[:, None, :], 0), axis=-1)
    return (doc_index, positions[None, :] - starts)


def rope_tables(within):
    steps_even = jnp.arange(0, HD, 2).astype(jnp.float32)
    inverse = rope_base ** (-steps_even / HD)
    phase = within.astype(jnp.float32)[:, None] * inverse[None, :]
    phase = jnp.concatenate([phase, phase], axis=-1)
    return jnp.cos(phase), jnp.sin(phase)


def square():
    return lax.axis_size("y") == 2 and lax.axis_size("x") == 2


def places():
    y, x = lax.axis_index("y"), lax.axis_index("x")
    if square():
        return [(y, x), (y, 1 - x), (1 - y, x), (1 - y, 1 - x)]
    return [(i, j) for i in range(lax.axis_size("y")) for j in range(lax.axis_size("x"))]


def chip_positions(y, x, shard_tokens):
    core = lax.axis_index("c")
    place = (y * lax.axis_size("x") + x) * 2
    lanes = jnp.arange(shard_tokens, dtype=jnp.int32)
    return [(place + k) * shard_tokens + lanes for k in (core, 1 - core)]


def position_tables(doc_lengths, shard_tokens):
    local_rows = doc_lengths.shape[0]
    query_pos = jnp.concatenate(
        chip_positions(lax.axis_index("y"), lax.axis_index("x"), shard_tokens)
    )
    key_pos = jnp.concatenate(
        [p for place in places() for p in chip_positions(*place, shard_tokens)]
    )
    doc_ends = jnp.cumsum(doc_lengths, axis=1)
    query_doc, query_within = doc_tables(doc_ends, doc_lengths, query_pos)
    key_doc, unused_within = doc_tables(doc_ends, doc_lengths, key_pos)
    allowed = (query_doc[:, :, None] == key_doc[:, None, :]) & (
        key_pos[None, None, :] <= query_pos[None, :, None]
    )
    query_within = query_within.reshape(local_rows, 2, shard_tokens).transpose(1, 0, 2)
    cosine, sine = rope_tables(query_within.reshape(-1))
    sign = jnp.where(jnp.arange(HD) < HD // 2, -1.0, 1.0)
    return cosine, sine * sign, wide(allowed)


def sync(*values):
    return lax.optimization_barrier(values)


def after(values, *others):
    return lax.optimization_barrier((values, others))[0]


def swapped(values, axis):
    return lax.ppermute(values, axis, [(0, 1), (1, 0)])


def shifted(values, amount):
    count = lax.axis_size("z")
    return lax.ppermute(values, "z", [(i, (i + amount) % count) for i in range(count)])


def every_shift():
    return range(1, lax.axis_size("z"))


def near_shifts():
    return sorted({1, lax.axis_size("z") - 1})


def far_shifts():
    return range(2, lax.axis_size("z") - 1)


def depth_gathered(rows, shifts):
    return {k: shifted(rows, k) for k in shifts}


def depth_sent(blocks, shifts):
    return {k: jax.tree.map(lambda v: shifted(v, k), blocks[k]) for k in shifts}


def in_order(pieces):
    return [pieces[k] for k in sorted(pieces)]


def plane_near(values):
    return swapped(values, "x"), swapped(values, "y")


def plane_gathered(rows):
    if not square():
        return lax.all_gather(rows, PLANE, axis=0)
    pair = jnp.stack([rows, swapped(rows, "x")])
    return jnp.concatenate([pair, swapped(pair, "y")], axis=0)


def plane_summed(blocks):
    if not square():
        return wide(lax.psum_scatter(blocks, PLANE, scatter_dimension=0, tiled=False))
    pair = low(wide(blocks[:2]) + wide(swapped(blocks[2:], "y")))
    return wide(pair[0]) + wide(swapped(pair[1], "x"))


def plane_whole(own):
    own = jnp.where(lax.axis_index("c") == 0, own, own[:, ::-1])
    whole = lax.all_gather(own, PLANE, axis=1, tiled=False)
    ny, nx = lax.axis_size("y"), lax.axis_size("x")
    return whole.reshape(own.shape[:1] + (ny, nx) + own.shape[1:])


LITTLE = pl.CostEstimate(flops=1, bytes_accessed=1, transcendentals=0)
SPACE = pltpu.CompilerParams(vmem_limit_bytes=20 << 20)
ROOM = pltpu.CompilerParams(vmem_limit_bytes=14 << 20)
VMEM = pl.BlockSpec(memory_space=pltpu.VMEM)
SMEM = pl.BlockSpec(memory_space=pltpu.SMEM)


def shape_of(dims, kind=jnp.bfloat16):
    return jax.ShapeDtypeStruct(tuple(dims), kind)


def run(kernel, shapes, here, *arrays):
    return pl.pallas_call(
        kernel,
        in_specs=[SMEM] + [VMEM] * len(arrays),
        out_specs=[VMEM] * len(shapes),
        out_shape=list(shapes),
        compiler_params=ROOM,
        cost_estimate=LITTLE,
    )(here, *arrays)


def run_grid(kernel, grid, specs, outs, here, *arrays):
    return pl.pallas_call(
        kernel,
        grid=(grid,),
        in_specs=[SMEM] + list(specs),
        out_specs=[spec for spec, shape in outs],
        out_shape=[shape for spec, shape in outs],
        compiler_params=SPACE,
        cost_estimate=LITTLE,
    )(here, *arrays)


def whole_block(array):
    dims = len(array.shape)
    return pl.BlockSpec(array.shape, lambda i: (0,) * dims)


def lead_block(shape):
    dims = len(shape)
    return pl.BlockSpec((1,) + tuple(shape[1:]), lambda i: (i,) + (0,) * (dims - 1))


def around(z, k, count):
    return lax.rem(z + (k + count), count)


def split_shares(here, pieces, gate_weight, up_weight, sizes, unit, lane, query_width, key_width):
    nz, ny, nx, nc = sizes
    rows = gate_weight.shape[0]
    half = query_width // 2
    hidden_width = lane * ny * nx
    inner_width = half + 2 * HD + 128
    count = len(pieces)

    def columns(piece, of):
        first, second = query_width + of * HD, query_width + key_width + of * HD
        return jnp.concatenate(
            [
                piece[:, of * half : (of + 1) * half],
                piece[:, first : first + HD],
                piece[:, second : second + HD],
                piece[:, query_width + 2 * key_width :],
            ],
            axis=1,
        )

    def kernel(here_ref, *refs):
        piece_refs, (gate_ref, up_ref) = refs[:count], refs[count : count + 2]
        mine_ref, share_ref, send_ref = refs[count + 2 :]
        core = here_ref[3]
        for k, ref in enumerate(piece_refs):
            at = around(here_ref[0], -k, nz)
            piece = ref[...]
            zero, one = columns(piece, 0), columns(piece, 1)
            mine_ref[at] = jnp.where(core == 0, zero, one)
            send_ref[at, 0, :, :inner_width] = jnp.where(core == 0, one, zero)
        share_ref[...] = jnp.zeros_like(share_ref)
        send_ref[:, 1:] = jnp.zeros_like(send_ref[:, 1:])
        for own in range(nc):

            @pl.when(core == own)
            def _():
                for m, ref in enumerate((gate_ref, up_ref)):
                    for d in range(nz * ny * nx * nc):
                        z, p, c = d // (ny * nx * nc), d // nc % (ny * nx), d % nc
                        columns = slice(lane * p, lane * p + unit)
                        value = ref[:, unit * d : unit * d + unit]
                        if c == own:
                            share_ref[z, m, :, columns] = value
                        else:
                            send_ref[z, 1 + m, :, columns] = value

    return run(
        kernel,
        (
            shape_of((nz, rows, inner_width)),
            shape_of((nz, 2, rows, hidden_width)),
            shape_of((nz, 3, rows, max(inner_width, hidden_width))),
        ),
        here,
        *pieces,
        gate_weight,
        up_weight,
    )


def share_blocks(here, mine, came, skip=0):
    nz, matrices = mine.shape[:2]
    width = mine.shape[3]
    block = (2,) + mine.shape[1:]
    single = (2,) + mine.shape[2:]

    def kernel(here_ref, mine_ref, came_ref, *outs):
        outs = list(outs)
        for k in range(nz):
            at = around(here_ref[0], k, nz)
            if nz == 4 and k == 2:
                for m in range(matrices):
                    out = outs.pop(0)
                    out[0] = mine_ref[at, m]
                    out[1] = came_ref[at, skip + m, :, :width]
            else:
                out = outs.pop(0)
                out[0] = mine_ref[at]
                out[1] = came_ref[at, skip:, :, :width]

    shapes = []
    for k in range(nz):
        shapes += [shape_of(single)] * matrices if nz == 4 and k == 2 else [shape_of(block)]
    out = list(run(kernel, shapes, here, mine, came))
    return [out[0], out[1], (out[2], out[3]), out[4]] if nz == 4 else out


def split_output(here, pieces):
    nz = len(pieces)
    rows, width = pieces[0].shape
    half = width // 2

    def kernel(here_ref, *refs):
        mine_ref, other_ref = refs[nz:]
        first = here_ref[3] == 0
        for k, ref in enumerate(refs[:nz]):
            at = around(here_ref[0], -k, nz)
            left, right = ref[:, :half], ref[:, half:]
            mine_ref[at] = jnp.where(first, left, right)
            other_ref[at] = jnp.where(first, right, left)

    return run(kernel, [shape_of((nz, rows, half))] * 2, here, *pieces)


def place_shares(here, pieces, last, split):
    nz = len(pieces) + (1 if last else 0)
    shifts = [0, 1, *range(2 + (1 if last else 0), nz)]
    pieces, number = list(pieces), len(pieces)
    cores, matrices, rows, width = pieces[0].shape

    def kernel(here_ref, *refs):
        first_ref, second_ref = refs[number + len(last) :]
        for k, ref in zip(shifts, refs[:number]):
            at = around(here_ref[0], -k, nz)
            for i in range(cores):
                for m in range(matrices):
                    first_ref[m, at, i] = ref[i, m, :, :split]
                    second_ref[m, at, i] = ref[i, m, :, split:]
        for m, ref in enumerate(refs[number : number + len(last)]):
            at = around(here_ref[0], -2, nz)
            for i in range(cores):
                first_ref[m, at, i] = ref[i, :, :split]
                second_ref[m, at, i] = ref[i, :, split:]

    return run(
        kernel,
        [shape_of((matrices, nz, cores, rows, n)) for n in (split, width - split)],
        here,
        *pieces,
        *last,
    )


def assemble(here_ref, refs, out, view=lambda ref: ref, at=0):
    y, x, c = here_ref[1], here_ref[2], here_ref[3]
    own, from_x, from_y, *far = refs
    columns = slice(at, at + own.shape[-1])
    for ref, at_y, at_x in ((own, y, x), (from_x, y, 1 - x), (from_y, 1 - y, x)):
        for z in range(out.shape[0]):
            for i in range(2):
                out[z, at_y, at_x, c if i == 0 else 1 - c, :, columns] = view(ref)[z, i]
    for z in range(out.shape[0]):
        for i in range(2):
            block = [ref[z, i] for ref in far]
            block = block[0] if len(block) == 1 else jnp.concatenate(block, axis=1)
            out[z, 1 - y, 1 - x, c if i == 0 else 1 - c, :, columns] = block


def six(own):
    return (own.shape[0], lax.axis_size("y"), lax.axis_size("x")) + own.shape[1:]


def turn(values, cosine, sine):
    return values * cosine + pltpu.roll(values, HD // 2, 1) * sine


def turn_back(values, cosine, sine):
    return values * cosine + pltpu.roll(values * sine, HD // 2, 1)


def key_places(core, width, owned, owned_key, shift):
    source = lax.broadcasted_iota(jnp.int32, (width, HD), 0)
    feature = lax.broadcasted_iota(jnp.int32, (width, HD), 1) + core * HD
    place = feature // owned_key * owned + feature % owned_key + shift
    return low(wide(source == place))


def inner_projections(here, own, other, weights, cosine, sine, owned, owned_key):
    local_rows, count, width = own.shape
    total = 2 * local_rows * count
    half = width // 2
    tables = len(weights)
    pieces = tables > 1
    dims = six(weights[0]) if pieces else weights[0].shape
    columns = dims[-1]

    def kernel(here_ref, own_ref, other_ref, cos_ref, sin_ref, *refs):
        weight_refs = refs[:tables]
        n_ref, q_ref, pair_ref, line_ref = refs[tables : tables + 4]
        if pieces:
            assemble(here_ref, weight_refs, refs[-1])
            weight = refs[-1][...].reshape(width, columns)
        else:
            weight = weight_refs[0][...]
        lines = wide(weight[:, columns - 128 :]).T
        core = here_ref[3]
        values = jnp.concatenate([own_ref[...], other_ref[...]], axis=0)
        values = wide(values.reshape(total, width))
        scale = lax.rsqrt(jnp.mean(values * values, axis=-1, keepdims=True) + epsilon)
        normed = low(values * scale * lines[1:2])
        n_ref[...] = normed
        line_ref[...] = lines[:8]
        small = low(lines[3:4])
        key_bias = nn(small, key_places(core, width, owned, owned_key, 0))
        value_bias = nn(small, key_places(core, width, owned, owned_key, owned_key))
        bias = jnp.where(core == 0, lines[0:1, :half], lines[0:1, half:])
        pre = nn(normed, weight[:, : half + 2 * HD])
        cosine, sine = cos_ref[...], sin_ref[...]
        for h in range(HPG):
            block = slice(h * HD, (h + 1) * HD)
            query = low(turn(pre[:, block] + bias[:, block], cosine, sine))
            query = query.reshape(2, local_rows, count, HD)
            for r in range(local_rows):
                q_ref[r, h] = query[:, r]
        key = low(turn(pre[:, half : half + HD] + key_bias, cosine, sine))
        value = low(pre[:, half + HD : half + 2 * HD] + value_bias)
        shape = (2, local_rows, count, HD)
        pair_ref[..., :HD] = key.reshape(shape)
        pair_ref[..., HD:] = value.reshape(shape)

    shapes = [
        shape_of((total, width)),
        shape_of((local_rows, HPG, 2, count, HD)),
        shape_of((2, local_rows, count, 2 * HD)),
        shape_of((8, width), jnp.float32),
    ]
    if pieces:
        shapes.append(shape_of(dims))
    out = run(kernel, shapes, here, own, other, cosine, sine, *weights)
    return out if pieces else list(out) + [weights[0]]


def row_scores(query, keys, allowed):
    return jnp.where(allowed, nt(query, keys) * (1.0 / math.sqrt(HD)), masked_value)


def row_specs(pairs, count):
    keys = pl.BlockSpec((pairs.shape[0], 2, 1, count, 2 * HD), lambda r: (0, 0, r, 0, 0))
    queries = pl.BlockSpec((1, HPG, 2, count, HD), lambda r: (r, 0, 0, 0, 0))
    flat = pl.BlockSpec((2, 1, count, HPG * HD), lambda r: (0, r, 0, 0))
    stats = pl.BlockSpec((1, HPG, 2 * count, HD), lambda r: (r, 0, 0, 0))
    allowed = pl.BlockSpec((1, 2 * count, pairs.shape[0] * 2 * count), lambda r: (r, 0, 0))
    return keys, queries, flat, stats, allowed


def attend(here, queries, pairs, allowed):
    local_rows, heads, cores, count, hd = queries.shape
    total = 2 * count
    keys, query_spec, flat, stats, allowed_spec = row_specs(pairs, count)

    def kernel(here_ref, q_ref, pair_ref, allowed_ref, out_ref, other_ref, stat_ref):
        pair = pair_ref[...].reshape(-1, 2 * HD)
        key, value = pair[:, :HD], pair[:, HD:]
        seen = allowed_ref[0] > 0
        for h in range(heads):
            scores = row_scores(q_ref[0, h].reshape(total, HD), key, seen)
            top = jnp.max(scores, axis=-1, keepdims=True)
            log_total = top + jnp.log(jnp.sum(jnp.exp(scores - top), axis=-1, keepdims=True))
            mixed = low(nn(low(jnp.exp(scores - log_total)), value)).reshape(2, count, HD)
            columns = slice(h * HD, (h + 1) * HD)
            for c in range(2):
                out_ref[c, 0, :, columns] = mixed[c]
                other_ref[1 - c, 0, :, columns] = mixed[c]
            stat_ref[0, h] = jnp.broadcast_to(log_total, (total, HD))

    flat_shape = shape_of((2, local_rows, count, heads * HD))
    stat_shape = shape_of((local_rows, heads, total, HD), jnp.float32)
    return run_grid(
        kernel,
        local_rows,
        [query_spec, keys, allowed_spec],
        [(flat, flat_shape), (flat, flat_shape), (stats, stat_shape)],
        here,
        queries,
        pairs,
        allowed,
    )


def attend_back(here, queries, pairs, allowed, stats, grads, came, cosine, sine):
    local_rows, heads, cores, count, hd = queries.shape
    total = 2 * count
    spots = pairs.shape[0]
    scaling = 1.0 / math.sqrt(HD)
    keys, query_spec, flat, stat_spec, allowed_spec = row_specs(pairs, count)
    table = pl.BlockSpec((2, 1, count, HD), lambda r: (0, r, 0, 0))
    half_keys = pl.BlockSpec((spots // 2, 2, 1, count, 2 * HD), lambda r: (0, 0, r, 0, 0))

    def kernel(here_ref, q_ref, pair_ref, allowed_ref, stat_ref, grad_ref, came_ref, cos_ref, sin_ref, out_ref, *parts):
        pair = pair_ref[...].reshape(-1, 2 * HD)
        key, value = pair[:, :HD], pair[:, HD:]
        seen = allowed_ref[0] > 0
        cosine, sine = (ref[...].reshape(total, HD) for ref in (cos_ref, sin_ref))
        key_part = jnp.zeros(key.shape, jnp.float32)
        value_part = jnp.zeros(key.shape, jnp.float32)
        for h in range(heads):
            columns = slice(h * HD, (h + 1) * HD)
            query = q_ref[0, h].reshape(total, HD)
            grad = low(grad_ref[:, 0, :, columns] + came_ref[:, 0, :, columns]).reshape(total, HD)
            probs = jnp.exp(row_scores(query, key, seen) - stat_ref[0, h][:, :1])
            back = nt(grad, value)
            delta = jnp.sum(probs * back, axis=-1, keepdims=True)
            score_grad = low(probs * (back - delta))
            key_part = key_part + tn(score_grad, query)
            value_part = value_part + tn(low(probs), grad)
            query_sum = nn(score_grad, key) * scaling
            turned = low(turn_back(query_sum, cosine, sine))
            out_ref[:, 0, :, columns] = turned.reshape(2, count, HD)
        shape = (2, spots // 2, 2, count, HD)
        key_part = low(key_part * scaling).reshape(shape)
        value_part = low(value_part).reshape(shape)
        for i, ref in enumerate(parts):
            ref[:, :, 0, :, :HD] = key_part[i]
            ref[:, :, 0, :, HD:] = value_part[i]

    part_shape = shape_of((spots // 2,) + pairs.shape[1:])
    return run_grid(
        kernel,
        local_rows,
        [query_spec, keys, allowed_spec, stat_spec, flat, flat, table, table],
        [
            (flat, shape_of((2, local_rows, count, heads * HD))),
            (half_keys, part_shape),
            (half_keys, part_shape),
        ],
        here,
        queries,
        pairs,
        allowed,
        stats,
        grads,
        came,
        cosine,
        sine,
    )


def output_projection(here, attended, came, weights):
    total, half = attended.shape
    width = 2 * half
    tables = len(weights)
    pieces = tables > 1
    dims = six(weights[0]) if pieces else weights[0].shape

    def kernel(here_ref, own_ref, came_ref, *refs):
        weight_refs = refs[:tables]
        part_ref, other_ref, all_ref = refs[tables : tables + 3]
        if pieces:
            assemble(here_ref, weight_refs, refs[-1])
            weight = refs[-1][...].reshape(width, half)
        else:
            weight = weight_refs[0][...]
        own, came = own_ref[...], came_ref[...]
        first = here_ref[3] == 0
        heads = jnp.concatenate([jnp.where(first, own, came), jnp.where(first, came, own)], axis=1)
        all_ref[...] = heads
        part = nn(heads, weight)
        part_ref[...] = part[: total // 2]
        other_ref[...] = part[total // 2 :]

    part_shape = shape_of((total // 2, half), jnp.float32)
    shapes = [part_shape, part_shape, shape_of((total, width))]
    if pieces:
        shapes.append(shape_of(dims))
    out = run(kernel, shapes, here, attended, came, *weights)
    return out if pieces else list(out) + [weights[0]]


def joined(first, own, came):
    return jnp.concatenate([jnp.where(first, own, came), jnp.where(first, came, own)], axis=1)


def second_norm(here, tokens, part, came, lines):
    count, width = tokens.shape

    def kernel(here_ref, tokens_ref, part_ref, came_ref, line_ref, hidden_ref, normed_ref):
        hidden = wide(tokens_ref[...]) + joined(here_ref[3] == 0, part_ref[...], came_ref[...])
        scale = lax.rsqrt(jnp.mean(hidden * hidden, axis=-1, keepdims=True) + epsilon)
        hidden_ref[...] = hidden
        normed_ref[...] = low(hidden * scale * line_ref[2:3])

    shapes = (shape_of((count, width), jnp.float32), shape_of((count, width)))
    return run(kernel, shapes, here, tokens, part, came, lines)


def halves_specs(width, tile, steps):
    first = pl.BlockSpec((tile, width), lambda i: (jnp.minimum(i, steps - 1), 0))
    second = pl.BlockSpec((tile, width), lambda i: (jnp.maximum(i - steps, 0), 0))
    return first, second


def feed_forward(here, normed, upstream, weights, weight_down):
    count, width = normed[0].shape
    hidden_width = weight_down.shape[0]
    tile = min(256, count)
    steps = count // tile
    tables = len(weights)
    pieces = tables > 2
    chunk = hidden_width // 3 if hidden_width % 384 == 0 else hidden_width
    spec_a, spec_b = halves_specs(width, tile, steps)

    def kernel(here_ref, na_ref, nb_ref, ua_ref, ub_ref, wd, *refs):
        weight_refs = refs[:tables]
        grad_a, grad_b, hidden_ref, gate_ref, up_ref = refs[tables : tables + 5]
        step = pl.program_id(0)
        if pieces:
            scratch = refs[-2:]

            @pl.when(step == 0)
            def _():
                at = 0
                for pack in (weight_refs[:5], weight_refs[5:]):
                    for m in range(2):
                        group = (*pack[:3], pack[3 + m])
                        assemble(here_ref, group, scratch[m], lambda ref, m=m: ref.at[m], at)
                    at += pack[0].shape[-1]

            wg, wu = (ref[...].reshape(width, hidden_width) for ref in scratch)
        else:
            wg, wu = (ref[...] for ref in weight_refs)
        early = step < steps
        normed = jnp.where(early, na_ref[...], nb_ref[...])
        upstream = jnp.where(early, ua_ref[...], ub_ref[...])
        for k in range(0, hidden_width, chunk):
            columns = slice(k, k + chunk)
            gate = nn(normed, wg[:, columns])
            up = nn(normed, wu[:, columns])
            back = nt(upstream, wd[columns, :])
            sigmoid = jax.nn.sigmoid(gate)
            silu = gate * sigmoid
            hidden_ref[:, columns] = low(silu * up)
            gate_ref[:, columns] = low(back * up * sigmoid * (1.0 + gate * (1.0 - sigmoid)))
            up_ref[:, columns] = low(back * silu)
        grad = low(nt(gate_ref[...], wg) + nt(up_ref[...], wu))

        @pl.when(early)
        def _():
            grad_a[...] = grad

        @pl.when(jnp.logical_not(early))
        def _():
            grad_b[...] = grad

    rows = pl.BlockSpec((tile, hidden_width), lambda i: (i, 0))
    group = shape_of((count, width))
    wide_rows = shape_of((2 * count, hidden_width))
    scratch = []
    if pieces:
        dims = six(weights[0][0])[:-1] + (hidden_width,)
        scratch = [pltpu.VMEM(dims, jnp.bfloat16)] * 2
    return pl.pallas_call(
        kernel,
        grid=(2 * steps,),
        in_specs=[SMEM, spec_a, spec_b, spec_a, spec_b, whole_block(weight_down)]
        + [whole_block(w) for w in weights],
        out_specs=[spec_a, spec_b, rows, rows, rows],
        out_shape=[group, group, wide_rows, wide_rows, wide_rows],
        scratch_shapes=scratch,
        compiler_params=pltpu.CompilerParams(vmem_limit_bytes=42 << 20),
        cost_estimate=LITTLE,
    )(here, *normed, *upstream, weight_down, *weights)


def feed_forward_output(here, hidden, weight_down):
    count = hidden.shape[0] // 2
    width = weight_down.shape[1]
    tile = min(256, count)
    steps = count // tile
    specs = halves_specs(width, tile, steps)

    def kernel(here_ref, hidden_ref, weight_ref, out_a, out_b):
        part = low(nn(hidden_ref[...], weight_ref[...]))

        @pl.when(pl.program_id(0) < steps)
        def _():
            out_a[...] = part

        @pl.when(pl.program_id(0) >= steps)
        def _():
            out_b[...] = part

    rows = pl.BlockSpec((tile, hidden.shape[1]), lambda i: (i, 0))
    shape = shape_of((count, width))
    return run_grid(
        kernel,
        2 * steps,
        [rows, whole_block(weight_down)],
        [(spec, shape) for spec in specs],
        here,
        hidden,
        weight_down,
    )


def column_block(array, width):
    return pl.BlockSpec((array.shape[0], width), lambda i: (0, i))


def weight_grads(here, lefts, rights):
    counts = [v.shape[0] for v in lefts]
    rows = lefts[0].shape[1]
    tile = 384 if rows % 384 == 0 else 128
    number = len(lefts)

    def kernel(here_ref, *refs):
        turned = jnp.concatenate([ref[...] for ref in refs[:number]], axis=0).T
        for right, out in zip(refs[number : number + len(rights)], refs[number + len(rights) :]):
            out[...] = low(nn(turned, right[...]))

    return run_grid(
        kernel,
        rows // tile,
        [column_block(v, tile) for v in lefts] + [whole_block(v) for v in rights],
        [
            (pl.BlockSpec((tile, v.shape[1]), lambda i: (i, 0)), shape_of((rows, v.shape[1])))
            for v in rights
        ],
        here,
        *lefts,
        *rights,
    )


def split_by_plane(here_ref, first, second, refs, rows):
    y, x = here_ref[1], here_ref[2]
    first_send, first_keep, second_send, second_keep = refs
    first = first.reshape(2, 2, rows, first.shape[1])
    second = second.reshape(2, 2, rows, second.shape[1])
    first_send[0] = jnp.where(y == 0, first[1], first[0])
    first_keep[0] = jnp.where(y == 0, first[0], first[1])
    second_send[0] = jnp.where(x == 0, second[:, 1], second[:, 0])
    second_keep[0] = jnp.where(x == 0, second[:, 0], second[:, 1])


def plane_outs(nz, rows, first, second):
    shapes = [shape_of((nz, 2, rows, n)) for n in (first, first, second, second)]
    return [(lead_block(s.shape), s) for s in shapes]


def share_grads(here, lefts, first, second, nz, rows, vectors=None):
    width = lefts[0].shape[1]
    block = width // nz
    number = len(lefts)
    (first, first_from, first_to), (second, second_from, second_to) = first, second
    arrays = list(lefts) + [first, second] + ([] if vectors is None else [vectors])

    def kernel(here_ref, *refs):
        turned = jnp.concatenate([ref[...] for ref in refs[:number]], axis=0).T
        one = low(nn(turned, refs[number][:, first_from:first_to]))
        two = low(nn(turned, refs[number + 1][:, second_from:second_to]))
        if vectors is not None:
            filled = jnp.concatenate(
                [refs[number + 2][...], jnp.zeros((120, block), jnp.float32)], axis=0
            )
            two = jnp.concatenate([two, low(filled.T)], axis=1)
        split_by_plane(here_ref, one, two, refs[len(arrays) :], rows)

    extra = 0 if vectors is None else 128
    return run_grid(
        kernel,
        nz,
        [column_block(v, block) for v in lefts]
        + [whole_block(first), whole_block(second)]
        + ([] if vectors is None else [column_block(vectors, block)]),
        plane_outs(nz, rows, first_to - first_from, second_to - second_from + extra),
        here,
        *arrays,
    )


def plane_step(here, keeps, cames):
    nz = keeps[0].shape[0]

    def kernel(here_ref, first_ref, first_came, second_ref, second_came, *outs):
        y, x = here_ref[1], here_ref[2]
        first = low(wide(first_ref[0]) + wide(first_came[0]))
        second = low(wide(second_ref[0]) + wide(second_came[0]))
        for value, at, send, keep in ((first, x, *outs[:2]), (second, y, *outs[2:])):
            send[0] = jnp.where(at == 0, value[1], value[0])
            keep[0] = jnp.where(at == 0, value[0], value[1])

    shapes = []
    for v in keeps:
        shapes += [shape_of((nz,) + v.shape[2:])] * 2
    return run_grid(
        kernel,
        nz,
        [lead_block(v.shape) for v in (keeps[0], cames[0], keeps[1], cames[1])],
        [(lead_block(s.shape), s) for s in shapes],
        here,
        keeps[0],
        cames[0],
        keeps[1],
        cames[1],
    )


def share_sums(here, keeps, cames):
    nz, cores, rows, width = keeps[0].shape

    def kernel(here_ref, g_ref, g_came, u_ref, u_came, mine_ref, send_ref):
        core = here_ref[3]
        for m, (ref, came) in enumerate(((g_ref, g_came), (u_ref, u_came))):
            mine_ref[0, m] = low(wide(ref[0, core]) + wide(came[0, core]))
            send_ref[0, m] = low(wide(ref[0, 1 - core]) + wide(came[0, 1 - core]))

    shape = shape_of((nz, 2, rows, width))
    arrays = (keeps[0], cames[0], keeps[1], cames[1])
    return run_grid(
        kernel,
        nz,
        [lead_block(v.shape) for v in arrays],
        [(lead_block(shape.shape), shape)] * 2,
        here,
        *arrays,
    )


def collect_columns(here, pieces, sizes, unit, lane):
    nz, ny, nx, nc = sizes
    rows = pieces[0].shape[2]
    flat = [v for piece in pieces for v in (piece if isinstance(piece, tuple) else (piece,))]
    number = len(flat)

    def kernel(here_ref, *refs):
        gate_ref, up_ref, placed = refs[number:]
        refs = list(refs[:number])
        core = here_ref[3]
        for k, piece in enumerate(pieces):
            at = around(here_ref[0], -k, nz)
            if isinstance(piece, tuple):
                for m in range(2):
                    ref = refs.pop(0)
                    placed[at, core, m] = ref[0]
                    placed[at, 1 - core, m] = ref[1]
            else:
                ref = refs.pop(0)
                placed[at, core] = ref[0]
                placed[at, 1 - core] = ref[1]
        for m, ref in enumerate((gate_ref, up_ref)):
            for d in range(nz * ny * nx * nc):
                z, p, c = d // (ny * nx * nc), d // nc % (ny * nx), d % nc
                ref[:, unit * d : unit * d + unit] = wide(
                    placed[z, c, m, :, lane * p : lane * p + unit]
                )

    shape = shape_of((rows, unit * nz * ny * nx * nc), jnp.float32)
    return pl.pallas_call(
        kernel,
        in_specs=[SMEM] + [VMEM] * number,
        out_specs=[VMEM] * 2,
        out_shape=[shape, shape],
        scratch_shapes=[pltpu.VMEM((nz,) + pieces[0].shape, jnp.bfloat16)],
        compiler_params=SPACE,
        cost_estimate=LITTLE,
    )(here, *flat)


def down_grads(here, hidden, upstream, lane):
    hidden_width = hidden.shape[1]
    width = upstream[0].shape[1]
    count = upstream[0].shape[0]
    part = lane // 2

    def kernel(here_ref, hidden_ref, other_ref, own_ref, *outs):
        refs, turned_ref = outs[:4], outs[4]
        y, x = here_ref[1], here_ref[2]
        turned_ref[...] = hidden_ref[...].T
        for p in range(4):
            left = turned_ref[lane * p : lane * (p + 1), :]
            block = low(nn(left[:, :count], other_ref[...]) + nn(left[:, count:], own_ref[...]))
            for half, at, here_at, slot in ((0, p // 2, y, p % 2), (1, p % 2, x, p // 2)):
                value = block[half * part : (half + 1) * part]

                @pl.when(here_at == at)
                def _():
                    refs[2 * half + 1][slot] = value

                @pl.when(here_at != at)
                def _():
                    refs[2 * half][slot] = value

    shape = shape_of((2, part, width))
    return pl.pallas_call(
        kernel,
        in_specs=[SMEM] + [VMEM] * 3,
        out_specs=[VMEM] * 4,
        out_shape=[shape] * 4,
        scratch_shapes=[pltpu.VMEM((hidden_width, 2 * count), jnp.bfloat16)],
        compiler_params=SPACE,
        cost_estimate=LITTLE,
    )(here, hidden, *upstream)


def down_step(here, keeps, cames):
    def kernel(here_ref, first_ref, first_came, second_ref, second_came, *outs):
        for at, ref, came, send, keep in (
            (here_ref[2], first_ref, first_came, *outs[:2]),
            (here_ref[1], second_ref, second_came, *outs[2:]),
        ):
            send[...] = low(wide(ref[1 - at]) + wide(came[1 - at]))
            keep[...] = low(wide(ref[at]) + wide(came[at]))

    shape = shape_of(keeps[0].shape[1:])
    return run(kernel, [shape] * 4, here, keeps[0], cames[0], keeps[1], cames[1])


def depth_blocks(here, own, came):
    nz = lax.axis_size("z")
    shape = (own.shape[0] // nz, own.shape[1])
    own, came = (v.reshape((nz,) + shape) for v in (own, came))

    def kernel(here_ref, own_ref, came_ref, *outs):
        for k, out in enumerate(outs):
            at = (nz - k) % nz
            out[...] = (wide(own_ref[at]) + wide(came_ref[at])).astype(out.dtype)

    shapes = [shape_of(shape, jnp.float32)] + [shape_of(shape)] * (nz - 1)
    return run(kernel, shapes, here, own, came)


def first_backward(here, own, pieces, hidden, upstream, lines):
    count, width = hidden.shape
    half = width // 2
    number = len(pieces)

    def kernel(here_ref, own_ref, hidden_ref, up_ref, line_ref, *refs):
        out_ref, mine_ref, other_ref, term_ref = refs[number:]
        grad = own_ref[...]
        for ref in refs[:number]:
            grad = grad + wide(ref[...])
        hidden = hidden_ref[...]
        scale = lax.rsqrt(jnp.mean(hidden * hidden, axis=-1, keepdims=True) + epsilon)
        normalized = hidden * scale
        term_ref[...] = jnp.sum(grad * normalized, axis=0, keepdims=True)
        scaled = grad * line_ref[2:3]
        mean = jnp.mean(scaled * normalized, axis=-1, keepdims=True)
        result = wide(up_ref[...]) + scale * (scaled - normalized * mean)
        out_ref[...] = result
        proj = low(result)
        first = here_ref[3] == 0
        mine_ref[...] = jnp.where(first, proj[:, :half], proj[:, half:])
        other_ref[...] = jnp.where(first, proj[:, half:], proj[:, :half])

    shapes = (
        shape_of((count, width), jnp.float32),
        shape_of((count, half)),
        shape_of((count, half)),
        shape_of((1, width), jnp.float32),
    )
    return run(kernel, shapes, here, own, hidden, upstream, lines, *pieces)


def attended_backward(here, mine, came, weight):
    count, half = mine.shape

    def kernel(here_ref, mine_ref, came_ref, weight_ref, keep_ref, send_ref, proj_ref):
        proj = jnp.concatenate([mine_ref[...], came_ref[...]], axis=0)
        proj_ref[...] = proj
        part = nt(proj, weight_ref[...])
        first = here_ref[3] == 0
        keep_ref[...] = jnp.where(first, part[:, :half], part[:, half:])
        send = jnp.where(first, part[:, half:], part[:, :half])
        send_ref[:count] = send[count:]
        send_ref[count:] = send[:count]

    shape = shape_of((2 * count, half), jnp.float32)
    return run(kernel, (shape, shape, shape_of((2 * count, half))), here, mine, came, weight)


def inner_backward(here, query_grad, pair_sum, cosine, sine, weight, owned, owned_key):
    total, half = query_grad.shape
    width = 2 * half
    inner = half + 2 * HD

    def kernel(here_ref, q_ref, pair_ref, cos_ref, sin_ref, weight_ref, out_ref, own_ref, other_ref, line_ref):
        core = here_ref[3]
        pair = pair_ref[...]
        key = low(turn_back(pair[:, :HD], cos_ref[...], sin_ref[...]))
        value = low(pair[:, HD:])
        grad = jnp.concatenate([q_ref[...], key, value], axis=1)
        out_ref[...] = grad
        part = nt(grad, weight_ref[:, :inner])
        own_ref[...] = part[: total // 2]
        other_ref[...] = part[total // 2 :]
        terms = jnp.sum(wide(grad), axis=0, keepdims=True)
        query = terms[:, :half]
        nothing = jnp.zeros_like(query)
        first = core == 0
        line_ref[0:1] = jnp.concatenate(
            [jnp.where(first, query, nothing), jnp.where(first, nothing, query)], axis=1
        )
        line_ref[1:2] = nt(
            low(terms[:, half : half + HD]), key_places(core, width, owned, owned_key, 0)
        ) + nt(
            low(terms[:, half + HD :]), key_places(core, width, owned, owned_key, owned_key)
        )

    shapes = (
        shape_of((total, inner)),
        shape_of((total // 2, width), jnp.float32),
        shape_of((total // 2, width), jnp.float32),
        shape_of((2, width), jnp.float32),
    )
    return run(kernel, shapes, here, query_grad, pair_sum, cosine, sine, weight)


def input_backward(here, tokens, own, came, hidden_grad, lines, post_term, bias_terms):
    count, width = tokens.shape

    def kernel(here_ref, t_ref, own_ref, came_ref, h_ref, line_ref, post_ref, bias_ref, out_ref, term_ref):
        values = wide(t_ref[...])
        scale = lax.rsqrt(jnp.mean(values * values, axis=-1, keepdims=True) + epsilon)
        normalized = values * scale
        grad = own_ref[...] + came_ref[...]
        scaled = grad * line_ref[1:2]
        mean = jnp.mean(scaled * normalized, axis=-1, keepdims=True)
        out_ref[...] = low(h_ref[...] + scale * (scaled - normalized * mean))
        term_ref[...] = jnp.concatenate(
            [
                bias_ref[0:1],
                jnp.sum(grad * normalized, axis=0, keepdims=True),
                post_ref[...],
                bias_ref[1:2],
                jnp.zeros((4, width), jnp.float32),
            ],
            axis=0,
        )

    shapes = (shape_of((count, width)), shape_of((8, width), jnp.float32))
    return run(
        kernel, shapes, here, tokens, own, came, hidden_grad, lines, post_term, bias_terms
    )


def inner_blocks(here, keeps, cames):
    nz, cores, rows, columns = keeps[0].shape
    columns = sum(v.shape[3] for v in keeps)
    number = len(keeps)

    def kernel(here_ref, *refs):
        pairs = list(zip(refs[:number], refs[number : 2 * number]))
        for k, out in enumerate(refs[2 * number :]):
            at = around(here_ref[0], k, nz)
            for c in range(cores):
                sums = [wide(a[at, c]) + wide(b[at, c]) for a, b in pairs]
                out[c] = jnp.concatenate(sums, axis=1).astype(out.dtype)

    shape = (cores, rows, columns)
    shapes = [shape_of(shape, jnp.float32)] + [shape_of(shape)] * (nz - 1)
    return run(kernel, shapes, here, *keeps, *cames)


def inner_sums(here, own, pieces):
    cores, rows, columns = own.shape
    number = len(pieces)

    def kernel(here_ref, own_ref, *refs):
        mine_ref, send_ref = refs[number:]
        core = here_ref[3]
        for at, out in ((core, mine_ref), (1 - core, send_ref)):
            total = own_ref[at]
            for ref in refs[:number]:
                total = total + wide(ref[at])
            out[...] = total.astype(out.dtype)

    shapes = (shape_of((rows, columns), jnp.float32), shape_of((rows, columns)))
    return run(kernel, shapes, here, own, *pieces)


def inner_results(here, mine, came, width, key_width):
    rows = mine.shape[0]
    half = width // 2
    ends = (half, 2 * half, 2 * half + HD, 2 * half + 2 * HD)

    def kernel(here_ref, mine_ref, came_ref, output_ref, query_ref, key_ref, value_ref, line_ref):
        first = here_ref[3] == 0
        mine, came = mine_ref[...], wide(came_ref[...])
        line_ref[...] = mine[:, ends[-1] :] + came[:, ends[-1] :]
        output_ref[...] = joined(first, mine[:, :half], came[:, :half])
        for ref, a, b in zip((query_ref, key_ref, value_ref), ends, ends[1:]):
            ref[...] = joined(first, mine[:, a:b], came[:, a:b])

    shapes = [
        shape_of((rows, n), jnp.float32) for n in (width, width, key_width, key_width, 128)
    ]
    return run(kernel, shapes, here, mine, came)


def column_pack(columns, rows):
    padded = [jnp.pad(v, (0, rows - v.shape[0])) for v in columns]
    packed = jnp.stack(padded, axis=1)
    return jnp.pad(packed, ((0, 0), (0, 128 - len(columns))))


def shards(
    tokens,
    doc_lengths,
    query_weight,
    key_weight,
    value_weight,
    query_bias,
    key_bias,
    value_bias,
    output_weight,
    attention_norm_gain,
    feedforward_norm_gain,
    gate_weight,
    up_weight,
    down_weight,
    cotangent,
):
    local_rows, shard_tokens, width = tokens.shape
    sizes = nz, ny, nx, nc = tuple(lax.axis_size(a) for a in EVERY)
    here = jnp.stack([lax.axis_index(a) for a in EVERY]).astype(jnp.int32)
    devices = nz * ny * nx * nc
    flat_count = local_rows * shard_tokens
    chip_count = 2 * flat_count
    owned, query_width = query_weight.shape
    key_width = key_weight.shape[1]
    owned_key = key_bias.shape[0]
    half = query_width // 2
    unit = gate_weight.shape[1] // devices
    lane = -(-ny * nx * unit // 128) * 128 // (ny * nx)
    hidden_width = ny * nx * lane
    in_square = square()
    own_tokens = tokens.reshape(flat_count, width)
    upstream = cotangent.reshape(flat_count, width)
    chip_shape = (2, local_rows, shard_tokens)

    vectors = column_pack(
        (
            query_bias,
            attention_norm_gain,
            feedforward_norm_gain,
            jnp.concatenate([key_bias, value_bias]),
        ),
        owned,
    )
    packed = jnp.concatenate([query_weight, key_weight, value_weight, vectors], axis=1)
    pieces = depth_gathered(packed, every_shift()) | {0: packed}
    cut = down_weight.shape[0] // 32 * 16
    down_near = [plane_near(down_weight[:cut])] if in_square else ()
    cosine, sine, allowed = position_tables(doc_lengths, shard_tokens)
    first_shift, last_shift = every_shift()[0], every_shift()[-1]
    pieces, down_near, cosine, sine, allowed = sync(pieces, down_near, cosine, sine, allowed)

    mine, shares, send = split_shares(
        here, in_order(pieces), gate_weight, up_weight, sizes, unit, lane, query_width, key_width
    )
    came = swapped(send, "c")
    late_output = after(output_weight, pieces)
    output_pieces = depth_gathered(late_output, near_shifts()) | {0: late_output}
    if in_square:
        down_near = [*down_near, plane_near(after(down_weight[cut:], pieces))]
    mine, came, shares, output_pieces, down_near = sync(
        mine, came, shares, output_pieces, down_near
    )

    inner_own = jnp.stack([mine, came[:, 0, :, : mine.shape[2]]], axis=1)
    share_parts = dict(enumerate(share_blocks(here, shares, came, 1)))
    inner_near = plane_near(inner_own) if in_square else ()
    output_pieces |= depth_gathered(after(late_output, mine), far_shifts())
    share_pieces = depth_sent(share_parts, [first_shift]) | {0: share_parts[0]}
    down_far = ()
    if in_square:
        down_far = swapped(down_near[0][0], "y"), swapped(down_near[1][1], "x")
    inner_own, inner_near, output_pieces, share_parts, share_pieces, down_far = sync(
        inner_own, inner_near, output_pieces, share_parts, share_pieces, down_far
    )

    middle = 512
    if in_square:
        inner_far = (
            swapped(inner_near[0][..., :middle], "y"),
            swapped(inner_near[1][..., middle:], "x"),
        )
        inner_weights = (inner_own, *inner_near, *inner_far)
    else:
        inner_weights = (plane_whole(inner_own).reshape(width, -1),)
    output_mine, output_send = split_output(here, in_order(output_pieces))
    output_came = swapped(output_send, "c")
    other_tokens = swapped(after(own_tokens, inner_own), "c")
    share_pieces |= depth_sent(share_parts, [last_shift])
    share_split = hidden_width // 256 * 128
    inner_weights, output_mine, output_came, other_tokens, share_pieces = sync(
        inner_weights, output_mine, output_came, other_tokens, share_pieces
    )

    output_own = jnp.stack([output_mine, output_came], axis=1)
    if nz == 4:
        gate_part, up_part = after(share_parts[2], output_mine)
        late_pieces = [shifted(gate_part, 2)]
    else:
        share_pieces |= depth_sent(after(share_parts, output_mine), far_shifts())
        late_pieces = []
    output_near = plane_near(output_own) if in_square else ()
    first_normed, queries, own_pair, lines, weight_inner = inner_projections(
        here,
        own_tokens.reshape(chip_shape[1:] + (width,)),
        other_tokens.reshape(chip_shape[1:] + (width,)),
        inner_weights,
        cosine,
        sine,
        owned,
        owned_key,
    )
    weight_inner = weight_inner.reshape(width, -1)
    cosine_chip = cosine.reshape(chip_shape + (HD,))
    sine_chip = sine.reshape(chip_shape + (HD,))
    late_upstream = after(upstream, inner_weights)
    upstream_pieces = depth_gathered(late_upstream, [first_shift]) | {0: late_upstream}
    own_pair, output_own, output_near, share_pieces, late_pieces, upstream_pieces = sync(
        own_pair, output_own, output_near, share_pieces, late_pieces, upstream_pieces
    )

    middle = half // 2
    if in_square:
        pairs = jnp.stack([own_pair, swapped(own_pair, "x")])
        output_near = after(output_near, pairs)
        output_far = (
            swapped(output_near[0][..., :middle], "y"),
            swapped(output_near[1][..., middle:], "x"),
        )
        output_weights = (output_own, *output_near, *output_far)
        pairs = jnp.concatenate([pairs, swapped(pairs, "y")], axis=0)
    else:
        pairs = plane_gathered(own_pair)
        output_weights = (plane_whole(output_own).reshape(width, -1),)
    if nz == 4:
        late_pieces.append(shifted(after(up_part, own_pair), 2))
    pairs, output_weights, late_pieces = sync(pairs, output_weights, late_pieces)

    first_own, second_own = place_shares(here, in_order(share_pieces), late_pieces, share_split)
    first_near = plane_near(first_own) if in_square else ()
    upstream_pieces |= depth_gathered(after(upstream, pairs), far_shifts())
    attended, turned, log_sums = attend(here, queries, pairs, allowed)
    attended, turned, first_near, second_own, upstream_pieces = sync(
        attended, turned, first_near, second_own, upstream_pieces
    )

    first_far = ()
    if in_square:
        first_far = swapped(first_near[0][0], "y"), swapped(first_near[1][1], "x")
    upstream_pieces |= depth_gathered(after(upstream, attended), [last_shift])
    came = swapped(turned.reshape(chip_count, half), "c")
    part, send, attended_all, weight_output = output_projection(
        here, attended.reshape(chip_count, half), came, output_weights
    )
    weight_output = weight_output.reshape(width, half)
    first_hidden, second_normed = second_norm(here, own_tokens, part, swapped(send, "c"), lines)
    second_normed, first_far, upstream_pieces = sync(second_normed, first_far, upstream_pieces)

    second_pieces = depth_gathered(second_normed, every_shift()) | {0: second_normed}
    if in_square:
        second_near = plane_near(after(second_own, second_normed))
        second_far = swapped(second_near[0][0], "y"), swapped(second_near[1][1], "x")
        weights = (first_own, *first_near, *first_far, second_own, *second_near, *second_far)
        second_pieces, weights = sync(second_pieces, weights)
        y, x = lax.axis_index("y"), lax.axis_index("x")
        weight_down = jnp.zeros((2, 2, lane, width), jnp.bfloat16)
        for block, index in (
            (down_weight, (y, x, 0, 0)),
            (down_near[0][0], (y, 1 - x, 0, 0)),
            (down_near[1][0], (y, 1 - x, cut, 0)),
            (down_near[0][1], (1 - y, x, 0, 0)),
            (down_near[1][1], (1 - y, x, cut, 0)),
            (down_far[0], (1 - y, 1 - x, 0, 0)),
            (down_far[1], (1 - y, 1 - x, cut, 0)),
        ):
            weight_down = lax.dynamic_update_slice(weight_down, block[None, None], index)
    else:
        weights = tuple(
            jnp.concatenate(
                [plane_whole(v[m]).reshape(width, -1) for v in (first_own, second_own)], axis=1
            )
            for m in range(2)
        )
        weight_down = lax.all_gather(down_weight, PLANE, axis=0)
        weight_down = jnp.pad(weight_down, ((0, 0), (0, lane - unit), (0, 0)))
        second_pieces, weights, weight_down = sync(second_pieces, weights, weight_down)
    weight_down = weight_down.reshape(hidden_width, width)

    second_mine = jnp.concatenate(in_order(second_pieces), axis=0)
    second_group = (swapped(second_mine, "c"), second_mine)
    upstream_mine = jnp.concatenate(in_order(upstream_pieces), axis=0)
    upstream_group = (swapped(upstream_mine, "c"), upstream_mine)
    normed_send, normed_own, hidden, gate_grad, up_grad = feed_forward(
        here, second_group, upstream_group, weights, weight_down
    )
    normed_came = swapped(normed_send, "c")
    rows = nc * owned
    if in_square:
        send_gate, gate_sum, send_up, up_sum = share_grads(
            here,
            second_group,
            (gate_grad, 0, hidden_width),
            (up_grad, 0, hidden_width),
            nz,
            rows,
        )
    else:
        send_gate, send_up = weight_grads(here, second_group, (gate_grad, up_grad))
        gate_sum = up_sum = ()
    normed_own, *normed_parts = depth_blocks(here, normed_own, normed_came)
    normed_parts = dict(enumerate(normed_parts, 1))
    normed_own, normed_parts, send_gate, gate_sum, send_up, up_sum = sync(
        normed_own, normed_parts, send_gate, gate_sum, send_up, up_sum
    )

    normed_pieces = depth_sent(normed_parts, every_shift())
    if in_square:
        came_gate, came_up = swapped(send_gate, "y"), swapped(send_up, "x")
        down_parts = down_grads(here, after(hidden, normed_own), upstream_group, lane)
    else:
        blocks = (nz, ny * nx, nc, owned, hidden_width)
        gate_sum, up_sum = (
            lax.psum_scatter(v.reshape(blocks), PLANE, scatter_dimension=1, tiled=False)
            for v in (send_gate, send_up)
        )
        (down_parts,) = weight_grads(
            here, (hidden,), (jnp.concatenate(upstream_group, axis=0),)
        )
    output_send, output_own = feed_forward_output(here, after(hidden, normed_own), weight_down)
    normed_pieces, down_parts, output_send, output_own = sync(
        normed_pieces, down_parts, output_send, output_own
    )

    hidden_one_grad, proj_mine, proj_send, post_term = first_backward(
        here, normed_own, in_order(normed_pieces), first_hidden, upstream, lines
    )
    keep, send, proj_grad = attended_backward(
        here, proj_mine, swapped(proj_send, "c"), weight_output
    )
    attended_came = swapped(send, "c")
    output_came = swapped(after(output_send, proj_mine), "c")
    if in_square:
        keep, attended_came, output_own, output_came, came_gate, came_up = sync(
            keep, attended_came, output_own, output_came, came_gate, came_up
        )
        send_gate, gate_sum, send_up, up_sum = plane_step(
            here, (gate_sum, up_sum), (came_gate, came_up)
        )
    else:
        keep, attended_came = sync(keep, attended_came)
    output_own, *output_parts = depth_blocks(here, output_own, output_came)
    output_parts = dict(enumerate(output_parts, 1))

    four = (nz, nc, owned, hidden_width)
    if in_square:
        came_gate, came_up = swapped(send_gate, "x"), swapped(send_up, "y")
    output_pieces = depth_sent(output_parts, far_shifts())
    if in_square:
        send_a, keep_a, send_b, keep_b = share_grads(
            here,
            (attended_all,),
            (proj_grad, 0, half // 2),
            (proj_grad, half // 2, half),
            nz,
            rows,
        )
    query_grad, part_near, part_far = attend_back(
        here,
        queries,
        pairs,
        allowed,
        log_sums,
        keep.reshape(chip_shape + (half,)),
        attended_came.reshape(chip_shape + (half,)),
        cosine_chip,
        sine_chip,
    )
    if in_square:
        part_near, part_far, came_gate, came_up, output_pieces, send_a, send_b = sync(
            part_near, part_far, came_gate, came_up, output_pieces, send_a, send_b
        )
    else:
        came_gate = came_up = jnp.zeros(four, jnp.bfloat16)

    shares, send_shares = share_sums(
        here,
        (gate_sum.reshape(four), up_sum.reshape(four)),
        (came_gate.reshape(four), came_up.reshape(four)),
    )
    came_shares = swapped(send_shares, "c")
    output_pieces |= depth_sent(after(output_parts, part_near), [first_shift])
    if in_square:
        step = low(wide(part_near) + wide(swapped(part_far, "y")))
        pair_sum = wide(step[0]) + wide(swapped(step[1], "x"))
    else:
        pair_sum = plane_summed(jnp.concatenate([part_near, part_far], axis=0))
    share_parts = dict(enumerate(share_blocks(here, shares, came_shares)))
    pair_sum, share_parts, output_pieces = sync(pair_sum, share_parts, output_pieces)

    share_pieces = depth_sent(share_parts, near_shifts()) | {0: share_parts[0]}
    if in_square:
        send_a, send_b = after((send_a, send_b), pair_sum)
        came_a, came_b = swapped(send_a, "y"), swapped(send_b, "x")
    else:
        down_sum = lax.psum_scatter(
            down_parts.reshape(ny * nx, lane, width), PLANE, scatter_dimension=0, tiled=False
        )
    inner_grad, own_part, send, bias_terms = inner_backward(
        here,
        query_grad.reshape(chip_count, half),
        pair_sum.reshape(chip_count, 2 * HD),
        cosine,
        sine,
        weight_inner,
        owned,
        owned_key,
    )
    input_grad, vector_terms = input_backward(
        here, own_tokens, own_part, swapped(send, "c"), hidden_one_grad, lines, post_term, bias_terms
    )
    share_parts = after(share_parts, inner_grad)
    if in_square:
        send_c, keep_c, send_d, keep_d = share_grads(
            here,
            (first_normed,),
            (inner_grad, 0, 512),
            (inner_grad, 512, half + 2 * HD),
            nz,
            rows,
            vector_terms,
        )
        send_c, keep_c, send_d, keep_d, came_a, came_b, share_parts, share_pieces = sync(
            send_c, keep_c, send_d, keep_d, came_a, came_b, share_parts, share_pieces
        )
        share_pieces |= depth_sent(share_parts, far_shifts())
        send_a, keep_a, send_b, keep_b = plane_step(here, (keep_a, keep_b), (came_a, came_b))
        came_a, came_b = swapped(send_a, "x"), swapped(send_b, "y")
        came_c, came_d = swapped(send_c, "y"), swapped(send_d, "x")
        came_a, came_b, came_c, came_d, share_pieces = sync(
            came_a, came_b, came_c, came_d, share_pieces
        )
        send_c, keep_c, send_d, keep_d = plane_step(here, (keep_c, keep_d), (came_c, came_d))
        came_c, came_d = swapped(send_c, "x"), swapped(send_d, "y")
        output_pieces |= depth_sent(after(output_parts, share_pieces), [last_shift])
        came_c, came_d, output_pieces = sync(came_c, came_d, output_pieces)
        keeps, cames = (
            [v.reshape(nz, nc, owned, -1) for v in group]
            for group in ((keep_a, keep_b, keep_c, keep_d), (came_a, came_b, came_c, came_d))
        )
    else:
        share_pieces |= depth_sent(share_parts, far_shifts())
        (output_term,) = weight_grads(here, (attended_all,), (proj_grad,))
        (inner_term,) = weight_grads(here, (first_normed,), (inner_grad,))
        inner_term = jnp.concatenate(
            [inner_term, jnp.pad(low(vector_terms.T), ((0, 0), (0, 120)))], axis=1
        )
        blocks = (nz, ny * nx, nc, owned, -1)
        keeps = [
            lax.psum_scatter(v.reshape(blocks), PLANE, scatter_dimension=1, tiled=False)
            for v in (output_term, inner_term)
        ]
        cames = [jnp.zeros_like(v) for v in keeps]
    if not in_square:
        output_pieces |= depth_sent(output_parts, [last_shift])
    layer_output = first_hidden + output_own + sum(wide(v) for v in in_order(output_pieces))
    gate_sum, up_sum = collect_columns(here, in_order(share_pieces), sizes, unit, lane)

    own, *parts = inner_blocks(here, keeps, cames)
    parts = dict(enumerate(parts, 1))
    pieces = depth_sent(parts, every_shift())
    if in_square:
        first_send, first_keep, second_send, second_keep = after(down_parts, came_c)
        came_first, came_second = swapped(first_send, "y"), swapped(second_send, "x")
        first_send, first_keep, second_send, second_keep = down_step(
            here, (first_keep, second_keep), (came_first, came_second)
        )
        first_send, second_send = after((first_send, second_send), pieces[first_shift])
        came_first, came_second = swapped(first_send, "x"), swapped(second_send, "y")
        down_sum = jnp.concatenate(
            [
                wide(first_keep) + wide(came_first),
                wide(second_keep) + wide(came_second),
            ],
            axis=0,
        )
    pieces, down_sum = sync(pieces, down_sum)
    mine, send = inner_sums(here, own, in_order(pieces))
    output_sum, query_sum, key_sum, value_sum, vector_sums = inner_results(
        here, mine, swapped(send, "c"), width, key_width
    )
    return (
        low(layer_output).reshape(local_rows, shard_tokens, width),
        input_grad.reshape(local_rows, shard_tokens, width),
        query_sum,
        key_sum,
        value_sum,
        vector_sums[:, 0],
        vector_sums[:owned_key, 3],
        vector_sums[owned_key : 2 * owned_key, 3],
        output_sum,
        vector_sums[:, 1],
        vector_sums[:, 2],
        gate_sum,
        up_sum,
        wide(down_sum)[:unit],
    )


def solution(mesh):
    depth, across = mesh.devices.shape
    plane = across // 2
    side = math.isqrt(plane)
    inner = Mesh(mesh.devices.reshape(depth, plane // side, side, 2), EVERY)
    over_rows = P("z", ROW, None)
    whole, flat = P(EVERY, None), P(EVERY)
    in_specs = (
        (over_rows, P("z", None))
        + (whole,) * 3
        + (flat,) * 3
        + (whole, flat, flat)
        + (whole,) * 3
        + (over_rows,)
    )
    out_specs = (
        (over_rows,) * 2 + (whole,) * 3 + (flat,) * 3 + (whole, flat, flat) + (whole,) * 3
    )
    return jax.shard_map(
        shards, mesh=inner, in_specs=in_specs, out_specs=out_specs, check_vma=False
    )
```

```python
import math

import jax
import jax.numpy as jnp
from jax import lax
from jax.experimental import pallas as pl
from jax.experimental.pallas import tpu as pltpu
from jax.sharding import Mesh
from jax.sharding import PartitionSpec as P

H = 12
KV = 2
HD = 128
HPG = 6

epsilon = 1e-06
rope_base = 10000.0
masked_value = -1e30

EVERY = ("z", "y", "x", "c")
ROW = ("y", "x", "c")
PLANE = ("y", "x")


def low(values):
    return values.astype(jnp.bfloat16)


def wide(values):
    return values.astype(jnp.float32)


def nn(left, right):
    return jnp.dot(left, right, preferred_element_type=jnp.float32)


def nt(left, right):
    return lax.dot_general(
        left, right, (((1,), (1,)), ((), ())), preferred_element_type=jnp.float32
    )


def tn(left, right):
    return lax.dot_general(
        left, right, (((0,), (0,)), ((), ())), preferred_element_type=jnp.float32
    )


def doc_tables(doc_ends, doc_lengths, positions):
    passed = doc_ends[:, None, :] <= positions[None, :, None]
    doc_index = jnp.sum(passed.astype(jnp.int32), axis=-1)
    starts = jnp.sum(jnp.where(passed, doc_lengths[:, None, :], 0), axis=-1)
    return (doc_index, positions[None, :] - starts)


def rope_tables(within):
    steps_even = jnp.arange(0, HD, 2).astype(jnp.float32)
    inverse = rope_base ** (-steps_even / HD)
    phase = within.astype(jnp.float32)[:, None] * inverse[None, :]
    phase = jnp.concatenate([phase, phase], axis=-1)
    return jnp.cos(phase), jnp.sin(phase)


def square():
    return lax.axis_size("y") == 2 and lax.axis_size("x") == 2


def places():
    y, x = lax.axis_index("y"), lax.axis_index("x")
    if square():
        return [(y, x), (y, 1 - x), (1 - y, x), (1 - y, 1 - x)]
    return [(i, j) for i in range(lax.axis_size("y")) for j in range(lax.axis_size("x"))]


def chip_positions(y, x, shard_tokens):
    core = lax.axis_index("c")
    place = (y * lax.axis_size("x") + x) * 2
    lanes = jnp.arange(shard_tokens, dtype=jnp.int32)
    return [(place + k) * shard_tokens + lanes for k in (core, 1 - core)]


def position_tables(doc_lengths, shard_tokens):
    local_rows = doc_lengths.shape[0]
    query_pos = jnp.concatenate(
        chip_positions(lax.axis_index("y"), lax.axis_index("x"), shard_tokens)
    )
    key_pos = jnp.concatenate(
        [p for place in places() for p in chip_positions(*place, shard_tokens)]
    )
    doc_ends = jnp.cumsum(doc_lengths, axis=1)
    query_doc, query_within = doc_tables(doc_ends, doc_lengths, query_pos)
    key_doc, unused_within = doc_tables(doc_ends, doc_lengths, key_pos)
    allowed = (query_doc[:, :, None] == key_doc[:, None, :]) & (
        key_pos[None, None, :] <= query_pos[None, :, None]
    )
    query_within = query_within.reshape(local_rows, 2, shard_tokens).transpose(1, 0, 2)
    cosine, sine = rope_tables(query_within.reshape(-1))
    sign = jnp.where(jnp.arange(HD) < HD // 2, -1.0, 1.0)
    return cosine, sine * sign, wide(allowed)


def sync(*values):
    return lax.optimization_barrier(values)


def after(values, *others):
    return lax.optimization_barrier((values, others))[0]


def swapped(values, axis):
    return lax.ppermute(values, axis, [(0, 1), (1, 0)])


def shifted(values, amount):
    count = lax.axis_size("z")
    return lax.ppermute(values, "z", [(i, (i + amount) % count) for i in range(count)])


def every_shift():
    return range(1, lax.axis_size("z"))


def near_shifts():
    return sorted({1, lax.axis_size("z") - 1})


def far_shifts():
    return range(2, lax.axis_size("z") - 1)


def depth_gathered(rows, shifts):
    return {k: shifted(rows, k) for k in shifts}


def depth_sent(blocks, shifts):
    return {k: jax.tree.map(lambda v: shifted(v, k), blocks[k]) for k in shifts}


def in_order(pieces):
    return [pieces[k] for k in sorted(pieces)]


def plane_near(values):
    return swapped(values, "x"), swapped(values, "y")


def plane_gathered(rows):
    if not square():
        return lax.all_gather(rows, PLANE, axis=0)
    pair = jnp.stack([rows, swapped(rows, "x")])
    return jnp.concatenate([pair, swapped(pair, "y")], axis=0)


def plane_summed(blocks):
    if not square():
        return wide(lax.psum_scatter(blocks, PLANE, scatter_dimension=0, tiled=False))
    pair = low(wide(blocks[:2]) + wide(swapped(blocks[2:], "y")))
    return wide(pair[0]) + wide(swapped(pair[1], "x"))


def plane_whole(own):
    own = jnp.where(lax.axis_index("c") == 0, own, own[:, ::-1])
    whole = lax.all_gather(own, PLANE, axis=1, tiled=False)
    ny, nx = lax.axis_size("y"), lax.axis_size("x")
    return whole.reshape(own.shape[:1] + (ny, nx) + own.shape[1:])


LITTLE = pl.CostEstimate(flops=1, bytes_accessed=1, transcendentals=0)
SPACE = pltpu.CompilerParams(vmem_limit_bytes=16 << 20)
ROOM = pltpu.CompilerParams(vmem_limit_bytes=12 << 20)
VMEM = pl.BlockSpec(memory_space=pltpu.VMEM)
SMEM = pl.BlockSpec(memory_space=pltpu.SMEM)


def shape_of(dims, kind=jnp.bfloat16):
    return jax.ShapeDtypeStruct(tuple(dims), kind)


def run(kernel, shapes, here, *arrays):
    return pl.pallas_call(
        kernel,
        in_specs=[SMEM] + [VMEM] * len(arrays),
        out_specs=[VMEM] * len(shapes),
        out_shape=list(shapes),
        compiler_params=ROOM,
        cost_estimate=LITTLE,
    )(here, *arrays)


def run_grid(kernel, grid, specs, outs, here, *arrays):
    return pl.pallas_call(
        kernel,
        grid=(grid,),
        in_specs=[SMEM] + list(specs),
        out_specs=[spec for spec, shape in outs],
        out_shape=[shape for spec, shape in outs],
        compiler_params=SPACE,
        cost_estimate=LITTLE,
    )(here, *arrays)


def whole_block(array):
    dims = len(array.shape)
    return pl.BlockSpec(array.shape, lambda i: (0,) * dims, pipeline_mode=pl.Buffered(1))


def lead_block(shape):
    dims = len(shape)
    return pl.BlockSpec((1,) + tuple(shape[1:]), lambda i: (i,) + (0,) * (dims - 1))


def around(z, k, count):
    return lax.rem(z + (k + count), count)


def split_shares(here, pieces, gate_weight, up_weight, sizes, unit, lane, query_width, key_width):
    nz, ny, nx, nc = sizes
    rows = gate_weight.shape[0]
    half = query_width // 2
    hidden_width = lane * ny * nx
    inner_width = half + 2 * HD + 128
    count = len(pieces)

    def columns(piece, of):
        first, second = query_width + of * HD, query_width + key_width + of * HD
        return jnp.concatenate(
            [
                piece[:, of * half : (of + 1) * half],
                piece[:, first : first + HD],
                piece[:, second : second + HD],
                piece[:, query_width + 2 * key_width :],
            ],
            axis=1,
        )

    def kernel(here_ref, *refs):
        piece_refs, (gate_ref, up_ref) = refs[:count], refs[count : count + 2]
        mine_ref, share_ref, send_ref = refs[count + 2 :]
        core = here_ref[3]
        for k, ref in enumerate(piece_refs):
            at = around(here_ref[0], -k, nz)
            piece = ref[...]
            zero, one = columns(piece, 0), columns(piece, 1)
            mine_ref[at] = jnp.where(core == 0, zero, one)
            send_ref[at, 0, :, :inner_width] = jnp.where(core == 0, one, zero)
        share_ref[...] = jnp.zeros_like(share_ref)
        send_ref[:, 1:] = jnp.zeros_like(send_ref[:, 1:])
        for own in range(nc):

            @pl.when(core == own)
            def _():
                for m, ref in enumerate((gate_ref, up_ref)):
                    for d in range(nz * ny * nx * nc):
                        z, p, c = d // (ny * nx * nc), d // nc % (ny * nx), d % nc
                        columns = slice(lane * p, lane * p + unit)
                        value = ref[:, unit * d : unit * d + unit]
                        if c == own:
                            share_ref[z, m, :, columns] = value
                        else:
                            send_ref[z, 1 + m, :, columns] = value

    return run(
        kernel,
        (
            shape_of((nz, rows, inner_width)),
            shape_of((nz, 2, rows, hidden_width)),
            shape_of((nz, 3, rows, max(inner_width, hidden_width))),
        ),
        here,
        *pieces,
        gate_weight,
        up_weight,
    )


def share_blocks(here, mine, came, skip=0):
    nz, matrices = mine.shape[:2]
    width = mine.shape[3]
    block = (2,) + mine.shape[1:]
    single = (2,) + mine.shape[2:]

    def kernel(here_ref, mine_ref, came_ref, *outs):
        outs = list(outs)
        for k in range(nz):
            at = around(here_ref[0], k, nz)
            if nz == 4 and k == 2:
                for m in range(matrices):
                    out = outs.pop(0)
                    out[0] = mine_ref[at, m]
                    out[1] = came_ref[at, skip + m, :, :width]
            else:
                out = outs.pop(0)
                out[0] = mine_ref[at]
                out[1] = came_ref[at, skip:, :, :width]

    shapes = []
    for k in range(nz):
        shapes += [shape_of(single)] * matrices if nz == 4 and k == 2 else [shape_of(block)]
    out = list(run(kernel, shapes, here, mine, came))
    return [out[0], out[1], (out[2], out[3]), out[4]] if nz == 4 else out


def split_output(here, pieces):
    nz = len(pieces)
    rows, width = pieces[0].shape
    half = width // 2

    def kernel(here_ref, *refs):
        mine_ref, other_ref = refs[nz:]
        first = here_ref[3] == 0
        for k, ref in enumerate(refs[:nz]):
            at = around(here_ref[0], -k, nz)
            left, right = ref[:, :half], ref[:, half:]
            mine_ref[at] = jnp.where(first, left, right)
            other_ref[at] = jnp.where(first, right, left)

    return run(kernel, [shape_of((nz, rows, half))] * 2, here, *pieces)


def place_shares(here, pieces, last, split):
    nz = len(pieces) + (1 if last else 0)
    shifts = [0, 1, *range(2 + (1 if last else 0), nz)]
    pieces, number = list(pieces), len(pieces)
    cores, matrices, rows, width = pieces[0].shape

    def kernel(here_ref, *refs):
        first_ref, second_ref = refs[number + len(last) :]
        for k, ref in zip(shifts, refs[:number]):
            at = around(here_ref[0], -k, nz)
            for i in range(cores):
                for m in range(matrices):
                    first_ref[m, at, i] = ref[i, m, :, :split]
                    second_ref[m, at, i] = ref[i, m, :, split:]
        for m, ref in enumerate(refs[number : number + len(last)]):
            at = around(here_ref[0], -2, nz)
            for i in range(cores):
                first_ref[m, at, i] = ref[i, :, :split]
                second_ref[m, at, i] = ref[i, :, split:]

    return run(
        kernel,
        [shape_of((matrices, nz, cores, rows, n)) for n in (split, width - split)],
        here,
        *pieces,
        *last,
    )


def assemble(here_ref, refs, out, view=lambda ref: ref, at=0):
    y, x, c = here_ref[1], here_ref[2], here_ref[3]
    own, from_x, from_y, *far = refs
    columns = slice(at, at + own.shape[-1])
    for ref, at_y, at_x in ((own, y, x), (from_x, y, 1 - x), (from_y, 1 - y, x)):
        for z in range(out.shape[0]):
            for i in range(2):
                out[z, at_y, at_x, c if i == 0 else 1 - c, :, columns] = view(ref)[z, i]
    for z in range(out.shape[0]):
        for i in range(2):
            block = [ref[z, i] for ref in far]
            block = block[0] if len(block) == 1 else jnp.concatenate(block, axis=1)
            out[z, 1 - y, 1 - x, c if i == 0 else 1 - c, :, columns] = block


def six(own):
    return (own.shape[0], lax.axis_size("y"), lax.axis_size("x")) + own.shape[1:]


def turn(values, cosine, sine):
    return values * cosine + pltpu.roll(values, HD // 2, 1) * sine


def turn_back(values, cosine, sine):
    return values * cosine + pltpu.roll(values * sine, HD // 2, 1)


def key_places(core, width, owned, owned_key, shift):
    source = lax.broadcasted_iota(jnp.int32, (width, HD), 0)
    feature = lax.broadcasted_iota(jnp.int32, (width, HD), 1) + core * HD
    place = feature // owned_key * owned + feature % owned_key + shift
    return low(wide(source == place))


def inner_projections(here, own, other, weights, cosine, sine, owned, owned_key):
    local_rows, count, width = own.shape
    total = 2 * local_rows * count
    half = width // 2
    tables = len(weights)
    pieces = tables > 1
    dims = six(weights[0]) if pieces else weights[0].shape
    columns = dims[-1]

    def kernel(here_ref, own_ref, other_ref, cos_ref, sin_ref, *refs):
        weight_refs = refs[:tables]
        n_ref, q_ref, pair_ref, line_ref = refs[tables : tables + 4]
        if pieces:
            assemble(here_ref, weight_refs, refs[-1])
            weight = refs[-1][...].reshape(width, columns)
        else:
            weight = weight_refs[0][...]
        lines = wide(weight[:, columns - 128 :]).T
        core = here_ref[3]
        values = jnp.concatenate([own_ref[...], other_ref[...]], axis=0)
        values = wide(values.reshape(total, width))
        scale = lax.rsqrt(jnp.mean(values * values, axis=-1, keepdims=True) + epsilon)
        normed = low(values * scale * lines[1:2])
        n_ref[...] = normed
        line_ref[...] = lines[:8]
        small = low(lines[3:4])
        key_bias = nn(small, key_places(core, width, owned, owned_key, 0))
        value_bias = nn(small, key_places(core, width, owned, owned_key, owned_key))
        bias = jnp.where(core == 0, lines[0:1, :half], lines[0:1, half:])
        pre = nn(normed, weight[:, : half + 2 * HD])
        cosine, sine = cos_ref[...], sin_ref[...]
        for h in range(HPG):
            block = slice(h * HD, (h + 1) * HD)
            query = low(turn(pre[:, block] + bias[:, block], cosine, sine))
            query = query.reshape(2, local_rows, count, HD)
            for r in range(local_rows):
                q_ref[r, h] = query[:, r]
        key = low(turn(pre[:, half : half + HD] + key_bias, cosine, sine))
        value = low(pre[:, half + HD : half + 2 * HD] + value_bias)
        shape = (2, local_rows, count, HD)
        pair_ref[..., :HD] = key.reshape(shape)
        pair_ref[..., HD:] = value.reshape(shape)

    shapes = [
        shape_of((total, width)),
        shape_of((local_rows, HPG, 2, count, HD)),
        shape_of((2, local_rows, count, 2 * HD)),
        shape_of((8, width), jnp.float32),
    ]
    if pieces:
        shapes.append(shape_of(dims))
    out = run(kernel, shapes, here, own, other, cosine, sine, *weights)
    return out if pieces else list(out) + [weights[0]]


def row_scores(query, keys, allowed):
    return jnp.where(allowed, nt(query, keys) * (1.0 / math.sqrt(HD)), masked_value)


def row_specs(pairs, count):
    keys = pl.BlockSpec((pairs.shape[0], 2, 1, count, 2 * HD), lambda r: (0, 0, r, 0, 0))
    queries = pl.BlockSpec((1, HPG, 2, count, HD), lambda r: (r, 0, 0, 0, 0))
    flat = pl.BlockSpec((2, 1, count, HPG * HD), lambda r: (0, r, 0, 0))
    stats = pl.BlockSpec((1, HPG, 2 * count, HD), lambda r: (r, 0, 0, 0))
    allowed = pl.BlockSpec((1, 2 * count, pairs.shape[0] * 2 * count), lambda r: (r, 0, 0))
    return keys, queries, flat, stats, allowed


def attend(here, queries, pairs, allowed):
    local_rows, heads, cores, count, hd = queries.shape
    total = 2 * count
    keys, query_spec, flat, stats, allowed_spec = row_specs(pairs, count)

    def kernel(here_ref, q_ref, pair_ref, allowed_ref, out_ref, other_ref, stat_ref):
        pair = pair_ref[...].reshape(-1, 2 * HD)
        key, value = pair[:, :HD], pair[:, HD:]
        seen = allowed_ref[0] > 0
        for h in range(heads):
            scores = row_scores(q_ref[0, h].reshape(total, HD), key, seen)
            top = jnp.max(scores, axis=-1, keepdims=True)
            log_total = top + jnp.log(jnp.sum(jnp.exp(scores - top), axis=-1, keepdims=True))
            mixed = low(nn(low(jnp.exp(scores - log_total)), value)).reshape(2, count, HD)
            columns = slice(h * HD, (h + 1) * HD)
            for c in range(2):
                out_ref[c, 0, :, columns] = mixed[c]
                other_ref[1 - c, 0, :, columns] = mixed[c]
            stat_ref[0, h] = jnp.broadcast_to(log_total, (total, HD))

    flat_shape = shape_of((2, local_rows, count, heads * HD))
    stat_shape = shape_of((local_rows, heads, total, HD), jnp.float32)
    return run_grid(
        kernel,
        local_rows,
        [query_spec, keys, allowed_spec],
        [(flat, flat_shape), (flat, flat_shape), (stats, stat_shape)],
        here,
        queries,
        pairs,
        allowed,
    )


def attend_back(here, queries, pairs, allowed, stats, grads, came, cosine, sine):
    local_rows, heads, cores, count, hd = queries.shape
    total = 2 * count
    spots = pairs.shape[0]
    scaling = 1.0 / math.sqrt(HD)
    keys, query_spec, flat, stat_spec, allowed_spec = row_specs(pairs, count)
    table = pl.BlockSpec((2, 1, count, HD), lambda r: (0, r, 0, 0))
    half_keys = pl.BlockSpec((spots // 2, 2, 1, count, 2 * HD), lambda r: (0, 0, r, 0, 0))

    def kernel(here_ref, q_ref, pair_ref, allowed_ref, stat_ref, grad_ref, came_ref, cos_ref, sin_ref, out_ref, *parts):
        pair = pair_ref[...].reshape(-1, 2 * HD)
        key, value = pair[:, :HD], pair[:, HD:]
        seen = allowed_ref[0] > 0
        cosine, sine = (ref[...].reshape(total, HD) for ref in (cos_ref, sin_ref))
        key_part = jnp.zeros(key.shape, jnp.float32)
        value_part = jnp.zeros(key.shape, jnp.float32)
        for h in range(heads):
            columns = slice(h * HD, (h + 1) * HD)
            query = q_ref[0, h].reshape(total, HD)
            grad = low(grad_ref[:, 0, :, columns] + came_ref[:, 0, :, columns]).reshape(total, HD)
            probs = jnp.exp(row_scores(query, key, seen) - stat_ref[0, h][:, :1])
            back = nt(grad, value)
            delta = jnp.sum(probs * back, axis=-1, keepdims=True)
            score_grad = low(probs * (back - delta))
            key_part = key_part + tn(score_grad, query)
            value_part = value_part + tn(low(probs), grad)
            query_sum = nn(score_grad, key) * scaling
            turned = low(turn_back(query_sum, cosine, sine))
            out_ref[:, 0, :, columns] = turned.reshape(2, count, HD)
        shape = (2, spots // 2, 2, count, HD)
        key_part = low(key_part * scaling).reshape(shape)
        value_part = low(value_part).reshape(shape)
        for i, ref in enumerate(parts):
            ref[:, :, 0, :, :HD] = key_part[i]
            ref[:, :, 0, :, HD:] = value_part[i]

    part_shape = shape_of((spots // 2,) + pairs.shape[1:])
    return run_grid(
        kernel,
        local_rows,
        [query_spec, keys, allowed_spec, stat_spec, flat, flat, table, table],
        [
            (flat, shape_of((2, local_rows, count, heads * HD))),
            (half_keys, part_shape),
            (half_keys, part_shape),
        ],
        here,
        queries,
        pairs,
        allowed,
        stats,
        grads,
        came,
        cosine,
        sine,
    )


def output_projection(here, attended, came, weights):
    total, half = attended.shape
    width = 2 * half
    tables = len(weights)
    pieces = tables > 1
    dims = six(weights[0]) if pieces else weights[0].shape

    def kernel(here_ref, own_ref, came_ref, *refs):
        weight_refs = refs[:tables]
        part_ref, other_ref, all_ref = refs[tables : tables + 3]
        if pieces:
            assemble(here_ref, weight_refs, refs[-1])
            weight = refs[-1][...].reshape(width, half)
        else:
            weight = weight_refs[0][...]
        own, came = own_ref[...], came_ref[...]
        first = here_ref[3] == 0
        heads = jnp.concatenate([jnp.where(first, own, came), jnp.where(first, came, own)], axis=1)
        all_ref[...] = heads
        part = nn(heads, weight)
        part_ref[...] = part[: total // 2]
        other_ref[...] = part[total // 2 :]

    part_shape = shape_of((total // 2, half), jnp.float32)
    shapes = [part_shape, part_shape, shape_of((total, width))]
    if pieces:
        shapes.append(shape_of(dims))
    out = run(kernel, shapes, here, attended, came, *weights)
    return out if pieces else list(out) + [weights[0]]


def joined(first, own, came):
    return jnp.concatenate([jnp.where(first, own, came), jnp.where(first, came, own)], axis=1)


def second_norm(here, tokens, part, came, lines):
    count, width = tokens.shape

    def kernel(here_ref, tokens_ref, part_ref, came_ref, line_ref, hidden_ref, normed_ref):
        hidden = wide(tokens_ref[...]) + joined(here_ref[3] == 0, part_ref[...], came_ref[...])
        scale = lax.rsqrt(jnp.mean(hidden * hidden, axis=-1, keepdims=True) + epsilon)
        hidden_ref[...] = hidden
        normed_ref[...] = low(hidden * scale * line_ref[2:3])

    shapes = (shape_of((count, width), jnp.float32), shape_of((count, width)))
    return run(kernel, shapes, here, tokens, part, came, lines)


def halves_specs(width, tile, steps):
    first = pl.BlockSpec((tile, width), lambda i: (jnp.minimum(i, steps - 1), 0))
    second = pl.BlockSpec((tile, width), lambda i: (jnp.maximum(i - steps, 0), 0))
    return first, second


def feed_forward(here, normed, upstream, weights, weight_down):
    count, width = normed[0].shape
    hidden_width = weight_down.shape[0]
    tile = min(256, count)
    steps = count // tile
    tables = len(weights)
    pieces = tables > 2
    chunk = hidden_width // 3 if hidden_width % 384 == 0 else hidden_width
    spec_a, spec_b = halves_specs(width, tile, steps)

    def kernel(here_ref, na_ref, nb_ref, ua_ref, ub_ref, wd, *refs):
        weight_refs = refs[:tables]
        grad_a, grad_b, hidden_ref, gate_ref, up_ref = refs[tables : tables + 5]
        step = pl.program_id(0)
        if pieces:
            scratch = refs[-2:]

            @pl.when(step == 0)
            def _():
                at = 0
                for pack in (weight_refs[:5], weight_refs[5:]):
                    for m in range(2):
                        group = (*pack[:3], pack[3 + m])
                        assemble(here_ref, group, scratch[m], lambda ref, m=m: ref.at[m], at)
                    at += pack[0].shape[-1]

            wg, wu = (ref[...].reshape(width, hidden_width) for ref in scratch)
        else:
            wg, wu = (ref[...] for ref in weight_refs)
        early = step < steps
        normed = jnp.where(early, na_ref[...], nb_ref[...])
        upstream = jnp.where(early, ua_ref[...], ub_ref[...])
        for k in range(0, hidden_width, chunk):
            columns = slice(k, k + chunk)
            gate = nn(normed, wg[:, columns])
            up = nn(normed, wu[:, columns])
            back = nt(upstream, wd[columns, :])
            sigmoid = jax.nn.sigmoid(gate)
            silu = gate * sigmoid
            hidden_ref[:, columns] = low(silu * up)
            gate_ref[:, columns] = low(back * up * sigmoid * (1.0 + gate * (1.0 - sigmoid)))
            up_ref[:, columns] = low(back * silu)
        grad = low(nt(gate_ref[...], wg) + nt(up_ref[...], wu))

        @pl.when(early)
        def _():
            grad_a[...] = grad

        @pl.when(jnp.logical_not(early))
        def _():
            grad_b[...] = grad

    rows = pl.BlockSpec((tile, hidden_width), lambda i: (i, 0))
    group = shape_of((count, width))
    wide_rows = shape_of((2 * count, hidden_width))
    scratch = []
    if pieces:
        dims = six(weights[0][0])[:-1] + (hidden_width,)
        scratch = [pltpu.VMEM(dims, jnp.bfloat16)] * 2
    return pl.pallas_call(
        kernel,
        grid=(2 * steps,),
        in_specs=[SMEM, spec_a, spec_b, spec_a, spec_b, whole_block(weight_down)]
        + [whole_block(w) for w in weights],
        out_specs=[spec_a, spec_b, rows, rows, rows],
        out_shape=[group, group, wide_rows, wide_rows, wide_rows],
        scratch_shapes=scratch,
        compiler_params=pltpu.CompilerParams(vmem_limit_bytes=30 << 20),
        cost_estimate=LITTLE,
    )(here, *normed, *upstream, weight_down, *weights)


def feed_forward_output(here, hidden, weight_down):
    count = hidden.shape[0] // 2
    width = weight_down.shape[1]
    tile = min(256, count)
    steps = count // tile
    specs = halves_specs(width, tile, steps)

    def kernel(here_ref, hidden_ref, weight_ref, out_a, out_b):
        part = low(nn(hidden_ref[...], weight_ref[...]))

        @pl.when(pl.program_id(0) < steps)
        def _():
            out_a[...] = part

        @pl.when(pl.program_id(0) >= steps)
        def _():
            out_b[...] = part

    rows = pl.BlockSpec((tile, hidden.shape[1]), lambda i: (i, 0))
    shape = shape_of((count, width))
    return run_grid(
        kernel,
        2 * steps,
        [rows, whole_block(weight_down)],
        [(spec, shape) for spec in specs],
        here,
        hidden,
        weight_down,
    )


def column_block(array, width):
    return pl.BlockSpec((array.shape[0], width), lambda i: (0, i))


def weight_grads(here, lefts, rights):
    counts = [v.shape[0] for v in lefts]
    rows = lefts[0].shape[1]
    tile = 384 if rows % 384 == 0 else 128
    number = len(lefts)

    def kernel(here_ref, *refs):
        turned = jnp.concatenate([ref[...] for ref in refs[:number]], axis=0).T
        for right, out in zip(refs[number : number + len(rights)], refs[number + len(rights) :]):
            out[...] = low(nn(turned, right[...]))

    return run_grid(
        kernel,
        rows // tile,
        [column_block(v, tile) for v in lefts] + [whole_block(v) for v in rights],
        [
            (pl.BlockSpec((tile, v.shape[1]), lambda i: (i, 0)), shape_of((rows, v.shape[1])))
            for v in rights
        ],
        here,
        *lefts,
        *rights,
    )


def split_by_plane(here_ref, first, second, refs, rows):
    y, x = here_ref[1], here_ref[2]
    first_send, first_keep, second_send, second_keep = refs
    first = first.reshape(2, 2, rows, first.shape[1])
    second = second.reshape(2, 2, rows, second.shape[1])
    first_send[0] = jnp.where(y == 0, first[1], first[0])
    first_keep[0] = jnp.where(y == 0, first[0], first[1])
    second_send[0] = jnp.where(x == 0, second[:, 1], second[:, 0])
    second_keep[0] = jnp.where(x == 0, second[:, 0], second[:, 1])


def plane_outs(nz, rows, first, second):
    shapes = [shape_of((nz, 2, rows, n)) for n in (first, first, second, second)]
    return [(lead_block(s.shape), s) for s in shapes]


def share_grads(here, lefts, first, second, nz, rows, vectors=None):
    width = lefts[0].shape[1]
    block = width // nz
    number = len(lefts)
    (first, first_from, first_to), (second, second_from, second_to) = first, second
    arrays = list(lefts) + [first, second] + ([] if vectors is None else [vectors])

    def kernel(here_ref, *refs):
        turned = jnp.concatenate([ref[...] for ref in refs[:number]], axis=0).T
        one = low(nn(turned, refs[number][:, first_from:first_to]))
        two = low(nn(turned, refs[number + 1][:, second_from:second_to]))
        if vectors is not None:
            filled = jnp.concatenate(
                [refs[number + 2][...], jnp.zeros((120, block), jnp.float32)], axis=0
            )
            two = jnp.concatenate([two, low(filled.T)], axis=1)
        split_by_plane(here_ref, one, two, refs[len(arrays) :], rows)

    extra = 0 if vectors is None else 128
    return run_grid(
        kernel,
        nz,
        [column_block(v, block) for v in lefts]
        + [whole_block(first), whole_block(second)]
        + ([] if vectors is None else [column_block(vectors, block)]),
        plane_outs(nz, rows, first_to - first_from, second_to - second_from + extra),
        here,
        *arrays,
    )


def plane_step(here, keeps, cames):
    nz = keeps[0].shape[0]

    def kernel(here_ref, first_ref, first_came, second_ref, second_came, *outs):
        y, x = here_ref[1], here_ref[2]
        first = low(wide(first_ref[0]) + wide(first_came[0]))
        second = low(wide(second_ref[0]) + wide(second_came[0]))
        for value, at, send, keep in ((first, x, *outs[:2]), (second, y, *outs[2:])):
            send[0] = jnp.where(at == 0, value[1], value[0])
            keep[0] = jnp.where(at == 0, value[0], value[1])

    shapes = []
    for v in keeps:
        shapes += [shape_of((nz,) + v.shape[2:])] * 2
    return run_grid(
        kernel,
        nz,
        [lead_block(v.shape) for v in (keeps[0], cames[0], keeps[1], cames[1])],
        [(lead_block(s.shape), s) for s in shapes],
        here,
        keeps[0],
        cames[0],
        keeps[1],
        cames[1],
    )


def share_sums(here, keeps, cames):
    nz, cores, rows, width = keeps[0].shape

    def kernel(here_ref, g_ref, g_came, u_ref, u_came, mine_ref, send_ref):
        core = here_ref[3]
        for m, (ref, came) in enumerate(((g_ref, g_came), (u_ref, u_came))):
            mine_ref[0, m] = low(wide(ref[0, core]) + wide(came[0, core]))
            send_ref[0, m] = low(wide(ref[0, 1 - core]) + wide(came[0, 1 - core]))

    shape = shape_of((nz, 2, rows, width))
    arrays = (keeps[0], cames[0], keeps[1], cames[1])
    return run_grid(
        kernel,
        nz,
        [lead_block(v.shape) for v in arrays],
        [(lead_block(shape.shape), shape)] * 2,
        here,
        *arrays,
    )


def collect_columns(here, pieces, sizes, unit, lane):
    nz, ny, nx, nc = sizes
    rows = pieces[0].shape[2]
    flat = [v for piece in pieces for v in (piece if isinstance(piece, tuple) else (piece,))]
    number = len(flat)

    def kernel(here_ref, *refs):
        gate_ref, up_ref, placed = refs[number:]
        refs = list(refs[:number])
        core = here_ref[3]
        for k, piece in enumerate(pieces):
            at = around(here_ref[0], -k, nz)
            if isinstance(piece, tuple):
                for m in range(2):
                    ref = refs.pop(0)
                    placed[at, core, m] = ref[0]
                    placed[at, 1 - core, m] = ref[1]
            else:
                ref = refs.pop(0)
                placed[at, core] = ref[0]
                placed[at, 1 - core] = ref[1]
        for m, ref in enumerate((gate_ref, up_ref)):
            for d in range(nz * ny * nx * nc):
                z, p, c = d // (ny * nx * nc), d // nc % (ny * nx), d % nc
                ref[:, unit * d : unit * d + unit] = wide(
                    placed[z, c, m, :, lane * p : lane * p + unit]
                )

    shape = shape_of((rows, unit * nz * ny * nx * nc), jnp.float32)
    return pl.pallas_call(
        kernel,
        in_specs=[SMEM] + [VMEM] * number,
        out_specs=[VMEM] * 2,
        out_shape=[shape, shape],
        scratch_shapes=[pltpu.VMEM((nz,) + pieces[0].shape, jnp.bfloat16)],
        compiler_params=SPACE,
        cost_estimate=LITTLE,
    )(here, *flat)


def down_grads(here, hidden, upstream, lane):
    hidden_width = hidden.shape[1]
    width = upstream[0].shape[1]
    count = upstream[0].shape[0]
    part = lane // 2

    def kernel(here_ref, hidden_ref, other_ref, own_ref, *outs):
        refs, turned_ref = outs[:4], outs[4]
        y, x = here_ref[1], here_ref[2]
        turned_ref[...] = hidden_ref[...].T
        for p in range(4):
            left = turned_ref[lane * p : lane * (p + 1), :]
            block = low(nn(left[:, :count], other_ref[...]) + nn(left[:, count:], own_ref[...]))
            for half, at, here_at, slot in ((0, p // 2, y, p % 2), (1, p % 2, x, p // 2)):
                value = block[half * part : (half + 1) * part]

                @pl.when(here_at == at)
                def _():
                    refs[2 * half + 1][slot] = value

                @pl.when(here_at != at)
                def _():
                    refs[2 * half][slot] = value

    shape = shape_of((2, part, width))
    return pl.pallas_call(
        kernel,
        in_specs=[SMEM] + [VMEM] * 3,
        out_specs=[VMEM] * 4,
        out_shape=[shape] * 4,
        scratch_shapes=[pltpu.VMEM((hidden_width, 2 * count), jnp.bfloat16)],
        compiler_params=SPACE,
        cost_estimate=LITTLE,
    )(here, hidden, *upstream)


def down_step(here, keeps, cames):
    def kernel(here_ref, first_ref, first_came, second_ref, second_came, *outs):
        for at, ref, came, send, keep in (
            (here_ref[2], first_ref, first_came, *outs[:2]),
            (here_ref[1], second_ref, second_came, *outs[2:]),
        ):
            send[...] = low(wide(ref[1 - at]) + wide(came[1 - at]))
            keep[...] = low(wide(ref[at]) + wide(came[at]))

    shape = shape_of(keeps[0].shape[1:])
    return run(kernel, [shape] * 4, here, keeps[0], cames[0], keeps[1], cames[1])


def depth_blocks(here, own, came):
    nz = lax.axis_size("z")
    shape = (own.shape[0] // nz, own.shape[1])
    own, came = (v.reshape((nz,) + shape) for v in (own, came))

    def kernel(here_ref, own_ref, came_ref, *outs):
        for k, out in enumerate(outs):
            at = (nz - k) % nz
            out[...] = (wide(own_ref[at]) + wide(came_ref[at])).astype(out.dtype)

    shapes = [shape_of(shape, jnp.float32)] + [shape_of(shape)] * (nz - 1)
    return run(kernel, shapes, here, own, came)


def first_backward(here, own, pieces, hidden, upstream, lines):
    count, width = hidden.shape
    half = width // 2
    number = len(pieces)

    def kernel(here_ref, own_ref, hidden_ref, up_ref, line_ref, *refs):
        out_ref, mine_ref, other_ref, term_ref = refs[number:]
        grad = own_ref[...]
        for ref in refs[:number]:
            grad = grad + wide(ref[...])
        hidden = hidden_ref[...]
        scale = lax.rsqrt(jnp.mean(hidden * hidden, axis=-1, keepdims=True) + epsilon)
        normalized = hidden * scale
        term_ref[...] = jnp.sum(grad * normalized, axis=0, keepdims=True)
        scaled = grad * line_ref[2:3]
        mean = jnp.mean(scaled * normalized, axis=-1, keepdims=True)
        result = wide(up_ref[...]) + scale * (scaled - normalized * mean)
        out_ref[...] = result
        proj = low(result)
        first = here_ref[3] == 0
        mine_ref[...] = jnp.where(first, proj[:, :half], proj[:, half:])
        other_ref[...] = jnp.where(first, proj[:, half:], proj[:, :half])

    shapes = (
        shape_of((count, width), jnp.float32),
        shape_of((count, half)),
        shape_of((count, half)),
        shape_of((1, width), jnp.float32),
    )
    return run(kernel, shapes, here, own, hidden, upstream, lines, *pieces)


def attended_backward(here, mine, came, weight):
    count, half = mine.shape

    def kernel(here_ref, mine_ref, came_ref, weight_ref, keep_ref, send_ref, proj_ref):
        proj = jnp.concatenate([mine_ref[...], came_ref[...]], axis=0)
        proj_ref[...] = proj
        part = nt(proj, weight_ref[...])
        first = here_ref[3] == 0
        keep_ref[...] = jnp.where(first, part[:, :half], part[:, half:])
        send = jnp.where(first, part[:, half:], part[:, :half])
        send_ref[:count] = send[count:]
        send_ref[count:] = send[:count]

    shape = shape_of((2 * count, half), jnp.float32)
    return run(kernel, (shape, shape, shape_of((2 * count, half))), here, mine, came, weight)


def inner_backward(here, query_grad, pair_sum, cosine, sine, weight, owned, owned_key):
    total, half = query_grad.shape
    width = 2 * half
    inner = half + 2 * HD

    def kernel(here_ref, q_ref, pair_ref, cos_ref, sin_ref, weight_ref, out_ref, own_ref, other_ref, line_ref):
        core = here_ref[3]
        pair = pair_ref[...]
        key = low(turn_back(pair[:, :HD], cos_ref[...], sin_ref[...]))
        value = low(pair[:, HD:])
        grad = jnp.concatenate([q_ref[...], key, value], axis=1)
        out_ref[...] = grad
        part = nt(grad, weight_ref[:, :inner])
        own_ref[...] = part[: total // 2]
        other_ref[...] = part[total // 2 :]
        terms = jnp.sum(wide(grad), axis=0, keepdims=True)
        query = terms[:, :half]
        nothing = jnp.zeros_like(query)
        first = core == 0
        line_ref[0:1] = jnp.concatenate(
            [jnp.where(first, query, nothing), jnp.where(first, nothing, query)], axis=1
        )
        line_ref[1:2] = nt(
            low(terms[:, half : half + HD]), key_places(core, width, owned, owned_key, 0)
        ) + nt(
            low(terms[:, half + HD :]), key_places(core, width, owned, owned_key, owned_key)
        )

    shapes = (
        shape_of((total, inner)),
        shape_of((total // 2, width), jnp.float32),
        shape_of((total // 2, width), jnp.float32),
        shape_of((2, width), jnp.float32),
    )
    return run(kernel, shapes, here, query_grad, pair_sum, cosine, sine, weight)


def input_backward(here, tokens, own, came, hidden_grad, lines, post_term, bias_terms):
    count, width = tokens.shape

    def kernel(here_ref, t_ref, own_ref, came_ref, h_ref, line_ref, post_ref, bias_ref, out_ref, term_ref):
        values = wide(t_ref[...])
        scale = lax.rsqrt(jnp.mean(values * values, axis=-1, keepdims=True) + epsilon)
        normalized = values * scale
        grad = own_ref[...] + came_ref[...]
        scaled = grad * line_ref[1:2]
        mean = jnp.mean(scaled * normalized, axis=-1, keepdims=True)
        out_ref[...] = low(h_ref[...] + scale * (scaled - normalized * mean))
        term_ref[...] = jnp.concatenate(
            [
                bias_ref[0:1],
                jnp.sum(grad * normalized, axis=0, keepdims=True),
                post_ref[...],
                bias_ref[1:2],
                jnp.zeros((4, width), jnp.float32),
            ],
            axis=0,
        )

    shapes = (shape_of((count, width)), shape_of((8, width), jnp.float32))
    return run(
        kernel, shapes, here, tokens, own, came, hidden_grad, lines, post_term, bias_terms
    )


def inner_blocks(here, keeps, cames):
    nz, cores, rows, columns = keeps[0].shape
    columns = sum(v.shape[3] for v in keeps)
    number = len(keeps)

    def kernel(here_ref, *refs):
        pairs = list(zip(refs[:number], refs[number : 2 * number]))
        for k, out in enumerate(refs[2 * number :]):
            at = around(here_ref[0], k, nz)
            for c in range(cores):
                sums = [wide(a[at, c]) + wide(b[at, c]) for a, b in pairs]
                out[c] = jnp.concatenate(sums, axis=1).astype(out.dtype)

    shape = (cores, rows, columns)
    shapes = [shape_of(shape, jnp.float32)] + [shape_of(shape)] * (nz - 1)
    return run(kernel, shapes, here, *keeps, *cames)


def inner_sums(here, groups):
    rows = groups[0][0].shape[1]
    columns = sum(own.shape[2] for own, pieces in groups)
    counts = [1 + len(pieces) for own, pieces in groups]

    def kernel(here_ref, *refs):
        mine_ref, send_ref = refs[sum(counts) :]
        core = here_ref[3]
        for at, out in ((core, mine_ref), (1 - core, send_ref)):
            parts, first = [], 0
            for count in counts:
                total = refs[first][at]
                for ref in refs[first + 1 : first + count]:
                    total = total + wide(ref[at])
                parts.append(total)
                first += count
            out[...] = jnp.concatenate(parts, axis=1).astype(out.dtype)

    shapes = (shape_of((rows, columns), jnp.float32), shape_of((rows, columns)))
    return run(kernel, shapes, here, *(v for own, pieces in groups for v in (own, *pieces)))


def inner_results(here, mine, came, width, key_width):
    rows = mine.shape[0]
    half = width // 2
    ends = (half, 2 * half, 2 * half + HD, 2 * half + 2 * HD)

    def kernel(here_ref, mine_ref, came_ref, output_ref, query_ref, key_ref, value_ref, line_ref):
        first = here_ref[3] == 0
        mine, came = mine_ref[...], wide(came_ref[...])
        line_ref[...] = mine[:, ends[-1] :] + came[:, ends[-1] :]
        output_ref[...] = joined(first, mine[:, :half], came[:, :half])
        for ref, a, b in zip((query_ref, key_ref, value_ref), ends, ends[1:]):
            ref[...] = joined(first, mine[:, a:b], came[:, a:b])

    shapes = [
        shape_of((rows, n), jnp.float32) for n in (width, width, key_width, key_width, 128)
    ]
    return run(kernel, shapes, here, mine, came)


def column_pack(columns, rows):
    padded = [jnp.pad(v, (0, rows - v.shape[0])) for v in columns]
    packed = jnp.stack(padded, axis=1)
    return jnp.pad(packed, ((0, 0), (0, 128 - len(columns))))


def shards(
    tokens,
    doc_lengths,
    query_weight,
    key_weight,
    value_weight,
    query_bias,
    key_bias,
    value_bias,
    output_weight,
    attention_norm_gain,
    feedforward_norm_gain,
    gate_weight,
    up_weight,
    down_weight,
    cotangent,
):
    local_rows, shard_tokens, width = tokens.shape
    sizes = nz, ny, nx, nc = tuple(lax.axis_size(a) for a in EVERY)
    here = jnp.stack([lax.axis_index(a) for a in EVERY]).astype(jnp.int32)
    devices = nz * ny * nx * nc
    flat_count = local_rows * shard_tokens
    chip_count = 2 * flat_count
    owned, query_width = query_weight.shape
    key_width = key_weight.shape[1]
    owned_key = key_bias.shape[0]
    half = query_width // 2
    unit = gate_weight.shape[1] // devices
    lane = -(-ny * nx * unit // 128) * 128 // (ny * nx)
    hidden_width = ny * nx * lane
    in_square = square()
    own_tokens = tokens.reshape(flat_count, width)
    upstream = cotangent.reshape(flat_count, width)
    chip_shape = (2, local_rows, shard_tokens)

    vectors = column_pack(
        (
            query_bias,
            attention_norm_gain,
            feedforward_norm_gain,
            jnp.concatenate([key_bias, value_bias]),
        ),
        owned,
    )
    packed = jnp.concatenate([query_weight, key_weight, value_weight, vectors], axis=1)
    pieces = depth_gathered(packed, every_shift()) | {0: packed}
    cut = down_weight.shape[0] // 32 * 16
    down_near = [plane_near(down_weight[:cut])] if in_square else ()
    cosine, sine, allowed = position_tables(doc_lengths, shard_tokens)
    first_shift, last_shift = every_shift()[0], every_shift()[-1]
    pieces, down_near, cosine, sine, allowed = sync(pieces, down_near, cosine, sine, allowed)

    mine, shares, send = split_shares(
        here, in_order(pieces), gate_weight, up_weight, sizes, unit, lane, query_width, key_width
    )
    came = swapped(send, "c")
    late_output = after(output_weight, pieces)
    output_pieces = depth_gathered(late_output, near_shifts()) | {0: late_output}
    if in_square:
        down_near = [*down_near, plane_near(after(down_weight[cut:], pieces))]
    mine, came, shares, output_pieces, down_near = sync(
        mine, came, shares, output_pieces, down_near
    )

    inner_own = jnp.stack([mine, came[:, 0, :, : mine.shape[2]]], axis=1)
    share_parts = dict(enumerate(share_blocks(here, shares, came, 1)))
    inner_near = plane_near(inner_own) if in_square else ()
    output_pieces |= depth_gathered(after(late_output, mine), far_shifts())
    share_pieces = depth_sent(share_parts, [first_shift]) | {0: share_parts[0]}
    down_far = ()
    if in_square:
        down_far = swapped(down_near[0][0], "y"), swapped(down_near[1][1], "x")
    inner_own, inner_near, output_pieces, share_parts, share_pieces, down_far = sync(
        inner_own, inner_near, output_pieces, share_parts, share_pieces, down_far
    )

    middle = 512
    if in_square:
        inner_far = (
            swapped(inner_near[0][..., :middle], "y"),
            swapped(inner_near[1][..., middle:], "x"),
        )
        inner_weights = (inner_own, *inner_near, *inner_far)
    else:
        inner_weights = (plane_whole(inner_own).reshape(width, -1),)
    output_mine, output_send = split_output(here, in_order(output_pieces))
    output_came = swapped(output_send, "c")
    other_tokens = swapped(after(own_tokens, inner_own), "c")
    share_pieces |= depth_sent(share_parts, [last_shift])
    share_split = hidden_width // 256 * 128
    inner_weights, output_mine, output_came, other_tokens, share_pieces = sync(
        inner_weights, output_mine, output_came, other_tokens, share_pieces
    )

    output_own = jnp.stack([output_mine, output_came], axis=1)
    if nz == 4:
        gate_part, up_part = after(share_parts[2], output_mine)
        late_pieces = [shifted(gate_part, 2)]
    else:
        share_pieces |= depth_sent(after(share_parts, output_mine), far_shifts())
        late_pieces = []
    output_near = plane_near(output_own) if in_square else ()
    first_normed, queries, own_pair, lines, weight_inner = inner_projections(
        here,
        own_tokens.reshape(chip_shape[1:] + (width,)),
        other_tokens.reshape(chip_shape[1:] + (width,)),
        inner_weights,
        cosine,
        sine,
        owned,
        owned_key,
    )
    weight_inner = weight_inner.reshape(width, -1)
    cosine_chip = cosine.reshape(chip_shape + (HD,))
    sine_chip = sine.reshape(chip_shape + (HD,))
    late_upstream = after(upstream, inner_weights)
    upstream_pieces = depth_gathered(late_upstream, [first_shift]) | {0: late_upstream}
    own_pair, output_own, output_near, share_pieces, late_pieces, upstream_pieces = sync(
        own_pair, output_own, output_near, share_pieces, late_pieces, upstream_pieces
    )

    middle = half // 2
    if in_square:
        pairs = jnp.stack([own_pair, swapped(own_pair, "x")])
        output_near = after(output_near, pairs)
        output_far = (
            swapped(output_near[0][..., :middle], "y"),
            swapped(output_near[1][..., middle:], "x"),
        )
        output_weights = (output_own, *output_near, *output_far)
        pairs = jnp.concatenate([pairs, swapped(pairs, "y")], axis=0)
    else:
        pairs = plane_gathered(own_pair)
        output_weights = (plane_whole(output_own).reshape(width, -1),)
    if nz == 4:
        late_pieces.append(shifted(after(up_part, own_pair), 2))
    pairs, output_weights, late_pieces = sync(pairs, output_weights, late_pieces)

    first_own, second_own = place_shares(here, in_order(share_pieces), late_pieces, share_split)
    first_near = plane_near(first_own) if in_square else ()
    upstream_pieces |= depth_gathered(after(upstream, pairs), far_shifts())
    attended, turned, log_sums = attend(here, queries, pairs, allowed)
    attended, turned, first_near, second_own, upstream_pieces = sync(
        attended, turned, first_near, second_own, upstream_pieces
    )

    first_far = ()
    if in_square:
        first_far = swapped(first_near[0][0], "y"), swapped(first_near[1][1], "x")
    upstream_pieces |= depth_gathered(after(upstream, attended), [last_shift])
    came = swapped(turned.reshape(chip_count, half), "c")
    part, send, attended_all, weight_output = output_projection(
        here, attended.reshape(chip_count, half), came, output_weights
    )
    weight_output = weight_output.reshape(width, half)
    first_hidden, second_normed = second_norm(here, own_tokens, part, swapped(send, "c"), lines)
    second_normed, first_far, upstream_pieces = sync(second_normed, first_far, upstream_pieces)

    second_pieces = depth_gathered(second_normed, every_shift()) | {0: second_normed}
    if in_square:
        second_near = plane_near(after(second_own, second_normed))
        second_far = swapped(second_near[0][0], "y"), swapped(second_near[1][1], "x")
        weights = (first_own, *first_near, *first_far, second_own, *second_near, *second_far)
        second_pieces, weights = sync(second_pieces, weights)
        y, x = lax.axis_index("y"), lax.axis_index("x")
        weight_down = jnp.zeros((2, 2, lane, width), jnp.bfloat16)
        for block, index in (
            (down_weight, (y, x, 0, 0)),
            (down_near[0][0], (y, 1 - x, 0, 0)),
            (down_near[1][0], (y, 1 - x, cut, 0)),
            (down_near[0][1], (1 - y, x, 0, 0)),
            (down_near[1][1], (1 - y, x, cut, 0)),
            (down_far[0], (1 - y, 1 - x, 0, 0)),
            (down_far[1], (1 - y, 1 - x, cut, 0)),
        ):
            weight_down = lax.dynamic_update_slice(weight_down, block[None, None], index)
    else:
        weights = tuple(
            jnp.concatenate(
                [plane_whole(v[m]).reshape(width, -1) for v in (first_own, second_own)], axis=1
            )
            for m in range(2)
        )
        weight_down = lax.all_gather(down_weight, PLANE, axis=0)
        weight_down = jnp.pad(weight_down, ((0, 0), (0, lane - unit), (0, 0)))
        second_pieces, weights, weight_down = sync(second_pieces, weights, weight_down)
    weight_down = weight_down.reshape(hidden_width, width)

    second_mine = jnp.concatenate(in_order(second_pieces), axis=0)
    second_group = (swapped(second_mine, "c"), second_mine)
    upstream_mine = jnp.concatenate(in_order(upstream_pieces), axis=0)
    upstream_group = (swapped(upstream_mine, "c"), upstream_mine)
    normed_send, normed_own, hidden, gate_grad, up_grad = feed_forward(
        here, second_group, upstream_group, weights, weight_down
    )
    normed_came = swapped(normed_send, "c")
    rows = nc * owned
    if in_square:
        send_gate, gate_sum, send_up, up_sum = share_grads(
            here,
            second_group,
            (gate_grad, 0, hidden_width),
            (up_grad, 0, hidden_width),
            nz,
            rows,
        )
    else:
        send_gate, send_up = weight_grads(here, second_group, (gate_grad, up_grad))
        gate_sum = up_sum = ()
    normed_own, *normed_parts = depth_blocks(here, normed_own, normed_came)
    normed_parts = dict(enumerate(normed_parts, 1))
    normed_own, normed_parts, send_gate, gate_sum, send_up, up_sum = sync(
        normed_own, normed_parts, send_gate, gate_sum, send_up, up_sum
    )

    normed_pieces = depth_sent(normed_parts, every_shift())
    if in_square:
        came_gate, came_up = swapped(send_gate, "y"), swapped(send_up, "x")
        down_parts = down_grads(here, after(hidden, normed_own), upstream_group, lane)
    else:
        blocks = (nz, ny * nx, nc, owned, hidden_width)
        gate_sum, up_sum = (
            lax.psum_scatter(v.reshape(blocks), PLANE, scatter_dimension=1, tiled=False)
            for v in (send_gate, send_up)
        )
        (down_parts,) = weight_grads(
            here, (hidden,), (jnp.concatenate(upstream_group, axis=0),)
        )
    output_send, output_own = feed_forward_output(here, after(hidden, normed_own), weight_down)
    normed_pieces, down_parts, output_send, output_own = sync(
        normed_pieces, down_parts, output_send, output_own
    )

    hidden_one_grad, proj_mine, proj_send, post_term = first_backward(
        here, normed_own, in_order(normed_pieces), first_hidden, upstream, lines
    )
    keep, send, proj_grad = attended_backward(
        here, proj_mine, swapped(proj_send, "c"), weight_output
    )
    attended_came = swapped(send, "c")
    output_came = swapped(after(output_send, proj_mine), "c")
    if in_square:
        keep, attended_came, output_own, output_came, came_gate, came_up = sync(
            keep, attended_came, output_own, output_came, came_gate, came_up
        )
        send_gate, gate_sum, send_up, up_sum = plane_step(
            here, (gate_sum, up_sum), (came_gate, came_up)
        )
    else:
        keep, attended_came = sync(keep, attended_came)
    output_own, *output_parts = depth_blocks(here, output_own, output_came)
    output_parts = dict(enumerate(output_parts, 1))

    four = (nz, nc, owned, hidden_width)
    if in_square:
        came_gate, came_up = swapped(send_gate, "x"), swapped(send_up, "y")
    output_pieces = depth_sent(output_parts, far_shifts())
    if in_square:
        send_a, keep_a, send_b, keep_b = share_grads(
            here,
            (attended_all,),
            (proj_grad, 0, half // 2),
            (proj_grad, half // 2, half),
            nz,
            rows,
        )
    query_grad, part_near, part_far = attend_back(
        here,
        queries,
        pairs,
        allowed,
        log_sums,
        keep.reshape(chip_shape + (half,)),
        attended_came.reshape(chip_shape + (half,)),
        cosine_chip,
        sine_chip,
    )
    if in_square:
        part_near, part_far, came_gate, came_up, output_pieces, send_a, send_b = sync(
            part_near, part_far, came_gate, came_up, output_pieces, send_a, send_b
        )
    else:
        came_gate = came_up = jnp.zeros(four, jnp.bfloat16)

    shares, send_shares = share_sums(
        here,
        (gate_sum.reshape(four), up_sum.reshape(four)),
        (came_gate.reshape(four), came_up.reshape(four)),
    )
    came_shares = swapped(send_shares, "c")
    output_pieces |= depth_sent(after(output_parts, part_near), [first_shift])
    if in_square:
        step = low(wide(part_near) + wide(swapped(part_far, "y")))
        pair_sum = wide(step[0]) + wide(swapped(step[1], "x"))
    else:
        pair_sum = plane_summed(jnp.concatenate([part_near, part_far], axis=0))
    share_parts = dict(enumerate(share_blocks(here, shares, came_shares)))
    pair_sum, share_parts, output_pieces = sync(pair_sum, share_parts, output_pieces)

    share_pieces = depth_sent(share_parts, near_shifts()) | {0: share_parts[0]}
    if in_square:
        send_a, send_b = after((send_a, send_b), pair_sum)
        came_a, came_b = swapped(send_a, "y"), swapped(send_b, "x")
    else:
        down_sum = lax.psum_scatter(
            down_parts.reshape(ny * nx, lane, width), PLANE, scatter_dimension=0, tiled=False
        )
    inner_grad, own_part, send, bias_terms = inner_backward(
        here,
        query_grad.reshape(chip_count, half),
        pair_sum.reshape(chip_count, 2 * HD),
        cosine,
        sine,
        weight_inner,
        owned,
        owned_key,
    )
    input_grad, vector_terms = input_backward(
        here, own_tokens, own_part, swapped(send, "c"), hidden_one_grad, lines, post_term, bias_terms
    )
    share_parts = after(share_parts, inner_grad)
    if in_square:
        send_c, keep_c, send_d, keep_d = share_grads(
            here,
            (first_normed,),
            (inner_grad, 0, 512),
            (inner_grad, 512, half + 2 * HD),
            nz,
            rows,
            vector_terms,
        )
        send_a, keep_a, send_b, keep_b = plane_step(here, (keep_a, keep_b), (came_a, came_b))
        came_a, came_b = swapped(send_a, "x"), swapped(send_b, "y")
        send_c, keep_c, send_d, keep_d, came_a, came_b, share_parts, share_pieces = sync(
            send_c, keep_c, send_d, keep_d, came_a, came_b, share_parts, share_pieces
        )
        share_pieces |= depth_sent(share_parts, far_shifts())
        came_c, came_d = swapped(send_c, "y"), swapped(send_d, "x")
        came_c, came_d, share_pieces = sync(came_c, came_d, share_pieces)
        send_c, keep_c, send_d, keep_d = plane_step(here, (keep_c, keep_d), (came_c, came_d))
        came_c, came_d = swapped(send_c, "x"), swapped(send_d, "y")
        keep_a, came_a, keep_b, came_b = (
            v.reshape(nz, nc, owned, -1) for v in (keep_a, came_a, keep_b, came_b)
        )
        own, *parts = inner_blocks(here, (keep_a, keep_b), (came_a, came_b))
        parts = dict(enumerate(parts, 1))
        parts = after(parts, share_pieces)
        pieces = depth_sent(parts, every_shift())
        gate_sum, up_sum = collect_columns(here, in_order(share_pieces), sizes, unit, lane)
        came_c, came_d, pieces, gate_sum, up_sum = sync(
            came_c, came_d, pieces, gate_sum, up_sum
        )
        groups = [(own, in_order(pieces))]
        keeps, cames = (
            [v.reshape(nz, nc, owned, -1) for v in group]
            for group in ((keep_c, keep_d), (came_c, came_d))
        )
    else:
        share_pieces |= depth_sent(share_parts, far_shifts())
        (output_term,) = weight_grads(here, (attended_all,), (proj_grad,))
        (inner_term,) = weight_grads(here, (first_normed,), (inner_grad,))
        inner_term = jnp.concatenate(
            [inner_term, jnp.pad(low(vector_terms.T), ((0, 0), (0, 120)))], axis=1
        )
        blocks = (nz, ny * nx, nc, owned, -1)
        keeps = [
            lax.psum_scatter(v.reshape(blocks), PLANE, scatter_dimension=1, tiled=False)
            for v in (output_term, inner_term)
        ]
        cames = [jnp.zeros_like(v) for v in keeps]
        groups = []
    if not in_square:
        output_pieces |= depth_sent(output_parts, [last_shift])
    if not in_square:
        gate_sum, up_sum = collect_columns(here, in_order(share_pieces), sizes, unit, lane)

    own, *parts = inner_blocks(here, keeps, cames)
    parts = dict(enumerate(parts, 1))
    pieces = depth_sent(parts, every_shift())
    if in_square:
        first_send, first_keep, second_send, second_keep = after(down_parts, came_c)
        came_first, came_second = swapped(first_send, "y"), swapped(second_send, "x")
        first_send, first_keep, second_send, second_keep = down_step(
            here, (first_keep, second_keep), (came_first, came_second)
        )
        early = in_order(pieces)
        first_send, second_send = after((first_send, second_send), early)
        groups.append((own, in_order(pieces)))
        output_pieces |= depth_sent(after(output_parts, early), [last_shift])
        came_first, came_second = swapped(first_send, "x"), swapped(second_send, "y")
        down_sum = jnp.concatenate(
            [
                wide(first_keep) + wide(came_first),
                wide(second_keep) + wide(came_second),
            ],
            axis=0,
        )
    else:
        groups = [(own, in_order(pieces))]
    layer_output = first_hidden + output_own + sum(wide(v) for v in in_order(output_pieces))
    groups, down_sum = sync(groups, down_sum)
    mine, send = inner_sums(here, groups)
    output_sum, query_sum, key_sum, value_sum, vector_sums = inner_results(
        here, mine, swapped(send, "c"), width, key_width
    )
    return (
        low(layer_output).reshape(local_rows, shard_tokens, width),
        input_grad.reshape(local_rows, shard_tokens, width),
        query_sum,
        key_sum,
        value_sum,
        vector_sums[:, 0],
        vector_sums[:owned_key, 3],
        vector_sums[owned_key : 2 * owned_key, 3],
        output_sum,
        vector_sums[:, 1],
        vector_sums[:, 2],
        gate_sum,
        up_sum,
        wide(down_sum)[:unit],
    )


def solution(mesh):
    depth, across = mesh.devices.shape
    plane = across // 2
    side = math.isqrt(plane)
    inner = Mesh(mesh.devices.reshape(depth, plane // side, side, 2), EVERY)
    over_rows = P("z", ROW, None)
    whole, flat = P(EVERY, None), P(EVERY)
    in_specs = (
        (over_rows, P("z", None))
        + (whole,) * 3
        + (flat,) * 3
        + (whole, flat, flat)
        + (whole,) * 3
        + (over_rows,)
    )
    out_specs = (
        (over_rows,) * 2 + (whole,) * 3 + (flat,) * 3 + (whole, flat, flat) + (whole,) * 3
    )
    return jax.shard_map(
        shards, mesh=inner, in_specs=in_specs, out_specs=out_specs, check_vma=False
    )
```
